32 devices in a mesh: dp: 4 (over x, core), space: 4 (over z), tm: 2 (over y).
Axes of the slice: x: 2, y: 2, z: 4, core: 2. Of those that a mesh axis runs over, the one named last changes fastest.
Arguments:
- inputs: bfloat16 [4, 20, 64, 1024], P('dp', None, 'space', 'tm'), may hold values from -6 to 6
- out_grad: bfloat16 [4, 20, 64, 1024], P('dp', None, 'space', 'tm'), may hold values from -6 to 6
- norm_gain: float32 [1024], replicated, may hold values from 0.1 to 1.9
- pos_bias: float32 [16, 39], P('tm'), may hold values from -4 to 4
- w_query: bfloat16 [1024, 1024], P(None, 'tm'), may hold values from -0.1875 to 0.1875
- w_key: bfloat16 [1024, 1024], P(None, 'tm'), may hold values from -0.1875 to 0.1875
- w_value: bfloat16 [1024, 1024], P(None, 'tm'), may hold values from -0.1875 to 0.1875
- w_out: bfloat16 [1024, 1024], P('tm'), may hold values from -0.1875 to 0.1875
Outputs:
- block_out: bfloat16 [4, 20, 64, 1024], P('dp', None, 'space', 'tm')
- input_grad: bfloat16 [4, 20, 64, 1024], P('dp', None, 'space', 'tm')
- gain_grad: float32 [1024], P('tm')
- bias_grad: float32 [16, 39], P('tm')
The draws below stay inside these ranges and needn't reach their ends.
All inputs are finite; a program needn't handle non-finite values.
Results may differ from the reference program's by a relative error of at most 0.0099.
Values may be sent and summed in bfloat16 or wider, within the bound.
No kernel may reach another device: no remote copies, remote signals or barrier semaphores. Data moves between devices by JAX's collectives and lax.ppermute only.
A program may use at most 64 MiB of HBM per device.

```python
import jax
import jax.numpy as jnp
from jax import lax

HEADS = 16
HEAD_DIM = 64
C = 1024
FRAMES = 20
PIXELS = 64
CLIPS = 4


def levels(stream_key, extent, pieces, low, top_value):
    loudness = 1.0
    for dim, shards_of in pieces:
        draws = jax.random.uniform(jax.random.fold_in(jax.random.fold_in(stream_key, 6), dim), (shards_of,), jnp.float32, low / len(pieces), top_value / len(pieces))
        loudness = loudness * jnp.repeat(jnp.exp(draws), extent[dim] // shards_of).reshape((-1,) + (1,) * (len(extent) - 1 - dim))
    return loudness


def bell_draw(rng, shape, spread, bound, shards=(), kind=jnp.bfloat16):
    gain = levels(rng, shape, shards, -0.22, 0.18) if shards else 1.0
    result = jax.random.normal(rng, shape, jnp.float32) * spread * gain
    return jnp.minimum(jnp.maximum(result, -bound), bound).astype(kind)


def setup_inputs(seed: int = 0) -> dict:
    seeds = jax.random.split(jax.random.key(seed), 9)
    inputs = bell_draw(seeds[0], (CLIPS, FRAMES, PIXELS, C), 1.0, 6.0, ((0, 4), (2, 4), (3, 2)))
    out_grad = bell_draw(seeds[1], (CLIPS, FRAMES, PIXELS, C), 1.0, 6.0, ((0, 4), (2, 4), (3, 2)))
    norm_gain = jnp.clip(1.0 + 0.18 * jax.random.normal(seeds[2], (C,), jnp.float32), 0.1, 1.9)
    pos_bias = bell_draw(seeds[3], (HEADS, 2 * FRAMES - 1), 1.0, 4.0, ((0, 2),), jnp.float32)
    w_query = bell_draw(seeds[4], (C, C), C ** -0.5, 0.1875, ((1, 2),))
    w_key = bell_draw(seeds[5], (C, C), C ** -0.5, 0.1875, ((1, 2),))
    w_value = bell_draw(seeds[6], (C, C), C ** -0.5, 0.1875, ((1, 2),))
    w_out = bell_draw(seeds[7], (C, C), C ** -0.5, 0.1875, ((0, 2),))
    return dict(inputs=inputs, out_grad=out_grad, norm_gain=norm_gain, pos_bias=pos_bias, w_query=w_query, w_key=w_key, w_value=w_value, w_out=w_out)


def reference(inputs, out_grad, norm_gain, pos_bias, w_query, w_key, w_value, w_out):
    frames = inputs.shape[1]
    chans = inputs.shape[3]
    scale = HEAD_DIM ** (-0.5)
    offsets = jnp.arange(frames)[None, :] - jnp.arange(frames)[:, None] + frames - 1
    rel_bias = pos_bias[:, offsets]

    def one_clip(pair):
        clip_in, clip_grad = pair
        pixels = clip_in.shape[1]
        x_full = clip_in.astype(jnp.float32)
        scale_inv = lax.rsqrt(lax.optimization_barrier(jnp.mean(x_full * x_full, axis=-1, keepdims=True)) + 1e-06)
        normed = (x_full * scale_inv * norm_gain).astype(jnp.bfloat16).reshape(-1, chans)

        def project(weight):
            out = jnp.dot(normed, weight, preferred_element_type=jnp.float32).astype(jnp.bfloat16)
            return out.reshape(frames, pixels, HEADS, HEAD_DIM).astype(jnp.float32)
        queries = project(w_query)
        key_rows = project(w_key)
        value_rows = project(w_value)
        scores = jnp.einsum('qphd,kphd->phqk', queries, key_rows) * scale + rel_bias[None]
        log_total = jax.nn.logsumexp(scores, axis=-1, keepdims=True)
        probs = jnp.exp(scores - log_total).astype(jnp.bfloat16).astype(jnp.float32)
        attended = jnp.einsum('phqk,kphd->qphd', probs, value_rows).astype(jnp.bfloat16)
        mixed = jnp.dot(attended.reshape(-1, chans), w_out, preferred_element_type=jnp.float32)
        block_out = (x_full + mixed.reshape(frames, pixels, chans)).astype(jnp.bfloat16)
        grad_att = jnp.dot(clip_grad.reshape(-1, chans), w_out.T, preferred_element_type=jnp.float32)
        grad_att = grad_att.astype(jnp.bfloat16).reshape(frames, pixels, HEADS, HEAD_DIM).astype(jnp.float32)
        grad_prob = jnp.einsum('qphd,kphd->phqk', grad_att, value_rows)
        row_dot = lax.optimization_barrier(jnp.sum(probs * grad_prob, axis=-1, keepdims=True))
        grad_score = probs * (grad_prob - row_dot)
        grad_scaled = (grad_score * scale).astype(jnp.bfloat16).astype(jnp.float32)
        grad_query = jnp.einsum('phqk,kphd->qphd', grad_scaled, key_rows).astype(jnp.bfloat16)
        grad_key = jnp.einsum('phqk,qphd->kphd', grad_scaled, queries).astype(jnp.bfloat16)
        grad_value = jnp.einsum('phqk,qphd->kphd', probs, grad_att).astype(jnp.bfloat16)
        grad_normed = jnp.dot(grad_query.reshape(-1, chans), w_query.T, preferred_element_type=jnp.float32)
        grad_normed = grad_normed + jnp.dot(grad_key.reshape(-1, chans), w_key.T, preferred_element_type=jnp.float32)
        grad_normed = grad_normed + jnp.dot(grad_value.reshape(-1, chans), w_value.T, preferred_element_type=jnp.float32)
        grad_normed = grad_normed.reshape(frames, pixels, chans)
        gain_grad = lax.optimization_barrier(jnp.sum(grad_normed * x_full * scale_inv, axis=(0, 1)))
        scaled_grad = grad_normed * norm_gain
        inner = lax.optimization_barrier(jnp.mean(scaled_grad * x_full, axis=-1, keepdims=True))
        input_grad = clip_grad.astype(jnp.float32) + scale_inv * scaled_grad - x_full * scale_inv ** 3 * inner
        score_sum = lax.optimization_barrier(jnp.sum(grad_score, axis=0))
        bias_grad = jnp.zeros((HEADS, 2 * frames - 1), jnp.float32).at[:, offsets].add(score_sum)
        return (block_out, input_grad.astype(jnp.bfloat16), gain_grad, bias_grad)
    block_out, input_grad, gain_grad, bias_grad = lax.map(one_clip, (inputs, out_grad))
    return (block_out, input_grad, lax.optimization_barrier(jnp.sum(gain_grad, axis=0)), lax.optimization_barrier(jnp.sum(bias_grad, axis=0)))
```

```python
import jax
import jax.numpy as jnp
from jax import lax
from jax.sharding import PartitionSpec as P


def offset_table(frames):
    query_idx = lax.iota(jnp.int32, frames)
    key_idx = lax.iota(jnp.int32, frames)
    offsets = key_idx[None, :] - query_idx[:, None] + frames - 1
    columns = lax.iota(jnp.int32, 2 * frames - 1)
    return (offsets[:, :, None] == columns[None, None, :]).astype(jnp.float32)


def shifted(value, axis, step):
    count = lax.axis_size(axis)
    return lax.ppermute(value, axis, [((i + step) % count, i) for i in range(count)])


def group_sum(value, axis):
    count = lax.axis_size(axis)
    stride = 1
    while stride < count:
        left = count // stride
        radix = 4 if left % 4 == 0 else 2 if left % 2 == 0 else left
        parts = [value]
        for step in range(1, radix):
            pairs = []
            for i in range(count):
                digit = i // stride % radix
                pairs.append((i + ((digit + step) % radix - digit) * stride, i))
            parts.append(lax.ppermute(value, axis, pairs))
        value = sum(parts[1:], parts[0])
        stride *= radix
    return value


def place(parts, axis, me, count):
    if count == 2:
        flip = me == 1
        return jnp.concatenate([jnp.where(flip, parts[1], parts[0]), jnp.where(flip, parts[0], parts[1])], axis)
    whole = jnp.concatenate(parts, axis)
    return jnp.roll(whole, me * parts[0].shape[axis], axis)


def per_device(inputs, out_grad, norm_gain, pos_bias, w_query, w_key, w_value, w_out):
    clips, frames, pixels, width = inputs.shape
    group = pos_bias.shape[0]
    tm = lax.axis_size("tm")
    me = lax.axis_index("tm")
    chans = width * tm
    head_dim = width // group
    scale = head_dim ** (-0.5)
    table = offset_table(frames)
    rel_bias = jnp.einsum("ho,qko->hqk", pos_bias, table, precision=lax.Precision.HIGHEST)
    x_parts = [inputs] + [shifted(inputs, "tm", k) for k in range(1, tm)]
    x_whole = place(x_parts, 3, me, tm).astype(jnp.float32)
    g_parts = [out_grad] + [shifted(out_grad, "tm", k) for k in range(1, tm)]
    g_whole = place(g_parts, 3, me, tm)
    scale_inv = lax.rsqrt(jnp.mean(x_whole * x_whole, axis=-1, keepdims=True) + 1e-06)
    normed = (x_whole * scale_inv * norm_gain).astype(jnp.bfloat16)

    def project(weight):
        out = jnp.einsum("bfpc,cd->bfpd", normed, weight, preferred_element_type=jnp.float32)
        return out.astype(jnp.bfloat16).reshape(clips, frames, pixels, group, head_dim)

    def heads(spec, a, b):
        return jnp.einsum(spec, a, b, preferred_element_type=jnp.float32)

    def scattered(partial):
        own = lax.dynamic_slice_in_dim(partial, me * width, width, 3)
        for k in range(1, tm):
            theirs = lax.dynamic_slice_in_dim(partial, (me + tm - k) % tm * width, width, 3)
            own = own + shifted(theirs.astype(jnp.bfloat16), "tm", k).astype(jnp.float32)
        return own

    queries, key_rows, value_rows = project(w_query), project(w_key), project(w_value)
    scores = heads("bqphd,bkphd->bphqk", queries, key_rows) * scale + rel_bias[None, None]
    log_total = jax.nn.logsumexp(scores, axis=-1, keepdims=True)
    probs = jnp.exp(scores - log_total).astype(jnp.bfloat16)
    attended = heads("bphqk,bkphd->bqphd", probs, value_rows).astype(jnp.bfloat16)
    attended = attended.reshape(clips, frames, pixels, width)
    mixed = scattered(heads("bfpd,dc->bfpc", attended, w_out))
    block_out = (inputs.astype(jnp.float32) + mixed).astype(jnp.bfloat16)

    grad_att = heads("bfpc,dc->bfpd", g_whole, w_out).astype(jnp.bfloat16)
    grad_att = grad_att.reshape(clips, frames, pixels, group, head_dim)
    grad_prob = heads("bqphd,bkphd->bphqk", grad_att, value_rows)
    probs_full = probs.astype(jnp.float32)
    row_dot = jnp.sum(probs_full * grad_prob, axis=-1, keepdims=True)
    grad_score = probs_full * (grad_prob - row_dot)
    grad_scaled = (grad_score * scale).astype(jnp.bfloat16)
    shape = (clips, frames, pixels, width)
    grad_query = heads("bphqk,bkphd->bqphd", grad_scaled, key_rows).astype(jnp.bfloat16).reshape(shape)
    grad_key = heads("bphqk,bqphd->bkphd", grad_scaled, queries).astype(jnp.bfloat16).reshape(shape)
    grad_value = heads("bphqk,bqphd->bkphd", probs, grad_att).astype(jnp.bfloat16).reshape(shape)
    partial = (
        heads("bfpd,cd->bfpc", grad_query, w_query)
        + heads("bfpd,cd->bfpc", grad_key, w_key)
        + heads("bfpd,cd->bfpc", grad_value, w_value)
    )
    scaled = partial * norm_gain
    inner = jnp.sum(scaled * x_whole, axis=-1, keepdims=True) / chans
    term = scale_inv * scaled - x_whole * scale_inv**3 * inner
    input_grad = out_grad.astype(jnp.float32) + scattered(term)

    gain_part = jnp.sum(partial * x_whole * scale_inv, axis=(0, 1, 2)).reshape(tm, width)
    bias_part = jnp.einsum(
        "hqk,qko->ho", jnp.sum(grad_score, axis=(0, 1)), table, precision=lax.Precision.HIGHEST
    )
    gain_own = lax.dynamic_index_in_dim(gain_part, me, 0, keepdims=False)
    for k in range(1, tm):
        gain_own = gain_own + shifted(
            lax.dynamic_index_in_dim(gain_part, (me + tm - k) % tm, 0, keepdims=False), "tm", k
        )
    small = jnp.concatenate([gain_own, bias_part.reshape(-1)])
    small = group_sum(group_sum(small, "dp"), "space")
    gain_grad, bias_grad = small[:width], small[width:].reshape(bias_part.shape)
    return (block_out, input_grad.astype(jnp.bfloat16), gain_grad, bias_grad)


def solution(mesh):
    return jax.shard_map(
        per_device,
        mesh=mesh,
        in_specs=(
            P("dp", None, "space", "tm"),
            P("dp", None, "space", "tm"),
            P(),
            P("tm", None),
            P(None, "tm"),
            P(None, "tm"),
            P(None, "tm"),
            P("tm", None),
        ),
        out_specs=(
            P("dp", None, "space", "tm"),
            P("dp", None, "space", "tm"),
            P("tm"),
            P("tm", None),
        ),
        check_vma=False,
    )
```

```python
import functools

import jax
import jax.numpy as jnp
from jax import lax
from jax.experimental import pallas as pl
from jax.experimental.pallas import tpu as pltpu
from jax.sharding import PartitionSpec as P

BAND = 8
LANES = 128
FAR = -1e30
F32, BF16 = jnp.float32, jnp.bfloat16
NT = (((1,), (1,)), ((), ()))
NN = (((1,), (0,)), ((), ()))
TN = (((0,), (0,)), ((), ()))
VMEM_LIMIT = 24 * 1024 * 1024


def mm(a, b, dims=NN):
    return lax.dot_general(a, b, dims, preferred_element_type=F32)


def band_rows(value, frames, pixels, band):
    value = value.astype(F32).reshape(frames, pixels // BAND, BAND, value.shape[-1])
    return value[:, band].reshape(frames * BAND, value.shape[-1])


def same_pixel(rows):
    row = lax.broadcasted_iota(jnp.int32, (BAND, rows), 0)
    lane = lax.broadcasted_iota(jnp.int32, (BAND, rows), 1)
    return (lane & (BAND - 1)) == row


def head_lanes(head_dim, rows):
    return lax.broadcasted_iota(jnp.int32, (rows, LANES), 1) // head_dim


def stack_heads(pair, owner, per_pair, factor=None):
    pair = pair if factor is None else pair * jnp.asarray(factor, pair.dtype)
    return jnp.concatenate([jnp.where(owner == h, pair, jnp.zeros_like(pair)) for h in range(per_pair)], 0)


def pick_heads(parts, owner):
    out = parts[0]
    for h in range(1, len(parts)):
        out = jnp.where(owner == h, parts[h], out)
    return out


def forward_kernel(dims, me_ref, *refs):
    tm, frames, pixels, width, group, head_dim, eps = dims
    x_refs = refs[:tm]
    gain_ref, bias_ref, wq_ref, wk_ref, wv_ref, wo_ref = refs[tm:tm + 6]
    q_ref, k_ref, v_ref, p_ref, own_ref = refs[tm + 6:tm + 11]
    msg_refs = refs[tm + 11:tm + 11 + tm - 1]
    xw_ref, mix_ref, rel_ref = refs[tm + 11 + tm - 1:]
    me = me_ref[0]
    rows = frames * BAND
    per_pair = LANES // head_dim
    scale = head_dim ** -0.5

    def place(k):
        return pl.multiple_of(lax.rem(me + k, tm) * width, width)

    for k in range(tm):
        xw_ref[:, pl.ds(place(k), width)] = x_refs[k][...]
    for i in range(frames):
        rel_ref[i] = bias_ref[:, (frames - 1 - i) * BAND:(frames - 1 - i) * BAND + rows]
    same = same_pixel(rows)[None]
    owner = head_lanes(head_dim, rows)
    for band in range(pixels // BAND):
        x = band_rows(xw_ref[...], frames, pixels, band)
        inv = lax.rsqrt(jnp.mean(x * x, axis=-1, keepdims=True) + eps)
        normed = (x * inv * gain_ref[...]).astype(BF16)
        q = mm(normed, wq_ref[...]).astype(BF16)
        k = mm(normed, wk_ref[...]).astype(BF16)
        v = mm(normed, wv_ref[...]).astype(BF16)
        q_ref[band], k_ref[band], v_ref[band] = q, k, v
        att = []
        for pair in range(width // LANES):
            cols = slice(pair * LANES, (pair + 1) * LANES)
            kp, vp = k[:, cols], v[:, cols]
            scores = mm(stack_heads(q[:, cols], owner, per_pair, scale), kp, NT)
            scores = scores.reshape(per_pair, frames, BAND, rows)
            outs = []
            for h in range(per_pair):
                head = pair * per_pair + h
                s = jnp.where(same, scores[h] + rel_ref[:, head:head + 1, :], FAR)
                s = s.reshape(rows, rows)
                e = jnp.exp(s - jnp.max(s, axis=-1, keepdims=True))
                probs = (e * (1.0 / jnp.sum(e, axis=-1, keepdims=True))).astype(BF16)
                p_ref[band, head] = probs
                outs.append(mm(probs, vp))
            att.append(pick_heads(outs, owner).astype(BF16))
        mixed = mm(jnp.concatenate(att, axis=1), wo_ref[...])
        mix_ref[:, band] = mixed.reshape(frames, BAND, mixed.shape[-1])
    total = frames * pixels
    for k in range(1, tm):
        part = mix_ref[:, :, :, pl.ds(place(tm - k), width)]
        msg_refs[k - 1][...] = part.reshape(total, width).astype(BF16)
    own = mix_ref[:, :, :, pl.ds(place(0), width)].reshape(total, width)
    own_ref[...] = own + x_refs[0][...].astype(F32)


def backward_kernel(dims, me_ref, *refs):
    tm, frames, pixels, width, group, head_dim, eps = dims
    x_refs, g_refs = refs[:tm], refs[tm:2 * tm]
    gain_ref, q_ref, k_ref, v_ref, p_ref, wq_ref, wk_ref, wv_ref, wo_ref = refs[2 * tm:2 * tm + 9]
    outs = refs[2 * tm + 9:]
    own_ref, gain_out, bias_out = outs[:3]
    msg_refs = outs[3:3 + tm - 1]
    xw_ref, gw_ref, term_ref = outs[3 + tm - 1:]
    me = me_ref[0]
    rows = frames * BAND
    per_pair = LANES // head_dim
    scale = head_dim ** -0.5
    chans = width * tm

    def place(k):
        return pl.multiple_of(lax.rem(me + k, tm) * width, width)

    for k in range(tm):
        xw_ref[:, pl.ds(place(k), width)] = x_refs[k][...]
        gw_ref[:, pl.ds(place(k), width)] = g_refs[k][...]
    owner = head_lanes(head_dim, rows)
    gain_sum = jnp.zeros((1, chans), F32)
    diag = [0.0] * group
    for band in range(pixels // BAND):
        g = band_rows(gw_ref[...], frames, pixels, band).astype(BF16)
        d_att = mm(g, wo_ref[...], NT).astype(BF16)
        dq, dk, dv = [], [], []
        for pair in range(width // LANES):
            cols = slice(pair * LANES, (pair + 1) * LANES)
            qp, kp, vp = q_ref[band, :, cols], k_ref[band, :, cols], v_ref[band, :, cols]
            da = d_att[:, cols]
            d_prob = mm(stack_heads(da, owner, per_pair), vp, NT)
            q_parts, k_parts, v_parts = [], [], []
            for h in range(per_pair):
                head = pair * per_pair + h
                probs = p_ref[band, head]
                full = probs.astype(F32)
                t = d_prob[h * rows:(h + 1) * rows]
                dot = jnp.sum(full * t, axis=-1, keepdims=True)
                score = full * (t - dot)
                diag[head] = diag[head] + jnp.sum(score.reshape(frames, BAND, rows), axis=1)
                score = (score * scale).astype(BF16)
                q_parts.append(mm(score, kp))
                k_parts.append(mm(score, qp, TN))
                v_parts.append(mm(probs, da, TN))
            dq.append(pick_heads(q_parts, owner).astype(BF16))
            dk.append(pick_heads(k_parts, owner).astype(BF16))
            dv.append(pick_heads(v_parts, owner).astype(BF16))
        grad = mm(jnp.concatenate(dq, axis=1), wq_ref[...], NT)
        grad = grad + mm(jnp.concatenate(dk, axis=1), wk_ref[...], NT)
        grad = grad + mm(jnp.concatenate(dv, axis=1), wv_ref[...], NT)
        x = band_rows(xw_ref[...], frames, pixels, band)
        inv = lax.rsqrt(jnp.mean(x * x, axis=-1, keepdims=True) + eps)
        gain_sum = gain_sum + jnp.sum(grad * x * inv, axis=0, keepdims=True)
        scaled = grad * gain_ref[...]
        inner = jnp.mean(scaled * x, axis=-1, keepdims=True)
        term = inv * scaled - x * (inv * inv * inv * inner)
        term_ref[:, band] = term.reshape(frames, BAND, chans)
    total = frames * pixels
    for k in range(1, tm):
        part = term_ref[:, :, :, pl.ds(place(tm - k), width)]
        msg_refs[k - 1][...] = part.reshape(total, width).astype(BF16)
    own = term_ref[:, :, :, pl.ds(place(0), width)].reshape(total, width)
    own_ref[...] = own + g_refs[0][...].astype(F32)
    gain_out[...] = gain_sum
    for head in range(group):
        row = jnp.zeros((1, (2 * frames - 1) * BAND), F32)
        for i in range(frames):
            row = row + jnp.pad(
                diag[head][i:i + 1], ((0, 0), ((frames - 1 - i) * BAND, i * BAND))
            )
        bias_out[head:head + 1, :] = row


def shifted(value, axis, step):
    count = lax.axis_size(axis)
    return lax.ppermute(value, axis, [((i + step) % count, i) for i in range(count)])


def per_device(inputs, out_grad, norm_gain, pos_bias, w_query, w_key, w_value, w_out):
    clips, frames, pixels, width = inputs.shape
    group = pos_bias.shape[0]
    tm = lax.axis_size("tm")
    me = lax.axis_index("tm")
    chans = width * tm
    head_dim = width // group
    total = frames * pixels
    bands = pixels // BAND
    rows = frames * BAND
    dims = (tm, frames, pixels, width, group, head_dim, 1e-06)
    x0, g0 = inputs.reshape(total, width), out_grad.reshape(total, width)
    x_parts = [x0] + [shifted(x0, "tm", k) for k in range(1, tm)]
    g_parts = [g0] + [shifted(g0, "tm", k) for k in range(1, tm)]
    me1 = me.astype(jnp.int32).reshape(1)
    gain = norm_gain.reshape(1, chans)
    spread = jnp.broadcast_to(pos_bias[:, :, None], (*pos_bias.shape, BAND)).reshape(group, -1)
    smem, vmem = pl.BlockSpec(memory_space=pltpu.SMEM), pl.BlockSpec(memory_space=pltpu.VMEM)
    params = pltpu.CompilerParams(vmem_limit_bytes=VMEM_LIMIT)
    half = jax.ShapeDtypeStruct((bands, rows, width), BF16)
    share = jax.ShapeDtypeStruct((total, width), BF16)
    own = jax.ShapeDtypeStruct((total, width), F32)
    q, k, v, probs, mix_own, *mix_out = pl.pallas_call(
        functools.partial(forward_kernel, dims),
        in_specs=[smem] + [vmem] * (tm + 6),
        out_specs=[vmem] * (5 + tm - 1),
        out_shape=[half, half, half, jax.ShapeDtypeStruct((bands, group, rows, rows), BF16), own] + [share] * (tm - 1),
        scratch_shapes=[
            pltpu.VMEM((total, chans), BF16),
            pltpu.VMEM((frames, bands, BAND, chans), F32),
            pltpu.VMEM((frames, group, rows), F32),
        ],
        compiler_params=params,
        cost_estimate=pl.CostEstimate(flops=8_000_000_000, bytes_accessed=8_000_000, transcendentals=0),
        name="attend",
    )(me1, *x_parts, gain, spread, w_query, w_key, w_value, w_out)
    mix_in = [shifted(mix_out[k - 1], "tm", k) for k in range(1, tm)]
    grad_own, gain_part, bias_part, *grad_out = pl.pallas_call(
        functools.partial(backward_kernel, dims),
        in_specs=[smem] + [vmem] * (2 * tm + 9),
        out_specs=[vmem] * (3 + tm - 1),
        out_shape=[
            own,
            jax.ShapeDtypeStruct((1, chans), F32),
            jax.ShapeDtypeStruct((group, (2 * frames - 1) * BAND), F32),
        ] + [share] * (tm - 1),
        scratch_shapes=[
            pltpu.VMEM((total, chans), BF16),
            pltpu.VMEM((total, chans), BF16),
            pltpu.VMEM((frames, bands, BAND, chans), F32),
        ],
        compiler_params=params,
        cost_estimate=pl.CostEstimate(flops=8_000_000_000, bytes_accessed=8_000_000, transcendentals=0),
        name="attend_back",
    )(me1, *x_parts, *g_parts, gain, q, k, v, probs, w_query, w_key, w_value, w_out)
    grad_in = [shifted(grad_out[k - 1], "tm", k) for k in range(1, tm)]

    bias_sum = jnp.sum(bias_part.reshape(group, -1, BAND), axis=-1)
    small = jnp.concatenate([gain_part.reshape(-1), bias_sum.reshape(-1)])
    length = -(-small.shape[0] // 1024) * 1024
    small = jnp.pad(small, (0, length - small.shape[0])).reshape(-1, LANES)
    everyone = lax.all_gather(small, ("dp", "space", "tm"), axis=0, tiled=True)
    everyone = everyone.reshape(-1, tm, length)
    gain_grad = jnp.sum(
        lax.dynamic_slice_in_dim(everyone[:, :, :chans], me * width, width, 2), axis=(0, 1)
    )
    bias_grad = jnp.sum(lax.dynamic_index_in_dim(everyone, me, 1, keepdims=False), axis=0)
    bias_grad = bias_grad[chans:chans + pos_bias.size]

    def finish(mine, others):
        for part in others:
            mine = mine + part.astype(F32)
        return mine.astype(BF16).reshape(inputs.shape)

    return (finish(mix_own, mix_in), finish(grad_own, grad_in), gain_grad, bias_grad.reshape(pos_bias.shape))


def solution(mesh):
    return jax.shard_map(
        per_device,
        mesh=mesh,
        in_specs=(
            P("dp", None, "space", "tm"),
            P("dp", None, "space", "tm"),
            P(),
            P("tm", None),
            P(None, "tm"),
            P(None, "tm"),
            P(None, "tm"),
            P("tm", None),
        ),
        out_specs=(
            P("dp", None, "space", "tm"),
            P("dp", None, "space", "tm"),
            P("tm"),
            P("tm", None),
        ),
        check_vma=False,
    )
```

```python
import functools

import jax
import jax.numpy as jnp
from jax import lax
from jax.experimental import pallas as pl
from jax.experimental.pallas import tpu as pltpu
from jax.sharding import PartitionSpec as P

BAND = 8
LANES = 128
FAR = -1e30
F32, BF16 = jnp.float32, jnp.bfloat16
NT = (((1,), (1,)), ((), ()))
NN = (((1,), (0,)), ((), ()))
TN = (((0,), (0,)), ((), ()))
VMEM_LIMIT = 24 * 1024 * 1024


def mm(a, b, dims=NN):
    return lax.dot_general(a, b, dims, preferred_element_type=F32)


def band_rows(value, frames, pixels, band):
    value = value.astype(F32).reshape(frames, pixels // BAND, BAND, value.shape[-1])
    return value[:, band].reshape(frames * BAND, value.shape[-1])


def same_pixel(rows):
    row = lax.broadcasted_iota(jnp.int32, (BAND, rows), 0)
    lane = lax.broadcasted_iota(jnp.int32, (BAND, rows), 1)
    return (lane & (BAND - 1)) == row


def head_lanes(head_dim, rows):
    return lax.broadcasted_iota(jnp.int32, (rows, LANES), 1) // head_dim


def stack_heads(pair, owner, per_pair, factor=None):
    pair = pair if factor is None else pair * jnp.asarray(factor, pair.dtype)
    return jnp.concatenate([jnp.where(owner == h, pair, jnp.zeros_like(pair)) for h in range(per_pair)], 0)


def pick_heads(parts, owner):
    out = parts[0]
    for h in range(1, len(parts)):
        out = jnp.where(owner == h, parts[h], out)
    return out


def stage_kernel(count, frames, bias_ref, *refs):
    sources, rel_ref, targets, sems = refs[:count], refs[count], refs[count + 1:2 * count + 1], refs[2 * count + 1]
    copies = [pltpu.make_async_copy(s, t, sems.at[n]) for n, (s, t) in enumerate(zip(sources, targets))]
    for copy in copies:
        copy.start()
    rows = rel_ref.shape[2]
    for i in range(frames):
        start = (frames - 1 - i) * BAND
        rel_ref[i] = bias_ref[:, start:start + rows]
    for copy in copies:
        copy.wait()


def forward_kernel(dims, me_ref, *refs):
    tm, frames, pixels, width, group, head_dim, eps = dims
    x_refs = refs[:tm]
    gain_ref, rel_ref, wq_ref, wk_ref, wv_ref, wo_ref = refs[tm:tm + 6]
    q_ref, k_ref, v_ref, p_ref, own_ref = refs[tm + 6:tm + 11]
    msg_refs = refs[tm + 11:tm + 11 + tm - 1]
    xw_ref, mix_ref = refs[tm + 11 + tm - 1:]
    me = me_ref[0]
    rows = frames * BAND
    per_pair = LANES // head_dim
    scale = head_dim ** -0.5

    def place(k):
        return pl.multiple_of(lax.rem(me + k, tm) * width, width)

    for k in range(tm):
        xw_ref[:, pl.ds(place(k), width)] = x_refs[k][...]
    same = same_pixel(rows)[None]
    owner = head_lanes(head_dim, rows)
    for band in range(pixels // BAND):
        x = band_rows(xw_ref[...], frames, pixels, band)
        inv = lax.rsqrt(jnp.mean(x * x, axis=-1, keepdims=True) + eps)
        normed = (x * inv * gain_ref[...]).astype(BF16)
        q = mm(normed, wq_ref[...]).astype(BF16)
        k = mm(normed, wk_ref[...]).astype(BF16)
        v = mm(normed, wv_ref[...]).astype(BF16)
        q_ref[band], k_ref[band], v_ref[band] = q, k, v
        att = []
        for pair in range(width // LANES):
            cols = slice(pair * LANES, (pair + 1) * LANES)
            kp, vp = k[:, cols], v[:, cols]
            scores = mm(stack_heads(q[:, cols], owner, per_pair, scale), kp, NT)
            scores = scores.reshape(per_pair, frames, BAND, rows)
            outs = []
            for h in range(per_pair):
                head = pair * per_pair + h
                s = jnp.where(same, scores[h] + rel_ref[:, head:head + 1, :], FAR)
                s = s.reshape(rows, rows)
                e = jnp.exp(s - jnp.max(s, axis=-1, keepdims=True))
                probs = (e * (1.0 / jnp.sum(e, axis=-1, keepdims=True))).astype(BF16)
                p_ref[band, head] = probs
                outs.append(mm(probs, vp))
            att.append(pick_heads(outs, owner).astype(BF16))
        mixed = mm(jnp.concatenate(att, axis=1), wo_ref[...])
        mix_ref[:, band] = mixed.reshape(frames, BAND, mixed.shape[-1])
    total = frames * pixels
    for k in range(1, tm):
        part = mix_ref[:, :, :, pl.ds(place(tm - k), width)]
        msg_refs[k - 1][...] = part.reshape(total, width).astype(BF16)
    own = mix_ref[:, :, :, pl.ds(place(0), width)].reshape(total, width)
    own_ref[...] = own + x_refs[0][...].astype(F32)


def backward_kernel(dims, me_ref, *refs):
    tm, frames, pixels, width, group, head_dim, eps = dims
    x_refs, g_refs = refs[:tm], refs[tm:2 * tm]
    gain_ref, q_ref, k_ref, v_ref, p_ref, wq_ref, wk_ref, wv_ref, wo_ref = refs[2 * tm:2 * tm + 9]
    outs = refs[2 * tm + 9:]
    own_ref, small_ref = outs[:2]
    msg_refs = outs[2:2 + tm - 1]
    xw_ref, gw_ref, term_ref = outs[2 + tm - 1:]
    me = me_ref[0]
    rows = frames * BAND
    per_pair = LANES // head_dim
    scale = head_dim ** -0.5
    chans = width * tm

    def place(k):
        return pl.multiple_of(lax.rem(me + k, tm) * width, width)

    for k in range(tm):
        xw_ref[:, pl.ds(place(k), width)] = x_refs[k][...]
        gw_ref[:, pl.ds(place(k), width)] = g_refs[k][...]
    owner = head_lanes(head_dim, rows)
    gain_sum = jnp.zeros((1, chans), F32)
    diag = [0.0] * group
    for band in range(pixels // BAND):
        g = band_rows(gw_ref[...], frames, pixels, band).astype(BF16)
        d_att = mm(g, wo_ref[...], NT).astype(BF16)
        dq, dk, dv = [], [], []
        for pair in range(width // LANES):
            cols = slice(pair * LANES, (pair + 1) * LANES)
            qp, kp, vp = q_ref[band, :, cols], k_ref[band, :, cols], v_ref[band, :, cols]
            da = d_att[:, cols]
            d_prob = mm(stack_heads(da, owner, per_pair), vp, NT)
            q_parts, k_parts, v_parts = [], [], []
            for h in range(per_pair):
                head = pair * per_pair + h
                probs = p_ref[band, head]
                full = probs.astype(F32)
                t = d_prob[h * rows:(h + 1) * rows]
                dot = jnp.sum(full * t, axis=-1, keepdims=True)
                score = full * (t - dot)
                diag[head] = diag[head] + jnp.sum(score.reshape(frames, BAND, rows), axis=1)
                score = (score * scale).astype(BF16)
                q_parts.append(mm(score, kp))
                k_parts.append(mm(score, qp, TN))
                v_parts.append(mm(probs, da, TN))
            dq.append(pick_heads(q_parts, owner).astype(BF16))
            dk.append(pick_heads(k_parts, owner).astype(BF16))
            dv.append(pick_heads(v_parts, owner).astype(BF16))
        grad = mm(jnp.concatenate(dq, axis=1), wq_ref[...], NT)
        grad = grad + mm(jnp.concatenate(dk, axis=1), wk_ref[...], NT)
        grad = grad + mm(jnp.concatenate(dv, axis=1), wv_ref[...], NT)
        x = band_rows(xw_ref[...], frames, pixels, band)
        inv = lax.rsqrt(jnp.mean(x * x, axis=-1, keepdims=True) + eps)
        gain_sum = gain_sum + jnp.sum(grad * x * inv, axis=0, keepdims=True)
        scaled = grad * gain_ref[...]
        inner = jnp.mean(scaled * x, axis=-1, keepdims=True)
        term = inv * scaled - x * (inv * inv * inv * inner)
        term_ref[:, band] = term.reshape(frames, BAND, chans)
    total = frames * pixels
    for k in range(1, tm):
        part = term_ref[:, :, :, pl.ds(place(tm - k), width)]
        msg_refs[k - 1][...] = part.reshape(total, width).astype(BF16)
    own = term_ref[:, :, :, pl.ds(place(0), width)].reshape(total, width)
    own_ref[...] = own + g_refs[0][...].astype(F32)
    offsets = 2 * frames - 1
    span = offsets * BAND
    gain_rows = width // LANES
    per_row = LANES // offsets
    small_ref[...] = jnp.zeros_like(small_ref)
    for t in range(tm):
        for r in range(gain_rows):
            start = t * width + r * LANES
            small_ref[t, r:r + 1, :] = gain_sum[:, start:start + LANES]
    lane = lax.broadcasted_iota(jnp.int32, (span, LANES), 1)
    offset = lax.broadcasted_iota(jnp.int32, (span, LANES), 0) // BAND
    for first in range(0, group, per_row):
        packed = jnp.zeros((1, LANES), F32)
        for head in range(first, min(first + per_row, group)):
            row = jnp.zeros((1, span), F32)
            for i in range(frames):
                row = row + jnp.pad(diag[head][i:i + 1], ((0, 0), ((frames - 1 - i) * BAND, i * BAND)))
            put = (lane == offset + (head - first) * offsets).astype(F32)
            packed = packed + lax.dot_general(
                row, put, NN, precision=lax.Precision.HIGHEST, preferred_element_type=F32
            )
        line = gain_rows + first // per_row
        small_ref[pl.ds(me, 1), line:line + 1, :] = packed[None]


def shifted(value, axis, step):
    count = lax.axis_size(axis)
    return lax.ppermute(value, axis, [((i + step) % count, i) for i in range(count)])


def per_device(inputs, out_grad, norm_gain, pos_bias, w_query, w_key, w_value, w_out):
    clips, frames, pixels, width = inputs.shape
    group = pos_bias.shape[0]
    tm = lax.axis_size("tm")
    me = lax.axis_index("tm")
    chans = width * tm
    head_dim = width // group
    total = frames * pixels
    bands = pixels // BAND
    rows = frames * BAND
    offsets = 2 * frames - 1
    per_row = LANES // offsets
    gain_rows, bias_rows = width // LANES, -(-group // per_row)
    lines = -(-(gain_rows + bias_rows) // BAND) * BAND
    dims = (tm, frames, pixels, width, group, head_dim, 1e-06)
    x0, g0 = inputs.reshape(total, width), out_grad.reshape(total, width)
    x_parts = [x0] + [shifted(x0, "tm", k) for k in range(1, tm)]
    g_parts = [g0] + [shifted(g0, "tm", k) for k in range(1, tm)]
    me1 = me.astype(jnp.int32).reshape(1)
    gain = norm_gain.reshape(1, chans)
    spread = jnp.broadcast_to(pos_bias[:, :, None], (*pos_bias.shape, BAND)).reshape(group, -1)
    smem, vmem = pl.BlockSpec(memory_space=pltpu.SMEM), pl.BlockSpec(memory_space=pltpu.VMEM)
    params = pltpu.CompilerParams(vmem_limit_bytes=VMEM_LIMIT)
    held = [x0, w_query, w_key, w_value, w_out, g0, gain]
    rel, *held = pl.pallas_call(
        functools.partial(stage_kernel, len(held), frames),
        in_specs=[vmem] + [pl.BlockSpec(memory_space=pltpu.HBM)] * len(held),
        out_specs=[vmem] * (1 + len(held)),
        out_shape=[jax.ShapeDtypeStruct((frames, group, rows), F32)]
        + [jax.ShapeDtypeStruct(h.shape, h.dtype) for h in held],
        scratch_shapes=[pltpu.SemaphoreType.DMA((len(held),))],
        compiler_params=params,
        cost_estimate=pl.CostEstimate(flops=0, bytes_accessed=8_000_000, transcendentals=0),
        name="stage",
    )(spread, *held)
    x0, w_query, w_key, w_value, w_out, g0, gain = held
    x_parts[0], g_parts[0] = x0, g0
    half = jax.ShapeDtypeStruct((bands, rows, width), BF16)
    share = jax.ShapeDtypeStruct((total, width), BF16)
    own = jax.ShapeDtypeStruct((total, width), F32)
    q, k, v, probs, mix_own, *mix_out = pl.pallas_call(
        functools.partial(forward_kernel, dims),
        in_specs=[smem] + [vmem] * (tm + 6),
        out_specs=[vmem] * (5 + tm - 1),
        out_shape=[half, half, half, jax.ShapeDtypeStruct((bands, group, rows, rows), BF16), own] + [share] * (tm - 1),
        scratch_shapes=[
            pltpu.VMEM((total, chans), BF16),
            pltpu.VMEM((frames, bands, BAND, chans), F32),
        ],
        compiler_params=params,
        cost_estimate=pl.CostEstimate(flops=8_000_000_000, bytes_accessed=8_000_000, transcendentals=0),
        name="attend",
    )(me1, *x_parts, gain, rel, w_query, w_key, w_value, w_out)
    mix_in = [shifted(mix_out[k - 1], "tm", k) for k in range(1, tm)]
    grad_own, small, *grad_out = pl.pallas_call(
        functools.partial(backward_kernel, dims),
        in_specs=[smem] + [vmem] * (2 * tm + 9),
        out_specs=[vmem] * (2 + tm - 1),
        out_shape=[own, jax.ShapeDtypeStruct((tm, lines, LANES), F32)] + [share] * (tm - 1),
        scratch_shapes=[
            pltpu.VMEM((total, chans), BF16),
            pltpu.VMEM((total, chans), BF16),
            pltpu.VMEM((frames, bands, BAND, chans), F32),
        ],
        compiler_params=params,
        cost_estimate=pl.CostEstimate(flops=8_000_000_000, bytes_accessed=8_000_000, transcendentals=0),
        name="attend_back",
    )(me1, *x_parts, *g_parts, gain, q, k, v, probs, w_query, w_key, w_value, w_out)
    grad_in = [shifted(grad_out[k - 1], "tm", k) for k in range(1, tm)]

    axes = ("dp", "space", "tm")
    others = lax.axis_size(axes) // tm
    small = jnp.broadcast_to(small[None], (others, tm, lines, LANES)).reshape(-1, LANES)
    small = lax.all_to_all(small, axes, split_axis=0, concat_axis=0, tiled=True)
    small = jnp.sum(small.reshape(-1, lines, LANES), axis=0)
    gain_grad = small[:gain_rows].reshape(width)
    bias_grad = small[gain_rows:gain_rows + bias_rows, :per_row * offsets].reshape(-1, offsets)[:group]

    def finish(mine, others):
        for part in others:
            mine = mine + part.astype(F32)
        return mine.astype(BF16).reshape(inputs.shape)

    return (finish(mix_own, mix_in), finish(grad_own, grad_in), gain_grad, bias_grad)


def solution(mesh):
    return jax.shard_map(
        per_device,
        mesh=mesh,
        in_specs=(
            P("dp", None, "space", "tm"),
            P("dp", None, "space", "tm"),
            P(),
            P("tm", None),
            P(None, "tm"),
            P(None, "tm"),
            P(None, "tm"),
            P("tm", None),
        ),
        out_specs=(
            P("dp", None, "space", "tm"),
            P("dp", None, "space", "tm"),
            P("tm"),
            P("tm", None),
        ),
        check_vma=False,
    )
```

```python
import functools

import jax
import jax.numpy as jnp
from jax import lax
from jax.experimental import pallas as pl
from jax.experimental.pallas import tpu as pltpu
from jax.sharding import PartitionSpec as P

BAND = 8
LANES = 128
FAR = -1e30
F32, BF16 = jnp.float32, jnp.bfloat16
NT = (((1,), (1,)), ((), ()))
NN = (((1,), (0,)), ((), ()))
TN = (((0,), (0,)), ((), ()))
VMEM_LIMIT = 24 * 1024 * 1024


def mm(a, b, dims=NN):
    return lax.dot_general(a, b, dims, preferred_element_type=F32)


def band_rows(value, frames, pixels, band):
    value = value.astype(F32).reshape(frames, pixels // BAND, BAND, value.shape[-1])
    return value[:, band].reshape(frames * BAND, value.shape[-1])


def same_pixel(rows):
    row = lax.broadcasted_iota(jnp.int32, (BAND, rows), 0)
    lane = lax.broadcasted_iota(jnp.int32, (BAND, rows), 1)
    return (lane & (BAND - 1)) == row


def head_lanes(head_dim, rows):
    return lax.broadcasted_iota(jnp.int32, (rows, LANES), 1) // head_dim


def stack_heads(pair, owner, per_pair, factor=None):
    pair = pair if factor is None else pair * jnp.asarray(factor, pair.dtype)
    return jnp.concatenate([jnp.where(owner == h, pair, jnp.zeros_like(pair)) for h in range(per_pair)], 0)


def pick_heads(parts, owner):
    out = parts[0]
    for h in range(1, len(parts)):
        out = jnp.where(owner == h, parts[h], out)
    return out


def stage_kernel(count, frames, bias_ref, *refs):
    sources, rel_ref, targets, sems = refs[:count], refs[count], refs[count + 1:2 * count + 1], refs[2 * count + 1]
    copies = [pltpu.make_async_copy(s, t, sems.at[n]) for n, (s, t) in enumerate(zip(sources, targets))]
    for copy in copies:
        copy.start()
    rows = rel_ref.shape[2]
    for i in range(frames):
        start = (frames - 1 - i) * BAND
        rel_ref[i] = bias_ref[:, start:start + rows]
    for copy in copies:
        copy.wait()


def forward_kernel(dims, me_ref, *refs):
    tm, frames, pixels, width, group, head_dim, eps = dims
    x_refs = refs[:tm]
    gain_ref, rel_ref, wq_ref, wk_ref, wv_ref, wo_ref = refs[tm:tm + 6]
    q_ref, k_ref, v_ref, p_ref, xb_ref, inv_ref, own_ref = refs[tm + 6:tm + 13]
    msg_refs = refs[tm + 13:tm + 13 + tm - 1]
    xw_ref, mix_ref = refs[tm + 13 + tm - 1:]
    me = me_ref[0]
    rows = frames * BAND
    per_pair = LANES // head_dim
    scale = head_dim ** -0.5

    def place(k):
        return pl.multiple_of(lax.rem(me + k, tm) * width, width)

    for k in range(tm):
        xw_ref[:, pl.ds(place(k), width)] = x_refs[k][...]
    same = same_pixel(rows)[None]
    owner = head_lanes(head_dim, rows)
    for band in range(pixels // BAND):
        x = band_rows(xw_ref[...], frames, pixels, band)
        inv = lax.rsqrt(jnp.mean(x * x, axis=-1, keepdims=True) + eps)
        normed = (x * inv * gain_ref[...]).astype(BF16)
        xb_ref[band] = x.astype(BF16)
        inv_ref[band] = jnp.broadcast_to(inv, (rows, LANES))
        q = mm(normed, wq_ref[...]).astype(BF16)
        k = mm(normed, wk_ref[...]).astype(BF16)
        v = mm(normed, wv_ref[...]).astype(BF16)
        q_ref[band], k_ref[band], v_ref[band] = q, k, v
        att = []
        for pair in range(width // LANES):
            cols = slice(pair * LANES, (pair + 1) * LANES)
            kp, vp = k[:, cols], v[:, cols]
            scores = mm(stack_heads(q[:, cols], owner, per_pair, scale), kp, NT)
            scores = scores.reshape(per_pair, frames, BAND, rows)
            outs = []
            for h in range(per_pair):
                head = pair * per_pair + h
                s = jnp.where(same, scores[h] + rel_ref[:, head:head + 1, :], FAR)
                s = s.reshape(rows, rows)
                e = jnp.exp(s - jnp.max(s, axis=-1, keepdims=True))
                probs = (e * (1.0 / jnp.sum(e, axis=-1, keepdims=True))).astype(BF16)
                p_ref[band, head] = probs
                outs.append(mm(probs, vp))
            att.append(pick_heads(outs, owner).astype(BF16))
        mixed = mm(jnp.concatenate(att, axis=1), wo_ref[...])
        mix_ref[:, band] = mixed.reshape(frames, BAND, mixed.shape[-1])
    total = frames * pixels
    for k in range(1, tm):
        part = mix_ref[:, :, :, pl.ds(place(tm - k), width)]
        msg_refs[k - 1][...] = part.reshape(total, width).astype(BF16)
    own = mix_ref[:, :, :, pl.ds(place(0), width)].reshape(total, width)
    own_ref[...] = own + x_refs[0][...].astype(F32)


def backward_kernel(dims, band, last, me_ref, *refs):
    tm, frames, pixels, width, group, head_dim, eps = dims
    g_refs = refs[:tm]
    gain_ref, q_ref, k_ref, v_ref, p_ref, xb_ref, inv_ref, wq_ref, wk_ref, wv_ref, wo_ref = refs[tm:tm + 11]
    rest = list(refs[tm + 11:])
    carried = (rest.pop(0), rest.pop(0)) if band else None
    own_ref = rest.pop(0)
    msg_refs = [rest.pop(0) for _ in range(tm - 1)]
    outs = [rest.pop(0)] if last else [rest.pop(0), rest.pop(0)]
    gw_ref, term_ref = rest
    me = me_ref[0]
    rows = frames * BAND
    per_pair = LANES // head_dim
    scale = head_dim ** -0.5

    def place(k):
        return pl.multiple_of(lax.rem(me + k, tm) * width, width)

    for k in range(tm):
        gw_ref[:, pl.ds(place(k), width)] = g_refs[k][...]
    owner = head_lanes(head_dim, rows)
    d_att = mm(gw_ref[...], wo_ref[...], NT).astype(BF16)
    dq, dk, dv, diag = [], [], [], []
    for pair in range(width // LANES):
        cols = slice(pair * LANES, (pair + 1) * LANES)
        qp, kp, vp = q_ref[band, :, cols], k_ref[band, :, cols], v_ref[band, :, cols]
        da = d_att[:, cols]
        d_prob = mm(stack_heads(da, owner, per_pair), vp, NT)
        q_parts, k_parts, v_parts = [], [], []
        for h in range(per_pair):
            head = pair * per_pair + h
            probs = p_ref[band, head]
            full = probs.astype(F32)
            t = d_prob[h * rows:(h + 1) * rows]
            dot = jnp.sum(full * t, axis=-1, keepdims=True)
            score = full * (t - dot)
            part = jnp.sum(score.reshape(frames, BAND, rows), axis=1)
            diag.append(part if carried is None else part + carried[1][head])
            score = (score * scale).astype(BF16)
            q_parts.append(mm(score, kp))
            k_parts.append(mm(score, qp, TN))
            v_parts.append(mm(probs, da, TN))
        dq.append(pick_heads(q_parts, owner).astype(BF16))
        dk.append(pick_heads(k_parts, owner).astype(BF16))
        dv.append(pick_heads(v_parts, owner).astype(BF16))
    grad = mm(jnp.concatenate(dq, axis=1), wq_ref[...], NT)
    grad = grad + mm(jnp.concatenate(dk, axis=1), wk_ref[...], NT)
    grad = grad + mm(jnp.concatenate(dv, axis=1), wv_ref[...], NT)
    x = xb_ref[band].astype(F32)
    inv = inv_ref[band][:, :1]
    gain_sum = jnp.sum(grad * x * inv, axis=0, keepdims=True)
    if carried is not None:
        gain_sum = gain_sum + carried[0][...]
    scaled = grad * gain_ref[...]
    inner = jnp.mean(scaled * x, axis=-1, keepdims=True)
    term_ref[...] = inv * scaled - x * (inv * inv * inv * inner)
    for k in range(1, tm):
        msg_refs[k - 1][...] = term_ref[:, pl.ds(place(tm - k), width)].astype(BF16)
    own_ref[...] = term_ref[:, pl.ds(place(0), width)] + g_refs[0][...].astype(F32)
    if not last:
        outs[0][...] = gain_sum
        for head in range(group):
            outs[1][head] = diag[head]
        return
    small_ref = outs[0]
    copies, lines = small_ref.shape[0], small_ref.shape[2]
    offsets = 2 * frames - 1
    span = offsets * BAND
    gain_rows = width // LANES
    per_row = LANES // offsets
    lane = lax.broadcasted_iota(jnp.int32, (span, LANES), 1)
    offset = lax.broadcasted_iota(jnp.int32, (span, LANES), 0) // BAND
    packed_rows = []
    for first in range(0, group, per_row):
        packed = jnp.zeros((1, LANES), F32)
        for head in range(first, min(first + per_row, group)):
            row = jnp.zeros((1, span), F32)
            for i in range(frames):
                row = row + jnp.pad(diag[head][i:i + 1], ((0, 0), ((frames - 1 - i) * BAND, i * BAND)))
            put = (lane == offset + (head - first) * offsets).astype(F32)
            packed = packed + lax.dot_general(
                row, put, NN, precision=lax.Precision.HIGHEST, preferred_element_type=F32
            )
        packed_rows.append(packed)
    filler = [jnp.zeros((1, LANES), F32)] * (lines - gain_rows - len(packed_rows))
    for t in range(tm):
        block = [gain_sum[:, t * width + r * LANES:t * width + (r + 1) * LANES] for r in range(gain_rows)]
        block += [jnp.where(me == t, row, 0.0) for row in packed_rows] + filler
        block = jnp.concatenate(block, axis=0)
        for c in range(copies):
            small_ref[c, t] = block


def finish_kernel(bands, frames, *refs):
    own_refs, in_refs, out_ref = refs[:bands], refs[bands:-1], refs[-1]
    each = len(in_refs) // bands
    parts = []
    for band in range(bands):
        value = own_refs[band][...]
        for ref in in_refs[band * each:(band + 1) * each]:
            value = value + ref[...].astype(F32)
        parts.append(value.reshape(frames, 1, BAND, value.shape[-1]))
    value = jnp.concatenate(parts, axis=1)
    out_ref[...] = value.reshape(out_ref.shape).astype(out_ref.dtype)


def sums_kernel(gain_rows, bias_rows, *refs):
    *block_refs, gain_ref, bias_ref = refs
    total = block_refs[0][...]
    for ref in block_refs[1:]:
        total = total + ref[...]
    for r in range(gain_rows):
        gain_ref[:, r * LANES:(r + 1) * LANES] = total[r:r + 1]
    group, offsets = bias_ref.shape
    per_row = LANES // offsets
    for head in range(group):
        line, start = gain_rows + head // per_row, head % per_row * offsets
        bias_ref[head:head + 1, :] = total[line:line + 1, start:start + offsets]


def shifted(value, axis, step):
    count = lax.axis_size(axis)
    return lax.ppermute(value, axis, [((i + step) % count, i) for i in range(count)])


def per_device(inputs, out_grad, norm_gain, pos_bias, w_query, w_key, w_value, w_out):
    clips, frames, pixels, width = inputs.shape
    group = pos_bias.shape[0]
    tm = lax.axis_size("tm")
    me = lax.axis_index("tm")
    chans = width * tm
    head_dim = width // group
    total = frames * pixels
    bands = pixels // BAND
    rows = frames * BAND
    offsets = 2 * frames - 1
    per_row = LANES // offsets
    gain_rows, bias_rows = width // LANES, -(-group // per_row)
    lines = -(-(gain_rows + bias_rows) // BAND) * BAND
    dims = (tm, frames, pixels, width, group, head_dim, 1e-06)
    x0 = inputs.reshape(total, width)
    g_bands = [out_grad[:, :, n * BAND:(n + 1) * BAND].reshape(rows, width) for n in range(bands)]
    x_parts = [x0] + [shifted(x0, "tm", k) for k in range(1, tm)]
    g_parts = [[g] + [shifted(g, "tm", k) for k in range(1, tm)] for g in g_bands]
    me1 = me.astype(jnp.int32).reshape(1)
    gain = norm_gain.reshape(1, chans)
    spread = jnp.broadcast_to(pos_bias[:, :, None], (*pos_bias.shape, BAND)).reshape(group, -1)
    smem, vmem = pl.BlockSpec(memory_space=pltpu.SMEM), pl.BlockSpec(memory_space=pltpu.VMEM)
    params = pltpu.CompilerParams(vmem_limit_bytes=VMEM_LIMIT)
    held = [x0, w_query, w_key, w_value, w_out, gain]
    held = [pltpu.with_memory_space_constraint(h, pltpu.HBM) for h in held]
    rel, x0, *weights, gain = pl.pallas_call(
        functools.partial(stage_kernel, len(held), frames),
        in_specs=[vmem] + [pl.BlockSpec(memory_space=pltpu.HBM)] * len(held),
        out_specs=[vmem] * (1 + len(held)),
        out_shape=[jax.ShapeDtypeStruct((frames, group, rows), F32)]
        + [jax.ShapeDtypeStruct(h.shape, h.dtype) for h in held],
        scratch_shapes=[pltpu.SemaphoreType.DMA((len(held),))],
        compiler_params=params,
        cost_estimate=pl.CostEstimate(flops=0, bytes_accessed=8_000_000, transcendentals=0),
        name="stage",
    )(spread, *held)
    x_parts[0] = x0
    half = jax.ShapeDtypeStruct((bands, rows, width), BF16)
    share = jax.ShapeDtypeStruct((total, width), BF16)
    q, k, v, probs, xb, inv, mix_own, *mix_out = pl.pallas_call(
        functools.partial(forward_kernel, dims),
        in_specs=[smem] + [vmem] * (tm + 6),
        out_specs=[vmem] * (7 + tm - 1),
        out_shape=[
            half, half, half,
            jax.ShapeDtypeStruct((bands, group, rows, rows), BF16),
            jax.ShapeDtypeStruct((bands, rows, chans), BF16),
            jax.ShapeDtypeStruct((bands, rows, LANES), F32),
            jax.ShapeDtypeStruct((total, width), F32),
        ] + [share] * (tm - 1),
        scratch_shapes=[
            pltpu.VMEM((total, chans), BF16),
            pltpu.VMEM((frames, bands, BAND, chans), F32),
        ],
        compiler_params=params,
        cost_estimate=pl.CostEstimate(flops=4_000_000_000, bytes_accessed=8_000_000, transcendentals=0),
        name="attend",
    )(me1, *x_parts, gain, rel, *weights)
    mix_in = [shifted(mix_out[k - 1], "tm", k) for k in range(1, tm)]

    others = lax.axis_size(("dp", "space"))
    copies = others if others <= 64 else 1
    owns, ins, carry = [], [], []
    for band in range(bands):
        last = band == bands - 1
        if last:
            extra = [jax.ShapeDtypeStruct((copies, tm, lines, LANES), F32)]
        else:
            extra = [jax.ShapeDtypeStruct((1, chans), F32), jax.ShapeDtypeStruct((group, frames, rows), F32)]
        own, *rest = pl.pallas_call(
            functools.partial(backward_kernel, dims, band, last),
            in_specs=[smem] + [vmem] * (tm + 11 + len(carry)),
            out_specs=[vmem] * (tm + len(extra)),
            out_shape=[jax.ShapeDtypeStruct((rows, width), F32)]
            + [jax.ShapeDtypeStruct((rows, width), BF16)] * (tm - 1) + extra,
            scratch_shapes=[pltpu.VMEM((rows, chans), BF16), pltpu.VMEM((rows, chans), F32)],
            compiler_params=params,
            cost_estimate=pl.CostEstimate(flops=4_000_000_000, bytes_accessed=4_000_000, transcendentals=0),
            name="attend_back",
        )(me1, *g_parts[band], gain, q, k, v, probs, xb, inv, *weights, *carry)
        sent, carry = rest[:tm - 1], rest[tm - 1:]
        if last:
            sent, mix_in = lax.optimization_barrier((sent, mix_in))
        owns.append(own)
        ins += [shifted(sent[k - 1], "tm", k) for k in range(1, tm)]

    small = carry[0]
    if copies < others:
        small = jnp.broadcast_to(small, (others, *small.shape[1:]))
    small = lax.all_to_all(small.reshape(-1, LANES), ("dp", "space"), split_axis=0, concat_axis=0, tiled=True)
    small = jnp.sum(small.reshape(others, tm, lines, LANES), axis=0)
    blocks = [lax.dynamic_index_in_dim(small, me, 0, keepdims=False)]
    for k in range(1, tm):
        theirs = lax.dynamic_index_in_dim(small, (me + tm - k) % tm, 0, keepdims=False)
        blocks.append(shifted(theirs, "tm", k))
    gain_grad, bias_grad = pl.pallas_call(
        functools.partial(sums_kernel, gain_rows, bias_rows),
        in_specs=[vmem] * tm,
        out_specs=[vmem] * 2,
        out_shape=[jax.ShapeDtypeStruct((1, width), F32), jax.ShapeDtypeStruct((group, offsets), F32)],
        name="sums",
    )(*blocks)
    input_grad = pl.pallas_call(
        functools.partial(finish_kernel, bands, frames),
        in_specs=[vmem] * (bands * tm),
        out_specs=vmem,
        out_shape=jax.ShapeDtypeStruct((total, width), BF16),
        compiler_params=params,
        name="finish",
    )(*owns, *ins)
    mixed = mix_own
    for part in mix_in:
        mixed = mixed + part.astype(F32)
    return (
        mixed.astype(BF16).reshape(inputs.shape),
        input_grad.reshape(inputs.shape),
        gain_grad.reshape(width),
        bias_grad,
    )


def solution(mesh):
    return jax.shard_map(
        per_device,
        mesh=mesh,
        in_specs=(
            P("dp", None, "space", "tm"),
            P("dp", None, "space", "tm"),
            P(),
            P("tm", None),
            P(None, "tm"),
            P(None, "tm"),
            P(None, "tm"),
            P("tm", None),
        ),
        out_specs=(
            P("dp", None, "space", "tm"),
            P("dp", None, "space", "tm"),
            P("tm"),
            P("tm", None),
        ),
        check_vma=False,
    )
```

```python
import functools

import jax
import jax.numpy as jnp
from jax import lax
from jax.experimental import pallas as pl
from jax.experimental.pallas import tpu as pltpu
from jax.sharding import PartitionSpec as P

CHUNK = 4
BAND = 8
LANES = 128
FAR = -1e30
F32, BF16 = jnp.float32, jnp.bfloat16
NT = (((1,), (1,)), ((), ()))
NN = (((1,), (0,)), ((), ()))
TN = (((0,), (0,)), ((), ()))
VMEM_LIMIT = 24 * 1024 * 1024


def mm(a, b, dims=NN):
    return lax.dot_general(a, b, dims, preferred_element_type=F32)


def same_pixel(rows):
    row = lax.broadcasted_iota(jnp.int32, (BAND, rows), 0)
    lane = lax.broadcasted_iota(jnp.int32, (BAND, rows), 1)
    return (lane & (BAND - 1)) == row


def head_lanes(head_dim, rows):
    return lax.broadcasted_iota(jnp.int32, (rows, LANES), 1) // head_dim


def stack_heads(pair, owner, per_pair, factor=None):
    pair = pair if factor is None else pair * jnp.asarray(factor, pair.dtype)
    return jnp.concatenate([jnp.where(owner == h, pair, jnp.zeros_like(pair)) for h in range(per_pair)], 0)


def pick_heads(parts, owner):
    out = parts[0]
    for h in range(1, len(parts)):
        out = jnp.where(owner == h, parts[h], out)
    return out


def stage_kernel(frames, width, bias_ref, x_ref, wq_ref, wk_ref, wv_ref, wo_ref, gain_ref,
                 rel_ref, x_out, proj_out, wo_out, gain_out, sems):
    pairs = [(x_ref, x_out), (wo_ref, wo_out), (gain_ref, gain_out)]
    pairs += [(w, proj_out.at[:, n * width:(n + 1) * width]) for n, w in enumerate((wq_ref, wk_ref, wv_ref))]
    copies = [pltpu.make_async_copy(source, target, sems.at[n]) for n, (source, target) in enumerate(pairs)]
    for copy in copies:
        copy.start()
    rows = rel_ref.shape[2]
    for i in range(frames):
        start = (frames - 1 - i) * BAND
        rel_ref[i] = bias_ref[:, start:start + rows]
    for copy in copies:
        copy.wait()


def forward_kernel(dims, me_ref, *refs):
    tm, frames, pixels, width, group, head_dim, eps = dims
    x_refs = refs[:tm]
    gain_ref, rel_ref, proj_ref, wo_ref = refs[tm:tm + 4]
    qkv_ref, p_ref, xb_ref, inv_ref, own_ref = refs[tm + 4:tm + 9]
    msg_refs = refs[tm + 9:tm + 9 + tm - 1]
    xw_ref, normed_ref = refs[tm + 9 + tm - 1:]
    me = me_ref[0]
    rows = frames * BAND
    bands = pixels // BAND
    per_pair = LANES // head_dim
    scale = head_dim ** -0.5

    def place(k):
        return pl.multiple_of(lax.rem(me + k, tm) * width, width)

    for k in range(tm):
        xw_ref[:, pl.ds(place(k), width)] = x_refs[k][...]
    for f in range(0, frames, 2):
        both = xw_ref[f * pixels:(f + 2) * pixels, :].astype(F32).reshape(2, bands, BAND, -1)
        for band in range(bands):
            x = both[:, band].reshape(2 * BAND, -1)
            inv = lax.rsqrt(jnp.mean(x * x, axis=-1, keepdims=True) + eps)
            at = slice(f * BAND, (f + 2) * BAND)
            normed_ref[band, at, :] = (x * inv * gain_ref[...]).astype(BF16)
            xb_ref[band, at, :] = x.astype(BF16)
            inv_ref[band, at, :] = jnp.broadcast_to(inv, (2 * BAND, LANES))
    same = same_pixel(rows)[None]
    owner = head_lanes(head_dim, rows)
    for band in range(bands):
        qkv_ref[band] = mm(normed_ref[band], proj_ref[...]).astype(BF16)
        att = []
        for pair in range(width // LANES):
            qp, kp, vp = (
                qkv_ref[band, :, n * width + pair * LANES:n * width + (pair + 1) * LANES] for n in range(3)
            )
            scores = mm(stack_heads(qp, owner, per_pair, scale), kp, NT)
            outs = []
            for h in range(per_pair):
                head = pair * per_pair + h
                for f in range(0, frames, CHUNK):
                    at = slice(f * BAND, (f + CHUNK) * BAND)
                    s = scores[h * rows + f * BAND:h * rows + (f + CHUNK) * BAND].reshape(CHUNK, BAND, rows)
                    s = jnp.where(same, s + rel_ref[f:f + CHUNK, head:head + 1, :], FAR)
                    s = s.reshape(CHUNK * BAND, rows)
                    e = jnp.exp(s - jnp.max(s, axis=-1, keepdims=True))
                    p_ref[band, head, at, :] = (e * (1.0 / jnp.sum(e, axis=-1, keepdims=True))).astype(BF16)
                outs.append(mm(p_ref[band, head], vp))
            att.append(pick_heads(outs, owner).astype(BF16))
        att = jnp.concatenate(att, axis=1)
        for k in range(1, tm):
            msg_refs[k - 1][band] = mm(att, wo_ref[:, pl.ds(place(tm - k), width)]).astype(BF16)
        own_ref[band] = mm(att, wo_ref[:, pl.ds(place(0), width)]) + xb_ref[band, :, pl.ds(place(0), width)].astype(F32)


def backward_kernel(dims, band, last, me_ref, *refs):
    tm, frames, pixels, width, group, head_dim, eps = dims
    g_refs = refs[:tm]
    gain_ref, qkv_ref, p_ref, xb_ref, inv_ref, proj_ref, wo_ref = refs[tm:tm + 7]
    rest = list(refs[tm + 7:])
    carried = (rest.pop(0), rest.pop(0)) if band else None
    own_ref = rest.pop(0)
    msg_refs = [rest.pop(0) for _ in range(tm - 1)]
    small_ref = rest.pop(0) if last else None
    gain_out = None if last else rest.pop(0)
    diag_ref = rest.pop() if last else rest.pop(0)
    gw_ref, ds_ref, grad_ref = rest
    me = me_ref[0]
    rows = frames * BAND
    per_pair = LANES // head_dim
    scale = head_dim ** -0.5
    chans = width * tm

    def place(k):
        return pl.multiple_of(lax.rem(me + k, tm) * width, width)

    for k in range(tm):
        gw_ref[:, pl.ds(place(k), width)] = g_refs[k][...]
    owner = head_lanes(head_dim, rows)
    d_att = mm(gw_ref[...], wo_ref[...], NT).astype(BF16)
    grads = [[], [], []]
    for pair in range(width // LANES):
        qp, kp, vp = (
            qkv_ref[band, :, n * width + pair * LANES:n * width + (pair + 1) * LANES] for n in range(3)
        )
        da = d_att[:, pair * LANES:(pair + 1) * LANES]
        d_prob = mm(stack_heads(da, owner, per_pair), vp, NT)
        parts = [[], [], []]
        for h in range(per_pair):
            head = pair * per_pair + h
            for f in range(0, frames, CHUNK):
                at = slice(f * BAND, (f + CHUNK) * BAND)
                full = p_ref[band, head, at, :].astype(F32)
                t = d_prob[h * rows + f * BAND:h * rows + (f + CHUNK) * BAND]
                score = full * (t - jnp.sum(full * t, axis=-1, keepdims=True))
                ds_ref[head, at, :] = (score * scale).astype(BF16)
                part = jnp.sum(score.reshape(CHUNK, BAND, rows), axis=1, keepdims=True)
                if carried is not None:
                    part = part + carried[1][f:f + CHUNK, head:head + 1, :]
                diag_ref[f:f + CHUNK, head:head + 1, :] = part
            probs, score = p_ref[band, head], ds_ref[head]
            parts[0].append(mm(score, kp))
            parts[1].append(mm(score, qp, TN))
            parts[2].append(mm(probs, da, TN))
        for n in range(3):
            grads[n].append(pick_heads(parts[n], owner).astype(BF16))
    grad_ref[...] = mm(jnp.concatenate(grads[0] + grads[1] + grads[2], axis=1), proj_ref[...], NT)
    gain_sum = jnp.zeros((BAND, chans), F32)
    for f in range(0, frames, 2):
        at = slice(f * BAND, (f + 2) * BAND)
        grad, x = grad_ref[at, :], xb_ref[band, at, :].astype(F32)
        inv = inv_ref[band, at, :1]
        scaled = x * inv
        gain_sum = gain_sum + jnp.sum((grad * scaled).reshape(2, BAND, chans), axis=0)
        term = grad * gain_ref[...]
        inner = jnp.mean(term * scaled, axis=-1, keepdims=True)
        grad_ref[at, :] = inv * (term - scaled * inner)
    for k in range(1, tm):
        msg_refs[k - 1][...] = grad_ref[:, pl.ds(place(tm - k), width)].astype(BF16)
    own_ref[...] = grad_ref[:, pl.ds(place(0), width)] + g_refs[0][...].astype(F32)
    gain_sum = jnp.sum(gain_sum, axis=0, keepdims=True)
    if carried is not None:
        gain_sum = gain_sum + carried[0][...]
    if not last:
        gain_out[...] = gain_sum
        return
    small_ref[...] = jnp.zeros_like(small_ref)
    for r in range(chans // LANES):
        small_ref[r:r + 1, :LANES] = gain_sum[:, r * LANES:(r + 1) * LANES]
    span = small_ref.shape[1] - LANES
    bias = jnp.zeros((group, span), F32)
    for i in range(frames):
        before = (frames - 1 - i) * BAND
        bias = bias + jnp.pad(diag_ref[i], ((0, 0), (before, span - before - rows)))
    small_ref[:group, LANES:] = bias


def finish_kernel(bands, frames, own_refs, in_refs, out_ref):
    each = len(in_refs) // bands
    parts = []
    for band in range(bands):
        value = own_refs[band][...]
        for ref in in_refs[band * each:(band + 1) * each]:
            value = value + ref[...].astype(F32)
        parts.append(value.reshape(frames, 1, BAND, value.shape[-1]))
    value = jnp.concatenate(parts, axis=1)
    out_ref[...] = value.reshape(out_ref.shape).astype(out_ref.dtype)


def finish_bands(bands, frames, *refs):
    finish_kernel(bands, frames, refs[:bands], refs[bands:-1], refs[-1])


def finish_whole(bands, frames, own_ref, *refs):
    in_refs = [ref.at[band] for band in range(bands) for ref in refs[:-1]]
    finish_kernel(bands, frames, [own_ref.at[band] for band in range(bands)], in_refs, refs[-1])


def bias_kernel(small_ref, out_ref):
    group, offsets = out_ref.shape
    value = small_ref[:group, LANES:]
    lane = lax.broadcasted_iota(jnp.int32, (value.shape[1], offsets), 0) // BAND
    put = (lane == lax.broadcasted_iota(jnp.int32, (value.shape[1], offsets), 1)).astype(F32)
    out_ref[...] = lax.dot_general(value, put, NN, precision=lax.Precision.HIGHEST, preferred_element_type=F32)


def gain_kernel(me_ref, *refs):
    *tile_refs, out_ref, sum_ref = refs
    total = tile_refs[0][...]
    for ref in tile_refs[1:]:
        total = total + ref[...]
    sum_ref[...] = total
    count = out_ref.shape[1] // LANES
    for r in range(count):
        out_ref[:, r * LANES:(r + 1) * LANES] = sum_ref[pl.ds(me_ref[0] * count + r, 1), :]


def shifted(value, axis, step):
    count = lax.axis_size(axis)
    return lax.ppermute(value, axis, [((i + step) % count, i) for i in range(count)])


def group_sum(value, axis, beside=()):
    count = lax.axis_size(axis)
    stride = 1
    while stride < count:
        left = count // stride
        radix = 4 if left % 4 == 0 else 2 if left % 2 == 0 else left
        parts = [value]
        for step in range(1, radix):
            pairs = []
            for i in range(count):
                digit = i // stride % radix
                other = digit ^ step if radix in (2, 4) else (digit + step) % radix
                pairs.append((i + (other - digit) * stride, i))
            parts.append(lax.ppermute(value, axis, pairs))
        parts, beside = lax.optimization_barrier((parts, beside))
        value = sum(parts[1:], parts[0])
        stride *= radix
    return value, beside


def per_device(inputs, out_grad, norm_gain, pos_bias, w_query, w_key, w_value, w_out):
    clips, frames, pixels, width = inputs.shape
    group = pos_bias.shape[0]
    tm = lax.axis_size("tm")
    me = lax.axis_index("tm")
    chans = width * tm
    head_dim = width // group
    total = frames * pixels
    bands = pixels // BAND
    rows = frames * BAND
    offsets = 2 * frames - 1
    span = -(-offsets * BAND // LANES) * LANES
    lines = -(-max(chans // LANES, group) // BAND) * BAND
    dims = (tm, frames, pixels, width, group, head_dim, 1e-06)
    x0 = inputs.reshape(total, width)
    g_bands = [out_grad[:, :, n * BAND:(n + 1) * BAND].reshape(rows, width) for n in range(bands)]
    x_parts = [x0] + [shifted(x0, "tm", k) for k in range(1, tm)]
    g_parts = [[g] + [shifted(g, "tm", k) for k in range(1, tm)] for g in g_bands]
    me1 = me.astype(jnp.int32).reshape(1)
    gain = norm_gain.reshape(1, chans)
    spread = jnp.broadcast_to(pos_bias[:, :, None], (*pos_bias.shape, BAND)).reshape(group, -1)
    smem, vmem = pl.BlockSpec(memory_space=pltpu.SMEM), pl.BlockSpec(memory_space=pltpu.VMEM)
    params = pltpu.CompilerParams(vmem_limit_bytes=VMEM_LIMIT)
    held = [x0, w_query, w_key, w_value, w_out, gain]
    held = [pltpu.with_memory_space_constraint(h, pltpu.HBM) for h in held]
    rel, x0, proj, w_out, gain = pl.pallas_call(
        functools.partial(stage_kernel, frames, width),
        in_specs=[vmem] + [pl.BlockSpec(memory_space=pltpu.HBM)] * len(held),
        out_specs=[vmem] * 5,
        out_shape=[
            jax.ShapeDtypeStruct((frames, group, rows), F32),
            jax.ShapeDtypeStruct((total, width), BF16),
            jax.ShapeDtypeStruct((chans, 3 * width), BF16),
            jax.ShapeDtypeStruct((width, chans), BF16),
            jax.ShapeDtypeStruct((1, chans), F32),
        ],
        scratch_shapes=[pltpu.SemaphoreType.DMA((len(held),))],
        compiler_params=params,
        cost_estimate=pl.CostEstimate(flops=0, bytes_accessed=8_000_000, transcendentals=0),
        name="stage",
    )(spread, *held)
    x_parts[0] = x0
    qkv, probs, xb, inv, mix_own, *mix_out = pl.pallas_call(
        functools.partial(forward_kernel, dims),
        in_specs=[smem] + [vmem] * (tm + 4),
        out_specs=[vmem] * (5 + tm - 1),
        out_shape=[
            jax.ShapeDtypeStruct((bands, rows, 3 * width), BF16),
            jax.ShapeDtypeStruct((bands, group, rows, rows), BF16),
            jax.ShapeDtypeStruct((bands, rows, chans), BF16),
            jax.ShapeDtypeStruct((bands, rows, LANES), F32),
            jax.ShapeDtypeStruct((bands, rows, width), F32),
        ] + [jax.ShapeDtypeStruct((bands, rows, width), BF16)] * (tm - 1),
        scratch_shapes=[pltpu.VMEM((total, chans), BF16), pltpu.VMEM((bands, rows, chans), BF16)],
        compiler_params=params,
        cost_estimate=pl.CostEstimate(flops=4_000_000_000, bytes_accessed=8_000_000, transcendentals=0),
        name="attend",
    )(me1, *x_parts, gain, rel, proj, w_out)
    mix_in = [shifted(mix_out[k - 1], "tm", k) for k in range(1, tm)]

    owns, ins, carry = [], [], []
    diag = (frames, group, rows)
    for band in range(bands):
        last = band == bands - 1
        scratch = [pltpu.VMEM((rows, chans), BF16), pltpu.VMEM((group, rows, rows), BF16), pltpu.VMEM((rows, chans), F32)]
        if last:
            extra = [jax.ShapeDtypeStruct((lines, LANES + span), F32)]
            scratch.append(pltpu.VMEM(diag, F32))
        else:
            extra = [jax.ShapeDtypeStruct((1, chans), F32), jax.ShapeDtypeStruct(diag, F32)]
        own, *rest = pl.pallas_call(
            functools.partial(backward_kernel, dims, band, last),
            in_specs=[smem] + [vmem] * (tm + 7 + len(carry)),
            out_specs=[vmem] * (tm + len(extra)),
            out_shape=[jax.ShapeDtypeStruct((rows, width), F32)]
            + [jax.ShapeDtypeStruct((rows, width), BF16)] * (tm - 1) + extra,
            scratch_shapes=scratch,
            compiler_params=params,
            cost_estimate=pl.CostEstimate(flops=2_500_000_000, bytes_accessed=0, transcendentals=0),
            name="attend_back",
        )(me1, *g_parts[band], gain, qkv, probs, xb, inv, proj, w_out, *carry)
        sent, carry = rest[:tm - 1], rest[tm - 1:]
        owns.append(own)
        ins += [shifted(sent[k - 1], "tm", k) for k in range(1, tm)]

    small, mix_in = lax.optimization_barrier((carry[0], mix_in))
    small, ins[:-1] = group_sum(small, "dp", ins[:-1])
    small, ins[-1:] = group_sum(small, "space", ins[-1:])
    bias_grad = pl.pallas_call(
        bias_kernel,
        in_specs=[vmem],
        out_specs=vmem,
        out_shape=jax.ShapeDtypeStruct((group, offsets), F32),
        name="bias_sum",
    )(small)
    tile = small[:chans // LANES, :LANES]
    tiles = [tile] + [shifted(tile, "tm", k) for k in range(1, tm)]
    gain_grad = pl.pallas_call(
        gain_kernel,
        in_specs=[smem] + [vmem] * tm,
        out_specs=vmem,
        out_shape=jax.ShapeDtypeStruct((1, width), F32),
        scratch_shapes=[pltpu.VMEM(tile.shape, F32)],
        name="gain_sum",
    )(me1, *tiles)
    result = jax.ShapeDtypeStruct((total, width), BF16)
    block_out = pl.pallas_call(
        functools.partial(finish_whole, bands, frames),
        in_specs=[vmem] * tm,
        out_specs=vmem,
        out_shape=result,
        compiler_params=params,
        cost_estimate=pl.CostEstimate(flops=0, bytes_accessed=1_500_000, transcendentals=0),
        name="finish_out",
    )(mix_own, *mix_in)
    input_grad = pl.pallas_call(
        functools.partial(finish_bands, bands, frames),
        in_specs=[vmem] * (bands * tm),
        out_specs=vmem,
        out_shape=result,
        compiler_params=params,
        cost_estimate=pl.CostEstimate(flops=0, bytes_accessed=1_500_000, transcendentals=0),
        name="finish_grad",
    )(*owns, *ins)
    return (block_out.reshape(inputs.shape), input_grad.reshape(inputs.shape), gain_grad.reshape(width), bias_grad)


def solution(mesh):
    return jax.shard_map(
        per_device,
        mesh=mesh,
        in_specs=(
            P("dp", None, "space", "tm"),
            P("dp", None, "space", "tm"),
            P(),
            P("tm", None),
            P(None, "tm"),
            P(None, "tm"),
            P(None, "tm"),
            P("tm", None),
        ),
        out_specs=(
            P("dp", None, "space", "tm"),
            P("dp", None, "space", "tm"),
            P("tm"),
            P("tm", None),
        ),
        check_vma=False,
    )
```

```python
import functools

import jax
import jax.numpy as jnp
from jax import lax
from jax.experimental import pallas as pl
from jax.experimental.pallas import tpu as pltpu
from jax.sharding import PartitionSpec as P

CHUNK = 4
BAND = 8
LANES = 128
FAR = -1e30
F32, BF16 = jnp.float32, jnp.bfloat16
NT = (((1,), (1,)), ((), ()))
NN = (((1,), (0,)), ((), ()))
TN = (((0,), (0,)), ((), ()))
VMEM_LIMIT = 24 * 1024 * 1024


def mm(a, b, dims=NN):
    return lax.dot_general(a, b, dims, preferred_element_type=F32)


def same_pixel(rows):
    row = lax.broadcasted_iota(jnp.int32, (BAND, rows), 0)
    lane = lax.broadcasted_iota(jnp.int32, (BAND, rows), 1)
    return (lane & (BAND - 1)) == row


def head_lanes(head_dim, rows):
    return lax.broadcasted_iota(jnp.int32, (rows, LANES), 1) // head_dim


def stack_heads(pair, owner, per_pair, factor=None):
    pair = pair if factor is None else pair * jnp.asarray(factor, pair.dtype)
    return jnp.concatenate([jnp.where(owner == h, pair, jnp.zeros_like(pair)) for h in range(per_pair)], 0)


def pick_heads(parts, owner):
    out = parts[0]
    for h in range(1, len(parts)):
        out = jnp.where(owner == h, parts[h], out)
    return out


def stage_kernel(frames, width, bias_ref, x_ref, wq_ref, wk_ref, wv_ref, wo_ref, gain_ref,
                 rel_ref, x_out, proj_out, wo_out, gain_out, sems):
    pairs = [(x_ref, x_out), (wo_ref, wo_out), (gain_ref, gain_out)]
    pairs += [(w, proj_out.at[:, n * width:(n + 1) * width]) for n, w in enumerate((wq_ref, wk_ref, wv_ref))]
    copies = [pltpu.make_async_copy(source, target, sems.at[n]) for n, (source, target) in enumerate(pairs)]
    for copy in copies:
        copy.start()
    rows = rel_ref.shape[2]
    for i in range(frames):
        start = (frames - 1 - i) * BAND
        rel_ref[i] = bias_ref[:, start:start + rows]
    for copy in copies:
        copy.wait()


def forward_kernel(dims, me_ref, *refs):
    tm, frames, pixels, width, group, head_dim, eps = dims
    x_refs = refs[:tm]
    gain_ref, rel_ref, proj_ref, wo_ref = refs[tm:tm + 4]
    qkv_ref, p_ref, xb_ref, inv_ref, own_ref = refs[tm + 4:tm + 9]
    msg_refs = refs[tm + 9:tm + 9 + tm - 1]
    xw_ref, normed_ref, att_ref = refs[tm + 9 + tm - 1:]
    me = me_ref[0]
    rows = frames * BAND
    bands = pixels // BAND
    per_pair = LANES // head_dim
    scale = head_dim ** -0.5

    def place(k):
        return pl.multiple_of(lax.rem(me + k, tm) * width, width)

    for k in range(tm):
        xw_ref[:, pl.ds(place(k), width)] = x_refs[k][...]
    for f in range(0, frames, 2):
        both = xw_ref[f * pixels:(f + 2) * pixels, :].astype(F32).reshape(2, bands, BAND, -1)
        for band in range(bands):
            x = both[:, band].reshape(2 * BAND, -1)
            inv = lax.rsqrt(jnp.mean(x * x, axis=-1, keepdims=True) + eps)
            at = slice(f * BAND, (f + 2) * BAND)
            normed_ref[band, at, :] = (x * inv * gain_ref[...]).astype(BF16)
            xb_ref[band, at, :] = x.astype(BF16)
            inv_ref[band, at, :] = jnp.broadcast_to(inv, (2 * BAND, LANES))
    same = same_pixel(rows)[None]
    owner = head_lanes(head_dim, rows)
    total = frames * pixels
    qkv = mm(normed_ref[...].reshape(total, -1), proj_ref[...]).astype(BF16)
    qkv_ref[...] = qkv.reshape(bands, rows, 3 * width)
    for band in range(bands):
        for pair in range(width // LANES):
            qp, kp, vp = (
                qkv_ref[band, :, n * width + pair * LANES:n * width + (pair + 1) * LANES] for n in range(3)
            )
            scores = mm(stack_heads(qp, owner, per_pair, scale), kp, NT)
            outs = []
            for h in range(per_pair):
                head = pair * per_pair + h
                for f in range(0, frames, CHUNK):
                    at = slice(f * BAND, (f + CHUNK) * BAND)
                    s = scores[h * rows + f * BAND:h * rows + (f + CHUNK) * BAND].reshape(CHUNK, BAND, rows)
                    s = jnp.where(same, s + rel_ref[f:f + CHUNK, head:head + 1, :], FAR)
                    s = s.reshape(CHUNK * BAND, rows)
                    e = jnp.exp(s - jnp.max(s, axis=-1, keepdims=True))
                    p_ref[band, head, at, :] = (e * (1.0 / jnp.sum(e, axis=-1, keepdims=True))).astype(BF16)
                outs.append(mm(p_ref[band, head], vp))
            att_ref[band, :, pair * LANES:(pair + 1) * LANES] = pick_heads(outs, owner).astype(BF16)
    att = att_ref[...].reshape(total, width)
    for k in range(1, tm):
        part = mm(att, wo_ref[:, pl.ds(place(tm - k), width)]).astype(BF16)
        msg_refs[k - 1][...] = part.reshape(bands, rows, width)
    own = mm(att, wo_ref[:, pl.ds(place(0), width)]).reshape(bands, rows, width)
    own_ref[...] = own + xb_ref[:, :, pl.ds(place(0), width)].astype(F32)


def backward_kernel(dims, band, last, me_ref, *refs):
    tm, frames, pixels, width, group, head_dim, eps = dims
    g_refs = refs[:tm]
    gain_ref, qkv_ref, p_ref, xb_ref, inv_ref, proj_ref, wo_ref = refs[tm:tm + 7]
    rest = list(refs[tm + 7:])
    carried = (rest.pop(0), rest.pop(0)) if band else None
    own_ref = rest.pop(0)
    msg_refs = [rest.pop(0) for _ in range(tm - 1)]
    small_ref = rest.pop(0) if last else None
    gain_out = None if last else rest.pop(0)
    diag_ref = rest.pop() if last else rest.pop(0)
    gw_ref, ds_ref, grad_ref = rest
    me = me_ref[0]
    rows = frames * BAND
    per_pair = LANES // head_dim
    scale = head_dim ** -0.5
    chans = width * tm

    def place(k):
        return pl.multiple_of(lax.rem(me + k, tm) * width, width)

    for k in range(tm):
        gw_ref[:, pl.ds(place(k), width)] = g_refs[k][...]
    owner = head_lanes(head_dim, rows)
    d_att = mm(gw_ref[...], wo_ref[...], NT).astype(BF16)
    grads = [[], [], []]
    for pair in range(width // LANES):
        qp, kp, vp = (
            qkv_ref[band, :, n * width + pair * LANES:n * width + (pair + 1) * LANES] for n in range(3)
        )
        da = d_att[:, pair * LANES:(pair + 1) * LANES]
        d_prob = mm(stack_heads(da, owner, per_pair), vp, NT)
        parts = [[], [], []]
        for h in range(per_pair):
            head = pair * per_pair + h
            for f in range(0, frames, CHUNK):
                at = slice(f * BAND, (f + CHUNK) * BAND)
                full = p_ref[band, head, at, :].astype(F32)
                t = d_prob[h * rows + f * BAND:h * rows + (f + CHUNK) * BAND]
                score = full * (t - jnp.sum(full * t, axis=-1, keepdims=True))
                ds_ref[head, at, :] = (score * scale).astype(BF16)
                part = jnp.sum(score.reshape(CHUNK, BAND, rows), axis=1, keepdims=True)
                if carried is not None:
                    part = part + carried[1][f:f + CHUNK, head:head + 1, :]
                diag_ref[f:f + CHUNK, head:head + 1, :] = part
            probs, score = p_ref[band, head], ds_ref[head]
            parts[0].append(mm(score, kp))
            parts[1].append(mm(score, qp, TN))
            parts[2].append(mm(probs, da, TN))
        for n in range(3):
            grads[n].append(pick_heads(parts[n], owner).astype(BF16))
    grad_ref[...] = mm(jnp.concatenate(grads[0] + grads[1] + grads[2], axis=1), proj_ref[...], NT)
    gain_sum = jnp.zeros((BAND, chans), F32)
    for f in range(0, frames, 2):
        at = slice(f * BAND, (f + 2) * BAND)
        grad, x = grad_ref[at, :], xb_ref[band, at, :].astype(F32)
        inv = inv_ref[band, at, :1]
        scaled = x * inv
        gain_sum = gain_sum + jnp.sum((grad * scaled).reshape(2, BAND, chans), axis=0)
        term = grad * gain_ref[...]
        inner = jnp.mean(term * scaled, axis=-1, keepdims=True)
        grad_ref[at, :] = inv * (term - scaled * inner)
    for k in range(1, tm):
        msg_refs[k - 1][...] = grad_ref[:, pl.ds(place(tm - k), width)].astype(BF16)
    own_ref[...] = grad_ref[:, pl.ds(place(0), width)] + g_refs[0][...].astype(F32)
    gain_sum = jnp.sum(gain_sum, axis=0, keepdims=True)
    if carried is not None:
        gain_sum = gain_sum + carried[0][...]
    if not last:
        gain_out[...] = gain_sum
        return
    small_ref[...] = jnp.zeros_like(small_ref)
    for r in range(chans // LANES):
        small_ref[r:r + 1, :LANES] = gain_sum[:, r * LANES:(r + 1) * LANES]
    span = small_ref.shape[1] - LANES
    bias = jnp.zeros((group, span), F32)
    for i in range(frames):
        before = (frames - 1 - i) * BAND
        bias = bias + jnp.pad(diag_ref[i], ((0, 0), (before, span - before - rows)))
    small_ref[:group, LANES:] = bias


def finish_kernel(bands, frames, own_refs, in_refs, out_ref):
    each = len(in_refs) // bands
    parts = []
    for band in range(bands):
        value = own_refs[band][...]
        for ref in in_refs[band * each:(band + 1) * each]:
            value = value + ref[...].astype(F32)
        parts.append(value.reshape(frames, 1, BAND, value.shape[-1]))
    value = jnp.concatenate(parts, axis=1)
    out_ref[...] = value.reshape(out_ref.shape).astype(out_ref.dtype)


def finish_grad_kernel(bands, frames, small_ref, *refs):
    *refs, out_ref, bias_ref = refs
    finish_kernel(bands, frames, refs[:bands], refs[bands:], out_ref)
    group, offsets = bias_ref.shape
    value = small_ref[:, LANES:]
    high = value.astype(BF16)
    rest = value - high.astype(F32)
    middle = rest.astype(BF16)
    low = (rest - middle.astype(F32)).astype(BF16)
    span = value.shape[1]
    lane = lax.broadcasted_iota(jnp.int32, (span, LANES), 0) // BAND
    put = (lane == lax.broadcasted_iota(jnp.int32, (span, LANES), 1)).astype(F32).astype(BF16)
    total = mm(high, put) + mm(middle, put) + mm(low, put)
    bias_ref[...] = total[:group, :offsets]


def finish_out_kernel(bands, frames, own_ref, *refs):
    in_refs = [ref.at[band] for band in range(bands) for ref in refs[:-1]]
    finish_kernel(bands, frames, [own_ref.at[band] for band in range(bands)], in_refs, refs[-1])


def gain_kernel(me_ref, *refs):
    *tile_refs, out_ref, sum_ref = refs
    total = tile_refs[0][...]
    for ref in tile_refs[1:]:
        total = total + ref[...]
    sum_ref[...] = total
    count = out_ref.shape[1] // LANES
    for r in range(count):
        out_ref[:, r * LANES:(r + 1) * LANES] = sum_ref[pl.ds(me_ref[0] * count + r, 1), :]


def shifted(value, axis, step):
    count = lax.axis_size(axis)
    return lax.ppermute(value, axis, [((i + step) % count, i) for i in range(count)])


def group_sum(value, axis, beside=()):
    count = lax.axis_size(axis)
    stride = 1
    while stride < count:
        left = count // stride
        radix = 4 if left % 4 == 0 else 2 if left % 2 == 0 else left
        parts = [value]
        for step in range(1, radix):
            pairs = []
            for i in range(count):
                digit = i // stride % radix
                other = digit ^ step if radix in (2, 4) else (digit + step) % radix
                pairs.append((i + (other - digit) * stride, i))
            parts.append(lax.ppermute(value, axis, pairs))
        parts, beside = lax.optimization_barrier((parts, beside))
        value = sum(parts[1:], parts[0])
        stride *= radix
    return value, beside


def per_device(inputs, out_grad, norm_gain, pos_bias, w_query, w_key, w_value, w_out):
    clips, frames, pixels, width = inputs.shape
    group = pos_bias.shape[0]
    tm = lax.axis_size("tm")
    me = lax.axis_index("tm")
    chans = width * tm
    head_dim = width // group
    total = frames * pixels
    bands = pixels // BAND
    rows = frames * BAND
    offsets = 2 * frames - 1
    span = -(-offsets * BAND // LANES) * LANES
    lines = -(-max(chans // LANES, group) // BAND) * BAND
    dims = (tm, frames, pixels, width, group, head_dim, 1e-06)
    x0 = inputs.reshape(total, width)
    g_bands = [out_grad[:, :, n * BAND:(n + 1) * BAND].reshape(rows, width) for n in range(bands)]
    x_parts = [x0] + [shifted(x0, "tm", k) for k in range(1, tm)]
    me1 = me.astype(jnp.int32).reshape(1)
    gain = norm_gain.reshape(1, chans)
    spread = jnp.broadcast_to(pos_bias[:, :, None], (*pos_bias.shape, BAND)).reshape(group, -1)
    smem, vmem = pl.BlockSpec(memory_space=pltpu.SMEM), pl.BlockSpec(memory_space=pltpu.VMEM)
    params = pltpu.CompilerParams(vmem_limit_bytes=VMEM_LIMIT)
    held = [x0, w_query, w_key, w_value, w_out, gain]
    held = [pltpu.with_memory_space_constraint(h, pltpu.HBM) for h in held]
    rel, x0, proj, w_out, gain = pl.pallas_call(
        functools.partial(stage_kernel, frames, width),
        in_specs=[vmem] + [pl.BlockSpec(memory_space=pltpu.HBM)] * len(held),
        out_specs=[vmem] * 5,
        out_shape=[
            jax.ShapeDtypeStruct((frames, group, rows), F32),
            jax.ShapeDtypeStruct((total, width), BF16),
            jax.ShapeDtypeStruct((chans, 3 * width), BF16),
            jax.ShapeDtypeStruct((width, chans), BF16),
            jax.ShapeDtypeStruct((1, chans), F32),
        ],
        scratch_shapes=[pltpu.SemaphoreType.DMA((len(held),))],
        compiler_params=params,
        cost_estimate=pl.CostEstimate(flops=0, bytes_accessed=8_000_000, transcendentals=0),
        name="stage",
    )(spread, *held)
    x_parts[0] = x0
    g_bands, rel = lax.optimization_barrier((g_bands, rel))
    g_parts = [[g] + [shifted(g, "tm", k) for k in range(1, tm)] for g in g_bands]
    qkv, probs, xb, inv, mix_own, *mix_out = pl.pallas_call(
        functools.partial(forward_kernel, dims),
        in_specs=[smem] + [vmem] * (tm + 4),
        out_specs=[vmem] * (5 + tm - 1),
        out_shape=[
            jax.ShapeDtypeStruct((bands, rows, 3 * width), BF16),
            jax.ShapeDtypeStruct((bands, group, rows, rows), BF16),
            jax.ShapeDtypeStruct((bands, rows, chans), BF16),
            jax.ShapeDtypeStruct((bands, rows, LANES), F32),
            jax.ShapeDtypeStruct((bands, rows, width), F32),
        ] + [jax.ShapeDtypeStruct((bands, rows, width), BF16)] * (tm - 1),
        scratch_shapes=[
            pltpu.VMEM((total, chans), BF16),
            pltpu.VMEM((bands, rows, chans), BF16),
            pltpu.VMEM((bands, rows, width), BF16),
        ],
        compiler_params=params,
        cost_estimate=pl.CostEstimate(flops=4_000_000_000, bytes_accessed=8_000_000, transcendentals=0),
        name="attend",
    )(me1, *x_parts, gain, rel, proj, w_out)
    owns, ins, carry = [], [], []
    diag = (frames, group, rows)
    for band in range(bands):
        last = band == bands - 1
        scratch = [pltpu.VMEM((rows, chans), BF16), pltpu.VMEM((group, rows, rows), BF16), pltpu.VMEM((rows, chans), F32)]
        if last:
            extra = [jax.ShapeDtypeStruct((lines, LANES + span), F32)]
            scratch.append(pltpu.VMEM(diag, F32))
        else:
            extra = [jax.ShapeDtypeStruct((1, chans), F32), jax.ShapeDtypeStruct(diag, F32)]
        own, *rest = pl.pallas_call(
            functools.partial(backward_kernel, dims, band, last),
            in_specs=[smem] + [vmem] * (tm + 7 + len(carry)),
            out_specs=[vmem] * (tm + len(extra)),
            out_shape=[jax.ShapeDtypeStruct((rows, width), F32)]
            + [jax.ShapeDtypeStruct((rows, width), BF16)] * (tm - 1) + extra,
            scratch_shapes=scratch,
            compiler_params=params,
            cost_estimate=pl.CostEstimate(flops=4_000_000_000, bytes_accessed=0, transcendentals=0),
            name="attend_back",
        )(me1, *g_parts[band], gain, qkv, probs, xb, inv, proj, w_out, *carry)
        sent, carry = rest[:tm - 1], rest[tm - 1:]
        if band == 0:
            sent, mix_out = lax.optimization_barrier((sent, mix_out))
            mix_in = [shifted(mix_out[k - 1], "tm", k) for k in range(1, tm)]
        owns.append(own)
        ins += [shifted(sent[k - 1], "tm", k) for k in range(1, tm)]

    result = jax.ShapeDtypeStruct((total, width), BF16)
    finish_cost = pl.CostEstimate(flops=0, bytes_accessed=1_500_000, transcendentals=0)
    block_out = pl.pallas_call(
        functools.partial(finish_out_kernel, bands, frames),
        in_specs=[vmem] * tm,
        out_specs=vmem,
        out_shape=result,
        compiler_params=params,
        cost_estimate=finish_cost,
        name="finish_out",
    )(mix_own, *mix_in)
    small, ins[:-1] = group_sum(carry[0], "dp", ins[:-1])
    small, (block_out, ins[-1]) = group_sum(small, "space", (block_out, ins[-1]))
    tile = small[:chans // LANES, :LANES]
    tiles = [shifted(tile, "tm", k) for k in range(1, tm)]
    input_grad, bias_grad = pl.pallas_call(
        functools.partial(finish_grad_kernel, bands, frames),
        in_specs=[vmem] * (1 + bands * tm),
        out_specs=[vmem] * 2,
        out_shape=[result, jax.ShapeDtypeStruct((group, offsets), F32)],
        compiler_params=params,
        cost_estimate=finish_cost,
        name="finish_grad",
    )(small, *owns, *ins)
    tiles, input_grad = lax.optimization_barrier((tiles, input_grad))
    gain_grad = pl.pallas_call(
        gain_kernel,
        in_specs=[smem] + [vmem] * tm,
        out_specs=vmem,
        out_shape=jax.ShapeDtypeStruct((1, width), F32),
        scratch_shapes=[pltpu.VMEM(tile.shape, F32)],
        compiler_params=params,
        name="gain_sum",
    )(me1, tile, *tiles)
    return (block_out.reshape(inputs.shape), input_grad.reshape(inputs.shape), gain_grad.reshape(width), bias_grad)


def solution(mesh):
    return jax.shard_map(
        per_device,
        mesh=mesh,
        in_specs=(
            P("dp", None, "space", "tm"),
            P("dp", None, "space", "tm"),
            P(),
            P("tm", None),
            P(None, "tm"),
            P(None, "tm"),
            P(None, "tm"),
            P("tm", None),
        ),
        out_specs=(
            P("dp", None, "space", "tm"),
            P("dp", None, "space", "tm"),
            P("tm"),
            P("tm", None),
        ),
        check_vma=False,
    )
```

```python
import functools

import jax
import jax.numpy as jnp
from jax import lax
from jax.experimental import pallas as pl
from jax.experimental.pallas import tpu as pltpu
from jax.sharding import PartitionSpec as P

CHUNK = 4
BAND = 8
LANES = 128
FAR = -1e30
F32, BF16 = jnp.float32, jnp.bfloat16
NT = (((1,), (1,)), ((), ()))
NN = (((1,), (0,)), ((), ()))
TN = (((0,), (0,)), ((), ()))
VMEM_LIMIT = 24 * 1024 * 1024


def mm(a, b, dims=NN):
    return lax.dot_general(a, b, dims, preferred_element_type=F32)


def same_pixel(rows):
    row = lax.broadcasted_iota(jnp.int32, (BAND, rows), 0)
    lane = lax.broadcasted_iota(jnp.int32, (BAND, rows), 1)
    return (lane & (BAND - 1)) == row


def head_lanes(head_dim, rows):
    return lax.broadcasted_iota(jnp.int32, (rows, LANES), 1) // head_dim


def stack_heads(pair, owner, per_pair, factor=None):
    pair = pair if factor is None else pair * jnp.asarray(factor, pair.dtype)
    return jnp.concatenate([jnp.where(owner == h, pair, jnp.zeros_like(pair)) for h in range(per_pair)], 0)


def pick_heads(parts, owner):
    out = parts[0]
    for h in range(1, len(parts)):
        out = jnp.where(owner == h, parts[h], out)
    return out


def stage_kernel(frames, width, bias_ref, x_ref, wq_ref, wk_ref, wv_ref, wo_ref, gain_ref,
                 rel_ref, x_out, proj_out, wo_out, gain_out, sems):
    pairs = [(x_ref, x_out), (wo_ref, wo_out), (gain_ref, gain_out)]
    pairs += [(w, proj_out.at[:, n * width:(n + 1) * width]) for n, w in enumerate((wq_ref, wk_ref, wv_ref))]
    copies = [pltpu.make_async_copy(source, target, sems.at[n]) for n, (source, target) in enumerate(pairs)]
    for copy in copies:
        copy.start()
    rows = rel_ref.shape[2]
    for i in range(frames):
        start = (frames - 1 - i) * BAND
        rel_ref[i] = bias_ref[:, start:start + rows]
    for copy in copies:
        copy.wait()


def forward_kernel(dims, me_ref, *refs):
    tm, frames, pixels, width, group, head_dim, eps = dims
    x_refs = refs[:tm]
    gain_ref, rel_ref, proj_ref, wo_ref = refs[tm:tm + 4]
    qkv_ref, p_ref, xb_ref, inv_ref, own_ref = refs[tm + 4:tm + 9]
    msg_refs = refs[tm + 9:tm + 9 + tm - 1]
    xw_ref, normed_ref, att_ref = refs[tm + 9 + tm - 1:]
    me = me_ref[0]
    rows = frames * BAND
    bands = pixels // BAND
    per_pair = LANES // head_dim
    scale = head_dim ** -0.5

    def place(k):
        return pl.multiple_of(lax.rem(me + k, tm) * width, width)

    for k in range(tm):
        xw_ref[:, pl.ds(place(k), width)] = x_refs[k][...]
    for f in range(0, frames, 2):
        both = xw_ref[f * pixels:(f + 2) * pixels, :].astype(F32).reshape(2, bands, BAND, -1)
        for band in range(bands):
            x = both[:, band].reshape(2 * BAND, -1)
            inv = lax.rsqrt(jnp.mean(x * x, axis=-1, keepdims=True) + eps)
            at = slice(f * BAND, (f + 2) * BAND)
            normed_ref[band, at, :] = (x * inv * gain_ref[...]).astype(BF16)
            xb_ref[band, at, :] = x.astype(BF16)
            inv_ref[band, at, :] = jnp.broadcast_to(inv, (2 * BAND, LANES))
    same = same_pixel(rows)[None]
    owner = head_lanes(head_dim, rows)
    total = frames * pixels
    qkv = mm(normed_ref[...].reshape(total, -1), proj_ref[...]).astype(BF16)
    qkv_ref[...] = qkv.reshape(bands, rows, 3 * width)
    for band in range(bands):
        for pair in range(width // LANES):
            qp, kp, vp = (
                qkv_ref[band, :, n * width + pair * LANES:n * width + (pair + 1) * LANES] for n in range(3)
            )
            scores = mm(stack_heads(qp, owner, per_pair, scale), kp, NT)
            outs = []
            for h in range(per_pair):
                head = pair * per_pair + h
                for f in range(0, frames, CHUNK):
                    at = slice(f * BAND, (f + CHUNK) * BAND)
                    s = scores[h * rows + f * BAND:h * rows + (f + CHUNK) * BAND].reshape(CHUNK, BAND, rows)
                    s = jnp.where(same, s + rel_ref[f:f + CHUNK, head:head + 1, :], FAR)
                    s = s.reshape(CHUNK * BAND, rows)
                    e = jnp.exp(s - jnp.max(s, axis=-1, keepdims=True))
                    p_ref[band, head, at, :] = (e * (1.0 / jnp.sum(e, axis=-1, keepdims=True))).astype(BF16)
                outs.append(mm(p_ref[band, head], vp))
            att_ref[band, :, pair * LANES:(pair + 1) * LANES] = pick_heads(outs, owner).astype(BF16)
    att = att_ref[...].reshape(total, width)
    for k in range(1, tm):
        part = mm(att, wo_ref[:, pl.ds(place(tm - k), width)]).astype(BF16)
        msg_refs[k - 1][...] = part.reshape(bands, rows, width)
    own = mm(att, wo_ref[:, pl.ds(place(0), width)]).reshape(bands, rows, width)
    own_ref[...] = own + xb_ref[:, :, pl.ds(place(0), width)].astype(F32)


def backward_kernel(dims, band, last, me_ref, *refs):
    tm, frames, pixels, width, group, head_dim, eps = dims
    g_refs = refs[:tm]
    gain_ref, qkv_ref, p_ref, xb_ref, inv_ref, proj_ref, wo_ref = refs[tm:tm + 7]
    rest = list(refs[tm + 7:])
    carried = (rest.pop(0), rest.pop(0)) if band else None
    own_ref = rest.pop(0)
    msg_refs = [rest.pop(0) for _ in range(tm - 1)]
    small_ref = rest.pop(0) if last else None
    gain_out = None if last else rest.pop(0)
    diag_ref = rest.pop() if last else rest.pop(0)
    gw_ref, ds_ref, grad_ref = rest
    me = me_ref[0]
    rows = frames * BAND
    per_pair = LANES // head_dim
    scale = head_dim ** -0.5
    chans = width * tm

    def place(k):
        return pl.multiple_of(lax.rem(me + k, tm) * width, width)

    for k in range(tm):
        gw_ref[:, pl.ds(place(k), width)] = g_refs[k][...]
    owner = head_lanes(head_dim, rows)
    d_att = mm(gw_ref[...], wo_ref[...], NT).astype(BF16)
    grads = [[], [], []]
    for pair in range(width // LANES):
        qp, kp, vp = (
            qkv_ref[band, :, n * width + pair * LANES:n * width + (pair + 1) * LANES] for n in range(3)
        )
        da = d_att[:, pair * LANES:(pair + 1) * LANES]
        d_prob = mm(stack_heads(da, owner, per_pair), vp, NT)
        parts = [[], [], []]
        for h in range(per_pair):
            head = pair * per_pair + h
            for f in range(0, frames, CHUNK):
                at = slice(f * BAND, (f + CHUNK) * BAND)
                full = p_ref[band, head, at, :].astype(F32)
                t = d_prob[h * rows + f * BAND:h * rows + (f + CHUNK) * BAND]
                score = full * (t - jnp.sum(full * t, axis=-1, keepdims=True))
                ds_ref[head, at, :] = (score * scale).astype(BF16)
                part = jnp.sum(score.reshape(CHUNK, BAND, rows), axis=1, keepdims=True)
                if carried is not None:
                    part = part + carried[1][f:f + CHUNK, head:head + 1, :]
                diag_ref[f:f + CHUNK, head:head + 1, :] = part
            probs, score = p_ref[band, head], ds_ref[head]
            parts[0].append(mm(score, kp))
            parts[1].append(mm(score, qp, TN))
            parts[2].append(mm(probs, da, TN))
        for n in range(3):
            grads[n].append(pick_heads(parts[n], owner).astype(BF16))
    grad_ref[...] = mm(jnp.concatenate(grads[0] + grads[1] + grads[2], axis=1), proj_ref[...], NT)
    gain_sum = jnp.zeros((BAND, chans), F32)
    for f in range(0, frames, 2):
        at = slice(f * BAND, (f + 2) * BAND)
        grad, x = grad_ref[at, :], xb_ref[band, at, :].astype(F32)
        inv = inv_ref[band, at, :1]
        scaled = x * inv
        gain_sum = gain_sum + jnp.sum((grad * scaled).reshape(2, BAND, chans), axis=0)
        term = grad * gain_ref[...]
        inner = jnp.mean(term * scaled, axis=-1, keepdims=True)
        grad_ref[at, :] = inv * (term - scaled * inner)
    for k in range(1, tm):
        msg_refs[k - 1][...] = grad_ref[:, pl.ds(place(tm - k), width)].astype(BF16)
    own_ref[...] = grad_ref[:, pl.ds(place(0), width)] + g_refs[0][...].astype(F32)
    gain_sum = jnp.sum(gain_sum, axis=0, keepdims=True)
    if carried is not None:
        gain_sum = gain_sum + carried[0][...]
    if not last:
        gain_out[...] = gain_sum
        return
    small_ref[...] = jnp.zeros_like(small_ref)
    for r in range(chans // LANES):
        small_ref[r:r + 1, :LANES] = gain_sum[:, r * LANES:(r + 1) * LANES]
    span = small_ref.shape[1] - LANES
    bias = jnp.zeros((group, span), F32)
    for i in range(frames):
        before = (frames - 1 - i) * BAND
        bias = bias + jnp.pad(diag_ref[i], ((0, 0), (before, span - before - rows)))
    small_ref[:group, LANES:] = bias


def finish_kernel(bands, frames, own_refs, in_refs, out_ref):
    each = len(in_refs) // bands
    parts = []
    for band in range(bands):
        value = own_refs[band][...]
        for ref in in_refs[band * each:(band + 1) * each]:
            value = value + ref[...].astype(F32)
        parts.append(value.reshape(frames, 1, BAND, value.shape[-1]))
    value = jnp.concatenate(parts, axis=1)
    out_ref[...] = value.reshape(out_ref.shape).astype(out_ref.dtype)


def finish_grad_kernel(bands, frames, small_ref, *refs):
    *refs, out_ref, bias_ref = refs
    finish_kernel(bands, frames, refs[:bands], refs[bands:], out_ref)
    group, offsets = bias_ref.shape
    value = small_ref[:, LANES:]
    high = value.astype(BF16)
    rest = value - high.astype(F32)
    middle = rest.astype(BF16)
    low = (rest - middle.astype(F32)).astype(BF16)
    span = value.shape[1]
    lane = lax.broadcasted_iota(jnp.int32, (span, LANES), 0) // BAND
    put = (lane == lax.broadcasted_iota(jnp.int32, (span, LANES), 1)).astype(F32).astype(BF16)
    total = mm(high, put) + mm(middle, put) + mm(low, put)
    bias_ref[...] = total[:group, :offsets]


def finish_out_kernel(bands, frames, own_ref, *refs):
    in_refs = [ref.at[band] for band in range(bands) for ref in refs[:-1]]
    finish_kernel(bands, frames, [own_ref.at[band] for band in range(bands)], in_refs, refs[-1])


def gain_kernel(me_ref, *refs):
    *tile_refs, out_ref, sum_ref = refs
    total = tile_refs[0][...]
    for ref in tile_refs[1:]:
        total = total + ref[...]
    sum_ref[...] = total
    count = out_ref.shape[1] // LANES
    for r in range(count):
        out_ref[:, r * LANES:(r + 1) * LANES] = sum_ref[pl.ds(me_ref[0] * count + r, 1), :]


def shifted(value, axis, step):
    count = lax.axis_size(axis)
    return lax.ppermute(value, axis, [((i + step) % count, i) for i in range(count)])


def group_sum(value, axis, beside=()):
    count = lax.axis_size(axis)
    stride = 1
    while stride < count:
        left = count // stride
        radix = 4 if left % 4 == 0 else 2 if left % 2 == 0 else left
        parts = [value]
        for step in range(1, radix):
            pairs = []
            for i in range(count):
                digit = i // stride % radix
                other = digit ^ step if radix in (2, 4) else (digit + step) % radix
                pairs.append((i + (other - digit) * stride, i))
            parts.append(lax.ppermute(value, axis, pairs))
        parts, beside = lax.optimization_barrier((parts, beside))
        value = sum(parts[1:], parts[0])
        stride *= radix
    return value, beside


def per_device(inputs, out_grad, norm_gain, pos_bias, w_query, w_key, w_value, w_out):
    clips, frames, pixels, width = inputs.shape
    group = pos_bias.shape[0]
    tm = lax.axis_size("tm")
    me = lax.axis_index("tm")
    chans = width * tm
    head_dim = width // group
    total = frames * pixels
    bands = pixels // BAND
    rows = frames * BAND
    offsets = 2 * frames - 1
    span = -(-offsets * BAND // LANES) * LANES
    lines = -(-max(chans // LANES, group) // BAND) * BAND
    dims = (tm, frames, pixels, width, group, head_dim, 1e-06)
    x0 = inputs.reshape(total, width)
    g_bands = [out_grad[:, :, n * BAND:(n + 1) * BAND].reshape(rows, width) for n in range(bands)]
    x_parts = [x0] + [shifted(x0, "tm", k) for k in range(1, tm)]
    g_parts = [[g] + [shifted(g, "tm", k) for k in range(1, tm)] for g in g_bands]
    me1 = me.astype(jnp.int32).reshape(1)
    gain = norm_gain.reshape(1, chans)
    spread = jnp.broadcast_to(pos_bias[:, :, None], (*pos_bias.shape, BAND)).reshape(group, -1)
    smem, vmem = pl.BlockSpec(memory_space=pltpu.SMEM), pl.BlockSpec(memory_space=pltpu.VMEM)
    params = pltpu.CompilerParams(vmem_limit_bytes=VMEM_LIMIT)
    held = [x0, w_query, w_key, w_value, w_out, gain]
    held = [pltpu.with_memory_space_constraint(h, pltpu.HBM) for h in held]
    rel, x0, proj, w_out, gain = pl.pallas_call(
        functools.partial(stage_kernel, frames, width),
        in_specs=[vmem] + [pl.BlockSpec(memory_space=pltpu.HBM)] * len(held),
        out_specs=[vmem] * 5,
        out_shape=[
            pltpu.VMEM((frames, group, rows), F32),
            pltpu.VMEM((total, width), BF16),
            pltpu.VMEM((chans, 3 * width), BF16),
            pltpu.VMEM((width, chans), BF16),
            pltpu.VMEM((1, chans), F32),
        ],
        scratch_shapes=[pltpu.SemaphoreType.DMA((len(held),))],
        compiler_params=params,
        cost_estimate=pl.CostEstimate(flops=0, bytes_accessed=8_000_000, transcendentals=0),
        name="stage",
    )(spread, *held)
    x_parts[0] = x0
    qkv, probs, xb, inv, mix_own, *mix_out = pl.pallas_call(
        functools.partial(forward_kernel, dims),
        in_specs=[smem] + [vmem] * (tm + 4),
        out_specs=[vmem] * (5 + tm - 1),
        out_shape=[
            pltpu.VMEM((bands, rows, 3 * width), BF16),
            pltpu.VMEM((bands, group, rows, rows), BF16),
            pltpu.VMEM((bands, rows, chans), BF16),
            pltpu.VMEM((bands, rows, LANES), F32),
            pltpu.VMEM((bands, rows, width), F32),
        ] + [pltpu.VMEM((bands, rows, width), BF16)] * (tm - 1),
        scratch_shapes=[
            pltpu.VMEM((total, chans), BF16),
            pltpu.VMEM((bands, rows, chans), BF16),
            pltpu.VMEM((bands, rows, width), BF16),
        ],
        compiler_params=params,
        cost_estimate=pl.CostEstimate(flops=4_000_000_000, bytes_accessed=8_000_000, transcendentals=0),
        name="attend",
    )(me1, *x_parts, gain, rel, proj, w_out)
    mix_in = [shifted(mix_out[k - 1], "tm", k) for k in range(1, tm)]
    owns, ins, carry = [], [], []
    diag = (frames, group, rows)
    for band in range(bands):
        last = band == bands - 1
        scratch = [pltpu.VMEM((rows, chans), BF16), pltpu.VMEM((group, rows, rows), BF16), pltpu.VMEM((rows, chans), F32)]
        if last:
            extra = [jax.ShapeDtypeStruct((lines, LANES + span), F32)]
            scratch.append(pltpu.VMEM(diag, F32))
        else:
            extra = [jax.ShapeDtypeStruct((1, chans), F32), jax.ShapeDtypeStruct(diag, F32)]
        own, *rest = pl.pallas_call(
            functools.partial(backward_kernel, dims, band, last),
            in_specs=[smem] + [vmem] * (tm + 7 + len(carry)),
            out_specs=[vmem] * (tm + len(extra)),
            out_shape=[jax.ShapeDtypeStruct((rows, width), F32)]
            + [jax.ShapeDtypeStruct((rows, width), BF16)] * (tm - 1) + extra,
            scratch_shapes=scratch,
            compiler_params=params,
            cost_estimate=pl.CostEstimate(flops=2_500_000_000, bytes_accessed=0, transcendentals=0),
            name="attend_back",
        )(me1, *g_parts[band], gain, qkv, probs, xb, inv, proj, w_out, *carry)
        sent, carry = rest[:tm - 1], rest[tm - 1:]
        owns.append(own)
        ins += [shifted(sent[k - 1], "tm", k) for k in range(1, tm)]

    result = jax.ShapeDtypeStruct((total, width), BF16)
    finish_cost = pl.CostEstimate(flops=0, bytes_accessed=1_500_000, transcendentals=0)
    small, (ins[:-1], mix_in) = group_sum(carry[0], "dp", (ins[:-1], mix_in))
    block_out = pl.pallas_call(
        functools.partial(finish_out_kernel, bands, frames),
        in_specs=[vmem] * tm,
        out_specs=vmem,
        out_shape=result,
        compiler_params=params,
        cost_estimate=finish_cost,
        name="finish_out",
    )(mix_own, *mix_in)
    small, (block_out, ins[-1]) = group_sum(small, "space", (block_out, ins[-1]))
    tile = small[:chans // LANES, :LANES]
    tiles = [shifted(tile, "tm", k) for k in range(1, tm)]
    input_grad, bias_grad = pl.pallas_call(
        functools.partial(finish_grad_kernel, bands, frames),
        in_specs=[vmem] * (1 + bands * tm),
        out_specs=[vmem] * 2,
        out_shape=[result, jax.ShapeDtypeStruct((group, offsets), F32)],
        compiler_params=params,
        cost_estimate=finish_cost,
        name="finish_grad",
    )(small, *owns, *ins)
    tiles, input_grad = lax.optimization_barrier((tiles, input_grad))
    gain_grad = pl.pallas_call(
        gain_kernel,
        in_specs=[smem] + [vmem] * tm,
        out_specs=vmem,
        out_shape=jax.ShapeDtypeStruct((1, width), F32),
        scratch_shapes=[pltpu.VMEM(tile.shape, F32)],
        compiler_params=params,
        name="gain_sum",
    )(me1, tile, *tiles)
    return (block_out.reshape(inputs.shape), input_grad.reshape(inputs.shape), gain_grad.reshape(width), bias_grad)


def solution(mesh):
    return jax.shard_map(
        per_device,
        mesh=mesh,
        in_specs=(
            P("dp", None, "space", "tm"),
            P("dp", None, "space", "tm"),
            P(),
            P("tm", None),
            P(None, "tm"),
            P(None, "tm"),
            P(None, "tm"),
            P("tm", None),
        ),
        out_specs=(
            P("dp", None, "space", "tm"),
            P("dp", None, "space", "tm"),
            P("tm"),
            P("tm", None),
        ),
        check_vma=False,
    )
```

```python
import functools

import jax
import jax.numpy as jnp
from jax import lax
from jax.experimental import pallas as pl
from jax.experimental.pallas import tpu as pltpu
from jax.sharding import PartitionSpec as P

CHUNK = 4
BAND = 8
LANES = 128
FAR = -1e30
F32, BF16 = jnp.float32, jnp.bfloat16
NT = (((1,), (1,)), ((), ()))
NN = (((1,), (0,)), ((), ()))
TN = (((0,), (0,)), ((), ()))
VMEM_LIMIT = 24 * 1024 * 1024


def mm(a, b, dims=NN):
    return lax.dot_general(a, b, dims, preferred_element_type=F32)


def same_pixel(rows):
    row = lax.broadcasted_iota(jnp.int32, (BAND, rows), 0)
    lane = lax.broadcasted_iota(jnp.int32, (BAND, rows), 1)
    return (lane & (BAND - 1)) == row


def head_lanes(head_dim, rows):
    return lax.broadcasted_iota(jnp.int32, (rows, LANES), 1) // head_dim


def stack_heads(pair, owner, per_pair, factor=None):
    pair = pair if factor is None else pair * jnp.asarray(factor, pair.dtype)
    return jnp.concatenate([jnp.where(owner == h, pair, jnp.zeros_like(pair)) for h in range(per_pair)], 0)


def pick_heads(parts, owner):
    out = parts[0]
    for h in range(1, len(parts)):
        out = jnp.where(owner == h, parts[h], out)
    return out


def stage_kernel(frames, width, bias_ref, x_ref, wq_ref, wk_ref, wv_ref, wo_ref, gain_ref,
                 rel_ref, x_out, proj_out, wo_out, gain_out, sems):
    pairs = [(x_ref, x_out), (wo_ref, wo_out), (gain_ref, gain_out)]
    pairs += [(w, proj_out.at[:, n * width:(n + 1) * width]) for n, w in enumerate((wq_ref, wk_ref, wv_ref))]
    copies = [pltpu.make_async_copy(source, target, sems.at[n]) for n, (source, target) in enumerate(pairs)]
    for copy in copies:
        copy.start()
    rows = rel_ref.shape[2]
    for i in range(frames):
        start = (frames - 1 - i) * BAND
        rel_ref[i] = bias_ref[:, start:start + rows]
    for copy in copies:
        copy.wait()


def forward_kernel(dims, me_ref, *refs):
    tm, frames, pixels, width, group, head_dim, eps = dims
    x_refs = refs[:tm]
    gain_ref, rel_ref, proj_ref, wo_ref = refs[tm:tm + 4]
    qkv_ref, p_ref, xb_ref, inv_ref, own_ref = refs[tm + 4:tm + 9]
    msg_refs = refs[tm + 9:tm + 9 + tm - 1]
    xw_ref, normed_ref, att_ref = refs[tm + 9 + tm - 1:]
    me = me_ref[0]
    rows = frames * BAND
    bands = pixels // BAND
    per_pair = LANES // head_dim
    scale = head_dim ** -0.5

    def place(k):
        return pl.multiple_of(lax.rem(me + k, tm) * width, width)

    for k in range(tm):
        xw_ref[:, pl.ds(place(k), width)] = x_refs[k][...]
    for f in range(0, frames, 2):
        both = xw_ref[f * pixels:(f + 2) * pixels, :].astype(F32).reshape(2, bands, BAND, -1)
        for band in range(bands):
            x = both[:, band].reshape(2 * BAND, -1)
            inv = lax.rsqrt(jnp.mean(x * x, axis=-1, keepdims=True) + eps)
            at = slice(f * BAND, (f + 2) * BAND)
            normed_ref[band, at, :] = (x * inv * gain_ref[...]).astype(BF16)
            xb_ref[band, at, :] = x.astype(BF16)
            inv_ref[band, at, :] = jnp.broadcast_to(inv, (2 * BAND, LANES))
    same = same_pixel(rows)[None]
    owner = head_lanes(head_dim, rows)
    total = frames * pixels
    qkv = mm(normed_ref[...].reshape(total, -1), proj_ref[...]).astype(BF16)
    qkv_ref[...] = qkv.reshape(bands, rows, 3 * width)
    for band in range(bands):
        for pair in range(width // LANES):
            qp, kp, vp = (
                qkv_ref[band, :, n * width + pair * LANES:n * width + (pair + 1) * LANES] for n in range(3)
            )
            scores = mm(stack_heads(qp, owner, per_pair, scale), kp, NT)
            outs = []
            for h in range(per_pair):
                head = pair * per_pair + h
                for f in range(0, frames, CHUNK):
                    at = slice(f * BAND, (f + CHUNK) * BAND)
                    s = scores[h * rows + f * BAND:h * rows + (f + CHUNK) * BAND].reshape(CHUNK, BAND, rows)
                    s = jnp.where(same, s + rel_ref[f:f + CHUNK, head:head + 1, :], FAR)
                    s = s.reshape(CHUNK * BAND, rows)
                    e = jnp.exp(s - jnp.max(s, axis=-1, keepdims=True))
                    p_ref[band, head, at, :] = (e * (1.0 / jnp.sum(e, axis=-1, keepdims=True))).astype(BF16)
                outs.append(mm(p_ref[band, head], vp))
            att_ref[band, :, pair * LANES:(pair + 1) * LANES] = pick_heads(outs, owner).astype(BF16)
    att = att_ref[...].reshape(total, width)
    for k in range(1, tm):
        part = mm(att, wo_ref[:, pl.ds(place(tm - k), width)]).astype(BF16)
        msg_refs[k - 1][...] = part.reshape(bands, rows, width)
    own = mm(att, wo_ref[:, pl.ds(place(0), width)]).reshape(bands, rows, width)
    own_ref[...] = own + xb_ref[:, :, pl.ds(place(0), width)].astype(F32)


def backward_kernel(dims, me_ref, *refs):
    tm, frames, pixels, width, group, head_dim, eps = dims
    g_refs = refs[:tm]
    gain_ref, qkv_ref, p_ref, xb_ref, inv_ref, proj_ref, wo_ref = refs[tm:tm + 7]
    own_ref, small_ref = refs[tm + 7:tm + 9]
    msg_refs = refs[tm + 9:tm + 9 + tm - 1]
    gw_ref, da_ref, ds_ref, dqkv_ref, grad_ref, diag_ref = refs[tm + 9 + tm - 1:]
    me = me_ref[0]
    rows = frames * BAND
    bands = pixels // BAND
    per_pair = LANES // head_dim
    scale = head_dim ** -0.5
    chans = width * tm
    total = frames * pixels

    def place(k):
        return pl.multiple_of(lax.rem(me + k, tm) * width, width)

    for k in range(tm):
        gw_ref[:, pl.ds(place(k), width)] = g_refs[k][...]
    owner = head_lanes(head_dim, rows)
    d_att = mm(gw_ref[...], wo_ref[...], NT).reshape(frames, bands, BAND, width)
    for band in range(bands):
        da_ref[band] = d_att[:, band].reshape(rows, width).astype(BF16)
    for band in range(bands):
        for pair in range(width // LANES):
            cols = [slice(n * width + pair * LANES, n * width + (pair + 1) * LANES) for n in range(3)]
            qp, kp, vp = (qkv_ref[band, :, c] for c in cols)
            da = da_ref[band, :, pair * LANES:(pair + 1) * LANES]
            d_prob = mm(stack_heads(da, owner, per_pair), vp, NT)
            parts = [[], [], []]
            for h in range(per_pair):
                head = pair * per_pair + h
                for f in range(0, frames, CHUNK):
                    at = slice(f * BAND, (f + CHUNK) * BAND)
                    full = p_ref[band, head, at, :].astype(F32)
                    t = d_prob[h * rows + f * BAND:h * rows + (f + CHUNK) * BAND]
                    score = full * (t - jnp.sum(full * t, axis=-1, keepdims=True))
                    ds_ref[band, head, at, :] = (score * scale).astype(BF16)
                    part = jnp.sum(score.reshape(CHUNK, BAND, rows), axis=1, keepdims=True)
                    if band:
                        part = part + diag_ref[f:f + CHUNK, head:head + 1, :]
                    diag_ref[f:f + CHUNK, head:head + 1, :] = part
                probs, score = p_ref[band, head], ds_ref[band, head]
                parts[0].append(mm(score, kp))
                parts[1].append(mm(score, qp, TN))
                parts[2].append(mm(probs, da, TN))
            for n in range(3):
                dqkv_ref[band, :, cols[n]] = pick_heads(parts[n], owner).astype(BF16)
    grad = mm(dqkv_ref[...].reshape(total, 3 * width), proj_ref[...], NT)
    grad_ref[...] = grad.reshape(bands, rows, chans)
    gain_sum = jnp.zeros((BAND, chans), F32)
    for f in range(0, frames, 2):
        at = slice(f * BAND, (f + 2) * BAND)
        for band in range(bands):
            grad, x = grad_ref[band, at, :], xb_ref[band, at, :].astype(F32)
            inv = inv_ref[band, at, :1]
            scaled = x * inv
            gain_sum = gain_sum + jnp.sum((grad * scaled).reshape(2, BAND, chans), axis=0)
            term = grad * gain_ref[...]
            inner = jnp.mean(term * scaled, axis=-1, keepdims=True)
            grad_ref[band, at, :] = inv * (term - scaled * inner)
    for k in range(1, tm):
        msg_refs[k - 1][...] = grad_ref[:, :, pl.ds(place(tm - k), width)].astype(BF16)
    for f in range(0, frames, 2):
        at = slice(f * BAND, (f + 2) * BAND)
        both = g_refs[0][f * pixels:(f + 2) * pixels, :].astype(F32).reshape(2, bands, BAND, width)
        for band in range(bands):
            own = grad_ref[band, at, pl.ds(place(0), width)]
            own_ref[band, at, :] = own + both[:, band].reshape(2 * BAND, width)
    gain_sum = jnp.sum(gain_sum, axis=0, keepdims=True)
    small_ref[...] = jnp.zeros_like(small_ref)
    for r in range(chans // LANES):
        small_ref[r:r + 1, :LANES] = gain_sum[:, r * LANES:(r + 1) * LANES]
    span = small_ref.shape[1] - LANES
    bias = jnp.zeros((group, span), F32)
    for i in range(frames):
        before = (frames - 1 - i) * BAND
        bias = bias + jnp.pad(diag_ref[i], ((0, 0), (before, span - before - rows)))
    small_ref[:group, LANES:] = bias


def finish_kernel(own_ref, in_refs, out_ref):
    bands, rows, width = own_ref.shape
    frames = rows // BAND
    parts = []
    for band in range(bands):
        value = own_ref[band]
        for ref in in_refs:
            value = value + ref[band].astype(F32)
        parts.append(value.reshape(frames, 1, BAND, width))
    value = jnp.concatenate(parts, axis=1)
    out_ref[...] = value.reshape(out_ref.shape).astype(out_ref.dtype)


def finish_grad_kernel(small_ref, own_ref, *refs):
    *in_refs, out_ref, bias_ref = refs
    finish_kernel(own_ref, in_refs, out_ref)
    group, offsets = bias_ref.shape
    value = small_ref[:, LANES:]
    high = value.astype(BF16)
    rest = value - high.astype(F32)
    middle = rest.astype(BF16)
    low = (rest - middle.astype(F32)).astype(BF16)
    span = value.shape[1]
    lane = lax.broadcasted_iota(jnp.int32, (span, LANES), 0) // BAND
    put = (lane == lax.broadcasted_iota(jnp.int32, (span, LANES), 1)).astype(F32).astype(BF16)
    total = mm(high, put) + mm(middle, put) + mm(low, put)
    bias_ref[...] = total[:group, :offsets]


def finish_out_kernel(own_ref, *refs):
    finish_kernel(own_ref, refs[:-1], refs[-1])


def gain_kernel(me_ref, *refs):
    *tile_refs, out_ref, sum_ref = refs
    total = tile_refs[0][...]
    for ref in tile_refs[1:]:
        total = total + ref[...]
    sum_ref[...] = total
    count = out_ref.shape[1] // LANES
    for r in range(count):
        out_ref[:, r * LANES:(r + 1) * LANES] = sum_ref[pl.ds(me_ref[0] * count + r, 1), :]


def shifted(value, axis, step):
    count = lax.axis_size(axis)
    return lax.ppermute(value, axis, [((i + step) % count, i) for i in range(count)])


def group_sum(value, axis):
    count = lax.axis_size(axis)
    step = 1
    while count % (2 * step) == 0:
        value = value + lax.ppermute(value, axis, [(i ^ step, i) for i in range(count)])
        step *= 2
    odd = count // step
    if odd > 1:
        pairs = [[((i + k * step) % count, i) for i in range(count)] for k in range(1, odd)]
        value = sum((lax.ppermute(value, axis, p) for p in pairs), value)
    return value


def per_device(inputs, out_grad, norm_gain, pos_bias, w_query, w_key, w_value, w_out):
    clips, frames, pixels, width = inputs.shape
    group = pos_bias.shape[0]
    tm = lax.axis_size("tm")
    me = lax.axis_index("tm")
    chans = width * tm
    head_dim = width // group
    total = frames * pixels
    bands = pixels // BAND
    rows = frames * BAND
    offsets = 2 * frames - 1
    span = -(-offsets * BAND // LANES) * LANES
    lines = -(-max(chans // LANES, group) // BAND) * BAND
    dims = (tm, frames, pixels, width, group, head_dim, 1e-06)
    x0, g0 = inputs.reshape(total, width), out_grad.reshape(total, width)
    x_parts = [x0] + [shifted(x0, "tm", k) for k in range(1, tm)]
    g_parts = [g0] + [shifted(g0, "tm", k) for k in range(1, tm)]
    me1 = me.astype(jnp.int32).reshape(1)
    gain = norm_gain.reshape(1, chans)
    spread = jnp.broadcast_to(pos_bias[:, :, None], (*pos_bias.shape, BAND)).reshape(group, -1)
    smem, vmem = pl.BlockSpec(memory_space=pltpu.SMEM), pl.BlockSpec(memory_space=pltpu.VMEM)
    params = pltpu.CompilerParams(vmem_limit_bytes=VMEM_LIMIT)
    held = [x0, w_query, w_key, w_value, w_out, gain]
    held = [pltpu.with_memory_space_constraint(h, pltpu.HBM) for h in held]
    rel, x0, proj, w_out, gain = pl.pallas_call(
        functools.partial(stage_kernel, frames, width),
        in_specs=[vmem] + [pl.BlockSpec(memory_space=pltpu.HBM)] * len(held),
        out_specs=[vmem] * 5,
        out_shape=[
            pltpu.VMEM((frames, group, rows), F32),
            pltpu.VMEM((total, width), BF16),
            pltpu.VMEM((chans, 3 * width), BF16),
            pltpu.VMEM((width, chans), BF16),
            pltpu.VMEM((1, chans), F32),
        ],
        scratch_shapes=[pltpu.SemaphoreType.DMA((len(held),))],
        compiler_params=params,
        cost_estimate=pl.CostEstimate(flops=0, bytes_accessed=8_000_000, transcendentals=0),
        name="stage",
    )(spread, *held)
    x_parts[0] = x0
    qkv, probs, xb, inv, mix_own, *mix_out = pl.pallas_call(
        functools.partial(forward_kernel, dims),
        in_specs=[smem] + [vmem] * (tm + 4),
        out_specs=[vmem] * (5 + tm - 1),
        out_shape=[
            pltpu.VMEM((bands, rows, 3 * width), BF16),
            pltpu.VMEM((bands, group, rows, rows), BF16),
            pltpu.VMEM((bands, rows, chans), BF16),
            pltpu.VMEM((bands, rows, LANES), F32),
            pltpu.VMEM((bands, rows, width), F32),
        ] + [pltpu.VMEM((bands, rows, width), BF16)] * (tm - 1),
        scratch_shapes=[
            pltpu.VMEM((total, chans), BF16),
            pltpu.VMEM((bands, rows, chans), BF16),
            pltpu.VMEM((bands, rows, width), BF16),
        ],
        compiler_params=params,
        cost_estimate=pl.CostEstimate(flops=4_000_000_000, bytes_accessed=8_000_000, transcendentals=0),
        name="attend",
    )(me1, *x_parts, gain, rel, proj, w_out)
    mix_in = [shifted(mix_out[k - 1], "tm", k) for k in range(1, tm)]
    grad_own, small, *grad_out = pl.pallas_call(
        functools.partial(backward_kernel, dims),
        in_specs=[smem] + [vmem] * (tm + 7),
        out_specs=[vmem] * (2 + tm - 1),
        out_shape=[
            pltpu.VMEM((bands, rows, width), F32),
            pltpu.VMEM((lines, LANES + span), F32),
        ] + [pltpu.VMEM((bands, rows, width), BF16)] * (tm - 1),
        scratch_shapes=[
            pltpu.VMEM((total, chans), BF16),
            pltpu.VMEM((bands, rows, width), BF16),
            pltpu.VMEM((bands, group, rows, rows), BF16),
            pltpu.VMEM((bands, rows, 3 * width), BF16),
            pltpu.VMEM((bands, rows, chans), F32),
            pltpu.VMEM((frames, group, rows), F32),
        ],
        compiler_params=params,
        cost_estimate=pl.CostEstimate(flops=6_000_000_000, bytes_accessed=0, transcendentals=0),
        name="attend_back",
    )(me1, *g_parts, gain, qkv, probs, xb, inv, proj, w_out)
    grad_in = [shifted(grad_out[k - 1], "tm", k) for k in range(1, tm)]
    result = jax.ShapeDtypeStruct((total, width), BF16)
    finish_cost = pl.CostEstimate(flops=0, bytes_accessed=1_500_000, transcendentals=0)
    block_out = pl.pallas_call(
        finish_out_kernel,
        in_specs=[vmem] * tm,
        out_specs=vmem,
        out_shape=result,
        compiler_params=params,
        cost_estimate=finish_cost,
        name="finish_out",
    )(mix_own, *mix_in)
    small, mix_in = lax.optimization_barrier((group_sum(small, "dp"), mix_in))
    small, block_out, grad_in = lax.optimization_barrier((group_sum(small, "space"), block_out, grad_in))
    tile = small[:chans // LANES, :LANES]
    tiles = [shifted(tile, "tm", k) for k in range(1, tm)]
    input_grad, bias_grad = pl.pallas_call(
        finish_grad_kernel,
        in_specs=[vmem] * (1 + tm),
        out_specs=[vmem] * 2,
        out_shape=[result, jax.ShapeDtypeStruct((group, offsets), F32)],
        compiler_params=params,
        cost_estimate=finish_cost,
        name="finish_grad",
    )(small, grad_own, *grad_in)
    tiles, input_grad = lax.optimization_barrier((tiles, input_grad))
    gain_grad = pl.pallas_call(
        gain_kernel,
        in_specs=[smem] + [vmem] * tm,
        out_specs=vmem,
        out_shape=jax.ShapeDtypeStruct((1, width), F32),
        scratch_shapes=[pltpu.VMEM(tile.shape, F32)],
        compiler_params=params,
        name="gain_sum",
    )(me1, tile, *tiles)
    return (block_out.reshape(inputs.shape), input_grad.reshape(inputs.shape), gain_grad.reshape(width), bias_grad)


def solution(mesh):
    return jax.shard_map(
        per_device,
        mesh=mesh,
        in_specs=(
            P("dp", None, "space", "tm"),
            P("dp", None, "space", "tm"),
            P(),
            P("tm", None),
            P(None, "tm"),
            P(None, "tm"),
            P(None, "tm"),
            P("tm", None),
        ),
        out_specs=(
            P("dp", None, "space", "tm"),
            P("dp", None, "space", "tm"),
            P("tm"),
            P("tm", None),
        ),
        check_vma=False,
    )
```

```python
import functools

import jax
import jax.numpy as jnp
from jax import lax
from jax.experimental import pallas as pl
from jax.experimental.pallas import tpu as pltpu
from jax.sharding import PartitionSpec as P

CHUNK = 4
BAND = 8
LANES = 128
FAR = -1e30
F32, BF16 = jnp.float32, jnp.bfloat16
NT = (((1,), (1,)), ((), ()))
NN = (((1,), (0,)), ((), ()))
TN = (((0,), (0,)), ((), ()))
VMEM_LIMIT = 24 * 1024 * 1024


def mm(a, b, dims=NN):
    return lax.dot_general(a, b, dims, preferred_element_type=F32)


def same_pixel(rows):
    row = lax.broadcasted_iota(jnp.int32, (BAND, rows), 0)
    lane = lax.broadcasted_iota(jnp.int32, (BAND, rows), 1)
    return (lane & (BAND - 1)) == row


def head_lanes(head_dim, rows):
    return lax.broadcasted_iota(jnp.int32, (rows, LANES), 1) // head_dim


def stack_heads(pair, owner, per_pair, factor=None):
    pair = pair if factor is None else pair * jnp.asarray(factor, pair.dtype)
    return jnp.concatenate([jnp.where(owner == h, pair, jnp.zeros_like(pair)) for h in range(per_pair)], 0)


def pick_heads(parts, owner):
    out = parts[0]
    for h in range(1, len(parts)):
        out = jnp.where(owner == h, parts[h], out)
    return out


def stage_kernel(frames, width, bias_ref, x_ref, wq_ref, wk_ref, wv_ref, wo_ref, gain_ref,
                 rel_ref, x_out, proj_out, wo_out, gain_out, sems):
    pairs = [(x_ref, x_out), (wo_ref, wo_out), (gain_ref, gain_out)]
    pairs += [(w, proj_out.at[:, n * width:(n + 1) * width]) for n, w in enumerate((wq_ref, wk_ref, wv_ref))]
    copies = [pltpu.make_async_copy(source, target, sems.at[n]) for n, (source, target) in enumerate(pairs)]
    for copy in copies:
        copy.start()
    rows = rel_ref.shape[2]
    for i in range(frames):
        start = (frames - 1 - i) * BAND
        rel_ref[i] = bias_ref[:, start:start + rows]
    for copy in copies:
        copy.wait()


def forward_kernel(dims, me_ref, *refs):
    tm, frames, pixels, width, group, head_dim, eps = dims
    x_refs = refs[:tm]
    gain_ref, rel_ref, proj_ref, wo_ref = refs[tm:tm + 4]
    qkv_ref, p_ref, xb_ref, inv_ref, own_ref = refs[tm + 4:tm + 9]
    msg_refs = refs[tm + 9:tm + 9 + tm - 1]
    xw_ref, normed_ref, att_ref = refs[tm + 9 + tm - 1:]
    me = me_ref[0]
    rows = frames * BAND
    bands = pixels // BAND
    per_pair = LANES // head_dim
    scale = head_dim ** -0.5

    def place(k):
        return pl.multiple_of(lax.rem(me + k, tm) * width, width)

    for k in range(tm):
        xw_ref[:, pl.ds(place(k), width)] = x_refs[k][...]
    for f in range(0, frames, 2):
        both = xw_ref[f * pixels:(f + 2) * pixels, :].astype(F32).reshape(2, bands, BAND, -1)
        for band in range(bands):
            x = both[:, band].reshape(2 * BAND, -1)
            inv = lax.rsqrt(jnp.mean(x * x, axis=-1, keepdims=True) + eps)
            at = slice(f * BAND, (f + 2) * BAND)
            normed_ref[band, at, :] = (x * inv * gain_ref[...]).astype(BF16)
            xb_ref[band, at, :] = x.astype(BF16)
            inv_ref[band, at, :] = jnp.broadcast_to(inv, (2 * BAND, LANES))
    same = same_pixel(rows)[None]
    owner = head_lanes(head_dim, rows)
    total = frames * pixels
    qkv = mm(normed_ref[...].reshape(total, -1), proj_ref[...]).astype(BF16)
    qkv_ref[...] = qkv.reshape(bands, rows, 3 * width)
    for band in range(bands):
        for pair in range(width // LANES):
            qp, kp, vp = (
                qkv_ref[band, :, n * width + pair * LANES:n * width + (pair + 1) * LANES] for n in range(3)
            )
            scores = mm(stack_heads(qp, owner, per_pair, scale), kp, NT)
            outs = []
            for h in range(per_pair):
                head = pair * per_pair + h
                for f in range(0, frames, CHUNK):
                    at = slice(f * BAND, (f + CHUNK) * BAND)
                    s = scores[h * rows + f * BAND:h * rows + (f + CHUNK) * BAND].reshape(CHUNK, BAND, rows)
                    s = jnp.where(same, s + rel_ref[f:f + CHUNK, head:head + 1, :], FAR)
                    s = s.reshape(CHUNK * BAND, rows)
                    e = jnp.exp(s - jnp.max(s, axis=-1, keepdims=True))
                    p_ref[band, head, at, :] = (e * (1.0 / jnp.sum(e, axis=-1, keepdims=True))).astype(BF16)
                outs.append(mm(p_ref[band, head], vp))
            att_ref[band, :, pair * LANES:(pair + 1) * LANES] = pick_heads(outs, owner).astype(BF16)
    att = att_ref[...].reshape(total, width)
    for k in range(1, tm):
        part = mm(att, wo_ref[:, pl.ds(place(tm - k), width)]).astype(BF16)
        msg_refs[k - 1][...] = part.reshape(bands, rows, width)
    own = mm(att, wo_ref[:, pl.ds(place(0), width)]).reshape(bands, rows, width)
    own_ref[...] = own + xb_ref[:, :, pl.ds(place(0), width)].astype(F32)


def backward_kernel(dims, me_ref, *refs):
    tm, frames, pixels, width, group, head_dim, eps = dims
    g_refs = refs[:tm]
    qkv_ref, p_ref, xb_ref, inv_ref, proj_ref, wo_ref = refs[tm:tm + 6]
    grad_ref, tile_ref, bias_ref, gw_ref, da_ref, ds_ref, dqkv_ref, diag_ref = refs[tm + 6:]
    me = me_ref[0]
    rows = frames * BAND
    bands = pixels // BAND
    per_pair = LANES // head_dim
    scale = head_dim ** -0.5
    chans = width * tm
    total = frames * pixels

    def place(k):
        return pl.multiple_of(lax.rem(me + k, tm) * width, width)

    for k in range(tm):
        gw_ref[:, pl.ds(place(k), width)] = g_refs[k][...]
    owner = head_lanes(head_dim, rows)
    d_att = mm(gw_ref[...], wo_ref[...], NT).reshape(frames, bands, BAND, width)
    for band in range(bands):
        da_ref[band] = d_att[:, band].reshape(rows, width).astype(BF16)
    for band in range(bands):
        for pair in range(width // LANES):
            cols = [slice(n * width + pair * LANES, n * width + (pair + 1) * LANES) for n in range(3)]
            qp, kp, vp = (qkv_ref[band, :, c] for c in cols)
            da = da_ref[band, :, pair * LANES:(pair + 1) * LANES]
            d_prob = mm(stack_heads(da, owner, per_pair), vp, NT)
            parts = [[], [], []]
            for h in range(per_pair):
                head = pair * per_pair + h
                for f in range(0, frames, CHUNK):
                    at = slice(f * BAND, (f + CHUNK) * BAND)
                    full = p_ref[band, head, at, :].astype(F32)
                    t = d_prob[h * rows + f * BAND:h * rows + (f + CHUNK) * BAND]
                    score = full * (t - jnp.sum(full * t, axis=-1, keepdims=True))
                    ds_ref[band, head, at, :] = (score * scale).astype(BF16)
                    part = jnp.sum(score.reshape(CHUNK, BAND, rows), axis=1, keepdims=True)
                    if band:
                        part = part + diag_ref[f:f + CHUNK, head:head + 1, :]
                    diag_ref[f:f + CHUNK, head:head + 1, :] = part
                probs, score = p_ref[band, head], ds_ref[band, head]
                parts[0].append(mm(score, kp))
                parts[1].append(mm(score, qp, TN))
                parts[2].append(mm(probs, da, TN))
            for n in range(3):
                dqkv_ref[band, :, cols[n]] = pick_heads(parts[n], owner).astype(BF16)
    grad = mm(dqkv_ref[...].reshape(total, 3 * width), proj_ref[...], NT)
    grad_ref[...] = grad.reshape(bands, rows, chans)
    gain_sum = jnp.zeros((BAND, chans), F32)
    for band in range(bands):
        for f in range(0, frames, 2):
            at = slice(f * BAND, (f + 2) * BAND)
            scaled = xb_ref[band, at, :].astype(F32) * inv_ref[band, at, :1]
            gain_sum = gain_sum + jnp.sum((grad_ref[band, at, :] * scaled).reshape(2, BAND, chans), axis=0)
    gain_sum = jnp.sum(gain_sum, axis=0, keepdims=True)
    tile_ref[...] = jnp.zeros_like(tile_ref)
    for r in range(chans // LANES):
        tile_ref[r:r + 1, :] = gain_sum[:, r * LANES:(r + 1) * LANES]
    span = bias_ref.shape[1]
    bias = jnp.zeros((group, span), F32)
    for i in range(frames):
        before = (frames - 1 - i) * BAND
        bias = bias + jnp.pad(diag_ref[i], ((0, 0), (before, span - before - rows)))
    bias_ref[...] = jnp.zeros_like(bias_ref)
    bias_ref[:group, :] = bias


def share_kernel(dims, me_ref, g_ref, gain_ref, grad_ref, xb_ref, inv_ref, own_ref, *refs):
    tm, frames, pixels, width = dims[:4]
    bands = pixels // BAND
    *msg_refs, term_ref = refs
    me = me_ref[0]

    def place(k):
        return pl.multiple_of(lax.rem(me + k, tm) * width, width)

    for f in range(0, frames, 2):
        at = slice(f * BAND, (f + 2) * BAND)
        both = g_ref[f * pixels:(f + 2) * pixels, :].astype(F32).reshape(2, bands, BAND, width)
        for band in range(bands):
            inv = inv_ref[band, at, :1]
            scaled = xb_ref[band, at, :].astype(F32) * inv
            term = grad_ref[band, at, :] * gain_ref[...]
            inner = jnp.mean(term * scaled, axis=-1, keepdims=True)
            term_ref[band, at, :] = inv * (term - scaled * inner)
            own = term_ref[band, at, pl.ds(place(0), width)]
            own_ref[band, at, :] = own + both[:, band].reshape(2 * BAND, width)
    for k in range(1, tm):
        msg_refs[k - 1][...] = term_ref[:, :, pl.ds(place(tm - k), width)].astype(BF16)


def finish_kernel(own_ref, in_refs, out_ref):
    bands, rows, width = own_ref.shape
    frames = rows // BAND
    parts = []
    for band in range(bands):
        value = own_ref[band]
        for ref in in_refs:
            value = value + ref[band].astype(F32)
        parts.append(value.reshape(frames, 1, BAND, width))
    value = jnp.concatenate(parts, axis=1)
    out_ref[...] = value.reshape(out_ref.shape).astype(out_ref.dtype)


def finish_shares(own_ref, *refs):
    finish_kernel(own_ref, refs[:-1], refs[-1])


def sums_kernel(me_ref, parts_ref, gain_ref, bias_ref, sum_ref):
    total = parts_ref[0]
    for n in range(1, parts_ref.shape[0]):
        total = total + parts_ref[n]
    sum_ref[...] = total[:, :LANES]
    count = gain_ref.shape[1] // LANES
    for r in range(count):
        gain_ref[:, r * LANES:(r + 1) * LANES] = sum_ref[pl.ds(me_ref[0] * count + r, 1), :]
    group, offsets = bias_ref.shape
    value = total[:, LANES:]
    high = value.astype(BF16)
    rest = value - high.astype(F32)
    middle = rest.astype(BF16)
    low = (rest - middle.astype(F32)).astype(BF16)
    span = value.shape[1]
    lane = lax.broadcasted_iota(jnp.int32, (span, LANES), 0) // BAND
    put = (lane == lax.broadcasted_iota(jnp.int32, (span, LANES), 1)).astype(F32).astype(BF16)
    summed = mm(high, put) + mm(middle, put) + mm(low, put)
    bias_ref[...] = summed[:group, :offsets]


def shifted(value, axis, step):
    count = lax.axis_size(axis)
    return lax.ppermute(value, axis, [((i + step) % count, i) for i in range(count)])


def to_all(value, axis):
    count = lax.axis_size(axis)
    copies = jnp.broadcast_to(value[None], (count, *value.shape))
    return lax.all_to_all(copies, axis, split_axis=0, concat_axis=0, tiled=True)


def per_device(inputs, out_grad, norm_gain, pos_bias, w_query, w_key, w_value, w_out):
    clips, frames, pixels, width = inputs.shape
    group = pos_bias.shape[0]
    tm = lax.axis_size("tm")
    me = lax.axis_index("tm")
    chans = width * tm
    head_dim = width // group
    total = frames * pixels
    bands = pixels // BAND
    rows = frames * BAND
    offsets = 2 * frames - 1
    span = -(-offsets * BAND // LANES) * LANES
    lines = -(-max(chans // LANES, group) // BAND) * BAND
    dims = (tm, frames, pixels, width, group, head_dim, 1e-06)
    x0, g0 = inputs.reshape(total, width), out_grad.reshape(total, width)
    x_parts = [x0] + [shifted(x0, "tm", k) for k in range(1, tm)]
    g_parts = [g0] + [shifted(g0, "tm", k) for k in range(1, tm)]
    me1 = me.astype(jnp.int32).reshape(1)
    gain = norm_gain.reshape(1, chans)
    spread = jnp.broadcast_to(pos_bias[:, :, None], (*pos_bias.shape, BAND)).reshape(group, -1)
    smem, vmem = pl.BlockSpec(memory_space=pltpu.SMEM), pl.BlockSpec(memory_space=pltpu.VMEM)
    params = pltpu.CompilerParams(vmem_limit_bytes=VMEM_LIMIT)
    held = [x0, w_query, w_key, w_value, w_out, gain]
    held = [pltpu.with_memory_space_constraint(h, pltpu.HBM) for h in held]
    rel, x0, proj, w_out, gain = pl.pallas_call(
        functools.partial(stage_kernel, frames, width),
        in_specs=[vmem] + [pl.BlockSpec(memory_space=pltpu.HBM)] * len(held),
        out_specs=[vmem] * 5,
        out_shape=[
            pltpu.VMEM((frames, group, rows), F32),
            pltpu.VMEM((total, width), BF16),
            pltpu.VMEM((chans, 3 * width), BF16),
            pltpu.VMEM((width, chans), BF16),
            pltpu.VMEM((1, chans), F32),
        ],
        scratch_shapes=[pltpu.SemaphoreType.DMA((len(held),))],
        compiler_params=params,
        cost_estimate=pl.CostEstimate(flops=0, bytes_accessed=8_000_000, transcendentals=0),
        name="stage",
    )(spread, *held)
    x_parts[0] = x0
    qkv, probs, xb, inv, mix_own, *mix_out = pl.pallas_call(
        functools.partial(forward_kernel, dims),
        in_specs=[smem] + [vmem] * (tm + 4),
        out_specs=[vmem] * (5 + tm - 1),
        out_shape=[
            pltpu.VMEM((bands, rows, 3 * width), BF16),
            pltpu.VMEM((bands, group, rows, rows), BF16),
            pltpu.VMEM((bands, rows, chans), BF16),
            pltpu.VMEM((bands, rows, LANES), F32),
            pltpu.VMEM((bands, rows, width), F32),
        ] + [pltpu.VMEM((bands, rows, width), BF16)] * (tm - 1),
        scratch_shapes=[
            pltpu.VMEM((total, chans), BF16),
            pltpu.VMEM((bands, rows, chans), BF16),
            pltpu.VMEM((bands, rows, width), BF16),
        ],
        compiler_params=params,
        cost_estimate=pl.CostEstimate(flops=4_000_000_000, bytes_accessed=8_000_000, transcendentals=0),
        name="attend",
    )(me1, *x_parts, gain, rel, proj, w_out)
    mix_in = [shifted(mix_out[k - 1], "tm", k) for k in range(1, tm)]
    grad, tile, bias = pl.pallas_call(
        functools.partial(backward_kernel, dims),
        in_specs=[smem] + [vmem] * (tm + 6),
        out_specs=[vmem] * 3,
        out_shape=[
            pltpu.VMEM((bands, rows, chans), F32),
            pltpu.VMEM((lines, LANES), F32),
            pltpu.VMEM((lines, span), F32),
        ],
        scratch_shapes=[
            pltpu.VMEM((total, chans), BF16),
            pltpu.VMEM((bands, rows, width), BF16),
            pltpu.VMEM((bands, group, rows, rows), BF16),
            pltpu.VMEM((bands, rows, 3 * width), BF16),
            pltpu.VMEM((frames, group, rows), F32),
        ],
        compiler_params=params,
        cost_estimate=pl.CostEstimate(flops=6_000_000_000, bytes_accessed=0, transcendentals=0),
        name="attend_back",
    )(me1, *g_parts, qkv, probs, xb, inv, proj, w_out)
    grad_own, *grad_out = pl.pallas_call(
        functools.partial(share_kernel, dims),
        in_specs=[smem] + [vmem] * 5,
        out_specs=[vmem] * tm,
        out_shape=[pltpu.VMEM((bands, rows, width), F32)] + [pltpu.VMEM((bands, rows, width), BF16)] * (tm - 1),
        scratch_shapes=[pltpu.VMEM((bands, rows, chans), F32)],
        compiler_params=params,
        cost_estimate=pl.CostEstimate(flops=2_000_000_000, bytes_accessed=0, transcendentals=0),
        name="share",
    )(me1, g0, gain, grad, xb, inv)
    tiles = [shifted(tile, "tm", k) for k in range(1, tm)]
    tiles, grad_out, mix_in = lax.optimization_barrier((tiles, grad_out, mix_in))
    grad_in = [shifted(grad_out[k - 1], "tm", k) for k in range(1, tm)]

    def finish(mine, others):
        return pl.pallas_call(
            finish_shares,
            in_specs=[vmem] * tm,
            out_specs=vmem,
            out_shape=jax.ShapeDtypeStruct((total, width), BF16),
            compiler_params=params,
            cost_estimate=pl.CostEstimate(flops=0, bytes_accessed=1_500_000, transcendentals=0),
            name="finish",
        )(mine, *others)

    small = jnp.concatenate([sum(tiles, tile), bias], axis=1)
    small, mix_in = lax.optimization_barrier((jnp.sum(to_all(small, "dp"), axis=0), mix_in))
    block_out, input_grad = finish(mix_own, mix_in), finish(grad_own, grad_in)
    parts = to_all(small, "space")
    parts, block_out, input_grad = lax.optimization_barrier((parts, block_out, input_grad))
    gain_grad, bias_grad = pl.pallas_call(
        sums_kernel,
        in_specs=[smem, vmem],
        out_specs=[vmem] * 2,
        out_shape=[jax.ShapeDtypeStruct((1, width), F32), jax.ShapeDtypeStruct((group, offsets), F32)],
        scratch_shapes=[pltpu.VMEM(tile.shape, F32)],
        compiler_params=params,
        name="sums",
    )(me1, parts)
    return (block_out.reshape(inputs.shape), input_grad.reshape(inputs.shape), gain_grad.reshape(width), bias_grad)


def solution(mesh):
    return jax.shard_map(
        per_device,
        mesh=mesh,
        in_specs=(
            P("dp", None, "space", "tm"),
            P("dp", None, "space", "tm"),
            P(),
            P("tm", None),
            P(None, "tm"),
            P(None, "tm"),
            P(None, "tm"),
            P("tm", None),
        ),
        out_specs=(
            P("dp", None, "space", "tm"),
            P("dp", None, "space", "tm"),
            P("tm"),
            P("tm", None),
        ),
        check_vma=False,
    )
```

```python
import functools

import jax
import jax.numpy as jnp
from jax import lax
from jax.experimental import pallas as pl
from jax.experimental.pallas import tpu as pltpu
from jax.sharding import PartitionSpec as P

CHUNK = 4
BAND = 8
LANES = 128
FAR = -1e30
F32, BF16 = jnp.float32, jnp.bfloat16
NT = (((1,), (1,)), ((), ()))
NN = (((1,), (0,)), ((), ()))
TN = (((0,), (0,)), ((), ()))
VMEM_LIMIT = 24 * 1024 * 1024


def mm(a, b, dims=NN):
    return lax.dot_general(a, b, dims, preferred_element_type=F32)


def same_pixel(rows):
    row = lax.broadcasted_iota(jnp.int32, (BAND, rows), 0)
    lane = lax.broadcasted_iota(jnp.int32, (BAND, rows), 1)
    return (lane & (BAND - 1)) == row


def head_lanes(head_dim, rows):
    return lax.broadcasted_iota(jnp.int32, (rows, LANES), 1) // head_dim


def stack_heads(pair, owner, per_pair, factor=None):
    pair = pair if factor is None else pair * jnp.asarray(factor, pair.dtype)
    return jnp.concatenate([jnp.where(owner == h, pair, jnp.zeros_like(pair)) for h in range(per_pair)], 0)


def pick_heads(parts, owner):
    out = parts[0]
    for h in range(1, len(parts)):
        out = jnp.where(owner == h, parts[h], out)
    return out


def row_sums(value):
    return mm(value.astype(BF16), jnp.ones((value.shape[1], LANES), BF16))


def over_lanes(tile, lanes):
    return jnp.concatenate([tile] * (lanes // LANES) + [tile[:, :lanes % LANES]], axis=1)


def stage_kernel(frames, width, bias_ref, x_ref, wq_ref, wk_ref, wv_ref, wo_ref, gain_ref,
                 rel_ref, x_out, proj_out, wo_out, gain_out, sems):
    pairs = [(x_ref, x_out), (wo_ref, wo_out), (gain_ref, gain_out)]
    pairs += [(w, proj_out.at[:, n * width:(n + 1) * width]) for n, w in enumerate((wq_ref, wk_ref, wv_ref))]
    copies = [pltpu.make_async_copy(source, target, sems.at[n]) for n, (source, target) in enumerate(pairs)]
    for copy in copies:
        copy.start()
    rows = rel_ref.shape[2]
    for i in range(frames):
        start = (frames - 1 - i) * BAND
        rel_ref[i] = bias_ref[:, start:start + rows]
    for copy in copies:
        copy.wait()


def forward_kernel(dims, me_ref, *refs):
    tm, frames, pixels, width, group, head_dim, eps = dims
    x_refs = refs[:tm]
    gain_ref, rel_ref, proj_ref, wo_ref = refs[tm:tm + 4]
    qkv_ref, p_ref, xb_ref, inv_ref, own_ref = refs[tm + 4:tm + 9]
    msg_refs = refs[tm + 9:tm + 9 + tm - 1]
    xw_ref, normed_ref, att_ref = refs[tm + 9 + tm - 1:]
    me = me_ref[0]
    rows = frames * BAND
    bands = pixels // BAND
    per_pair = LANES // head_dim
    scale = head_dim ** -0.5

    def place(k):
        return pl.multiple_of(lax.rem(me + k, tm) * width, width)

    for k in range(tm):
        xw_ref[:, pl.ds(place(k), width)] = x_refs[k][...]
    for f in range(0, frames, 2):
        both = xw_ref[f * pixels:(f + 2) * pixels, :].astype(F32).reshape(2, bands, BAND, -1)
        for band in range(bands):
            x = both[:, band].reshape(2 * BAND, -1)
            inv = lax.rsqrt(jnp.mean(x * x, axis=-1, keepdims=True) + eps)
            at = slice(f * BAND, (f + 2) * BAND)
            normed_ref[band, at, :] = (x * inv * gain_ref[...]).astype(BF16)
            xb_ref[band, at, :] = x.astype(BF16)
            inv_ref[band, at, :] = jnp.broadcast_to(inv, (2 * BAND, LANES))
    same = same_pixel(rows)[None]
    owner = head_lanes(head_dim, rows)
    total = frames * pixels
    qkv = mm(normed_ref[...].reshape(total, -1), proj_ref[...]).astype(BF16)
    qkv_ref[...] = qkv.reshape(bands, rows, 3 * width)
    for band in range(bands):
        for pair in range(width // LANES):
            qp, kp, vp = (
                qkv_ref[band, :, n * width + pair * LANES:n * width + (pair + 1) * LANES] for n in range(3)
            )
            scores = mm(stack_heads(qp, owner, per_pair, scale), kp, NT)
            outs = []
            for h in range(per_pair):
                head = pair * per_pair + h
                for f in range(0, frames, CHUNK):
                    at = slice(f * BAND, (f + CHUNK) * BAND)
                    s = scores[h * rows + f * BAND:h * rows + (f + CHUNK) * BAND].reshape(CHUNK, BAND, rows)
                    s = jnp.where(same, s + rel_ref[f:f + CHUNK, head:head + 1, :], FAR)
                    s = s.reshape(CHUNK * BAND, rows)
                    e = jnp.exp(s - jnp.max(s, axis=-1, keepdims=True))
                    p_ref[band, head, at, :] = (e * over_lanes(1.0 / row_sums(e), rows)).astype(BF16)
                outs.append(mm(p_ref[band, head], vp))
            att_ref[band, :, pair * LANES:(pair + 1) * LANES] = pick_heads(outs, owner).astype(BF16)
    att = att_ref[...].reshape(total, width)
    for k in range(1, tm):
        part = mm(att, wo_ref[:, pl.ds(place(tm - k), width)]).astype(BF16)
        msg_refs[k - 1][...] = part.reshape(bands, rows, width)
    own = mm(att, wo_ref[:, pl.ds(place(0), width)]).reshape(bands, rows, width)
    own_ref[...] = own + xb_ref[:, :, pl.ds(place(0), width)].astype(F32)


def backward_kernel(dims, band, last, me_ref, *refs):
    tm, frames, pixels, width, group, head_dim, eps = dims
    g_refs = refs[:tm]
    gain_ref, qkv_ref, p_ref, xb_ref, inv_ref, proj_ref, wo_ref = refs[tm:tm + 7]
    rest = list(refs[tm + 7:])
    carried = (rest.pop(0), rest.pop(0)) if band else None
    own_ref = rest.pop(0)
    msg_refs = [rest.pop(0) for _ in range(tm - 1)]
    small_ref = rest.pop(0) if last else None
    gain_out = None if last else rest.pop(0)
    diag_ref = rest.pop() if last else rest.pop(0)
    gw_ref, ds_ref, grad_ref = rest
    me = me_ref[0]
    rows = frames * BAND
    per_pair = LANES // head_dim
    scale = head_dim ** -0.5
    chans = width * tm

    def place(k):
        return pl.multiple_of(lax.rem(me + k, tm) * width, width)

    for k in range(tm):
        gw_ref[:, pl.ds(place(k), width)] = g_refs[k][...]
    owner = head_lanes(head_dim, rows)
    d_att = mm(gw_ref[...], wo_ref[...], NT).astype(BF16)
    grads = [[], [], []]
    for pair in range(width // LANES):
        qp, kp, vp = (
            qkv_ref[band, :, n * width + pair * LANES:n * width + (pair + 1) * LANES] for n in range(3)
        )
        da = d_att[:, pair * LANES:(pair + 1) * LANES]
        d_prob = mm(stack_heads(da, owner, per_pair), vp, NT)
        q_turned, da_turned = qp.T, da.T
        parts = [[], [], []]
        for h in range(per_pair):
            head = pair * per_pair + h
            for f in range(0, frames, CHUNK):
                at = slice(f * BAND, (f + CHUNK) * BAND)
                full = p_ref[band, head, at, :].astype(F32)
                t = d_prob[h * rows + f * BAND:h * rows + (f + CHUNK) * BAND]
                score = full * (t - jnp.sum(full * t, axis=-1, keepdims=True))
                ds_ref[head, at, :] = (score * scale).astype(BF16)
                part = jnp.sum(score.reshape(CHUNK, BAND, rows), axis=1, keepdims=True)
                if carried is not None:
                    part = part + carried[1][f:f + CHUNK, head:head + 1, :]
                diag_ref[f:f + CHUNK, head:head + 1, :] = part
            probs, score = p_ref[band, head], ds_ref[head]
            own = slice(h * head_dim, (h + 1) * head_dim)
            parts[0].append(mm(score, kp))
            parts[1].append(mm(q_turned[own], score))
            parts[2].append(mm(da_turned[own], probs))
        grads[0].append(pick_heads(parts[0], owner).astype(BF16))
        for n in (1, 2):
            grads[n].append(jnp.concatenate(parts[n], axis=0).astype(BF16).T)
    grad_ref[...] = mm(jnp.concatenate(grads[0] + grads[1] + grads[2], axis=1), proj_ref[...], NT)
    gain_sum = jnp.zeros((BAND, chans), F32)
    for f in range(0, frames, 2):
        at = slice(f * BAND, (f + 2) * BAND)
        grad, x = grad_ref[at, :], xb_ref[band, at, :].astype(F32)
        inv = inv_ref[band, at, :1]
        scaled = x * inv
        gain_sum = gain_sum + jnp.sum((grad * scaled).reshape(2, BAND, chans), axis=0)
        term = grad * gain_ref[...]
        inner = jnp.mean(term * scaled, axis=-1, keepdims=True)
        grad_ref[at, :] = inv * (term - scaled * inner)
    for k in range(1, tm):
        msg_refs[k - 1][...] = grad_ref[:, pl.ds(place(tm - k), width)].astype(BF16)
    own_ref[...] = grad_ref[:, pl.ds(place(0), width)] + g_refs[0][...].astype(F32)
    gain_sum = jnp.sum(gain_sum, axis=0, keepdims=True)
    if carried is not None:
        gain_sum = gain_sum + carried[0][...]
    if not last:
        gain_out[...] = gain_sum
        return
    small_ref[...] = jnp.zeros_like(small_ref)
    for r in range(chans // LANES):
        small_ref[r:r + 1, :LANES] = gain_sum[:, r * LANES:(r + 1) * LANES]
    span = small_ref.shape[1] - LANES
    bias = jnp.zeros((group, span), F32)
    for i in range(frames):
        before = (frames - 1 - i) * BAND
        bias = bias + jnp.pad(diag_ref[i], ((0, 0), (before, span - before - rows)))
    small_ref[:group, LANES:] = bias


def finish_kernel(bands, frames, own_refs, in_refs, out_ref):
    each = len(in_refs) // bands
    parts = []
    for band in range(bands):
        value = own_refs[band][...]
        for ref in in_refs[band * each:(band + 1) * each]:
            value = value + ref[...].astype(F32)
        parts.append(value.reshape(frames, 1, BAND, value.shape[-1]))
    value = jnp.concatenate(parts, axis=1)
    out_ref[...] = value.reshape(out_ref.shape).astype(out_ref.dtype)


def finish_grad_kernel(bands, frames, small_ref, *refs):
    *refs, out_ref, bias_ref = refs
    finish_kernel(bands, frames, refs[:bands], refs[bands:], out_ref)
    group, offsets = bias_ref.shape
    value = small_ref[:, LANES:]
    high = value.astype(BF16)
    rest = value - high.astype(F32)
    middle = rest.astype(BF16)
    low = (rest - middle.astype(F32)).astype(BF16)
    span = value.shape[1]
    lane = lax.broadcasted_iota(jnp.int32, (span, LANES), 0) // BAND
    put = (lane == lax.broadcasted_iota(jnp.int32, (span, LANES), 1)).astype(F32).astype(BF16)
    total = mm(high, put) + mm(middle, put) + mm(low, put)
    bias_ref[...] = total[:group, :offsets]


def finish_out_kernel(bands, frames, own_ref, *refs):
    in_refs = [ref.at[band] for band in range(bands) for ref in refs[:-1]]
    finish_kernel(bands, frames, [own_ref.at[band] for band in range(bands)], in_refs, refs[-1])


def gain_kernel(me_ref, *refs):
    *tile_refs, out_ref, sum_ref = refs
    total = tile_refs[0][...]
    for ref in tile_refs[1:]:
        total = total + ref[...]
    sum_ref[...] = total
    count = out_ref.shape[1] // LANES
    for r in range(count):
        out_ref[:, r * LANES:(r + 1) * LANES] = sum_ref[pl.ds(me_ref[0] * count + r, 1), :]


def shifted(value, axis, step):
    count = lax.axis_size(axis)
    return lax.ppermute(value, axis, [((i + step) % count, i) for i in range(count)])


def group_sum(value, axis, beside=()):
    count = lax.axis_size(axis)
    stride = 1
    while stride < count:
        left = count // stride
        radix = 4 if left % 4 == 0 else 2 if left % 2 == 0 else left
        parts = [value]
        for step in range(1, radix):
            pairs = []
            for i in range(count):
                digit = i // stride % radix
                other = digit ^ step if radix in (2, 4) else (digit + step) % radix
                pairs.append((i + (other - digit) * stride, i))
            parts.append(lax.ppermute(value, axis, pairs))
        parts, beside = lax.optimization_barrier((parts, beside))
        value = sum(parts[1:], parts[0])
        stride *= radix
    return value, beside


def per_device(inputs, out_grad, norm_gain, pos_bias, w_query, w_key, w_value, w_out):
    clips, frames, pixels, width = inputs.shape
    group = pos_bias.shape[0]
    tm = lax.axis_size("tm")
    me = lax.axis_index("tm")
    chans = width * tm
    head_dim = width // group
    total = frames * pixels
    bands = pixels // BAND
    rows = frames * BAND
    offsets = 2 * frames - 1
    span = -(-offsets * BAND // LANES) * LANES
    lines = -(-max(chans // LANES, group) // BAND) * BAND
    dims = (tm, frames, pixels, width, group, head_dim, 1e-06)
    x0 = inputs.reshape(total, width)
    g_bands = [out_grad[:, :, n * BAND:(n + 1) * BAND].reshape(rows, width) for n in range(bands)]
    x_parts = [x0] + [shifted(x0, "tm", k) for k in range(1, tm)]
    g_parts = [[g] + [shifted(g, "tm", k) for k in range(1, tm)] for g in g_bands]
    me1 = me.astype(jnp.int32).reshape(1)
    gain = norm_gain.reshape(1, chans)
    spread = jnp.broadcast_to(pos_bias[:, :, None], (*pos_bias.shape, BAND)).reshape(group, -1)
    smem, vmem = pl.BlockSpec(memory_space=pltpu.SMEM), pl.BlockSpec(memory_space=pltpu.VMEM)
    params = pltpu.CompilerParams(vmem_limit_bytes=VMEM_LIMIT)
    held = [x0, w_query, w_key, w_value, w_out, gain]
    held = [pltpu.with_memory_space_constraint(h, pltpu.HBM) for h in held]
    rel, x0, proj, w_out, gain = pl.pallas_call(
        functools.partial(stage_kernel, frames, width),
        in_specs=[vmem] + [pl.BlockSpec(memory_space=pltpu.HBM)] * len(held),
        out_specs=[vmem] * 5,
        out_shape=[
            pltpu.VMEM((frames, group, rows), F32),
            pltpu.VMEM((total, width), BF16),
            pltpu.VMEM((chans, 3 * width), BF16),
            pltpu.VMEM((width, chans), BF16),
            pltpu.VMEM((1, chans), F32),
        ],
        scratch_shapes=[pltpu.SemaphoreType.DMA((len(held),))],
        compiler_params=params,
        cost_estimate=pl.CostEstimate(flops=0, bytes_accessed=8_000_000, transcendentals=0),
        name="stage",
    )(spread, *held)
    x_parts[0] = x0
    qkv, probs, xb, inv, mix_own, *mix_out = pl.pallas_call(
        functools.partial(forward_kernel, dims),
        in_specs=[smem] + [vmem] * (tm + 4),
        out_specs=[vmem] * (5 + tm - 1),
        out_shape=[
            pltpu.VMEM((bands, rows, 3 * width), BF16),
            pltpu.VMEM((bands, group, rows, rows), BF16),
            pltpu.VMEM((bands, rows, chans), BF16),
            pltpu.VMEM((bands, rows, LANES), F32),
            pltpu.VMEM((bands, rows, width), F32),
        ] + [pltpu.VMEM((bands, rows, width), BF16)] * (tm - 1),
        scratch_shapes=[
            pltpu.VMEM((total, chans), BF16),
            pltpu.VMEM((bands, rows, chans), BF16),
            pltpu.VMEM((bands, rows, width), BF16),
        ],
        compiler_params=params,
        cost_estimate=pl.CostEstimate(flops=4_000_000_000, bytes_accessed=8_000_000, transcendentals=0),
        name="attend",
    )(me1, *x_parts, gain, rel, proj, w_out)
    mix_in = [shifted(mix_out[k - 1], "tm", k) for k in range(1, tm)]
    owns, ins, carry = [], [], []
    diag = (frames, group, rows)
    for band in range(bands):
        last = band == bands - 1
        scratch = [pltpu.VMEM((rows, chans), BF16), pltpu.VMEM((group, rows, rows), BF16), pltpu.VMEM((rows, chans), F32)]
        if last:
            extra = [jax.ShapeDtypeStruct((lines, LANES + span), F32)]
            scratch.append(pltpu.VMEM(diag, F32))
        else:
            extra = [jax.ShapeDtypeStruct((1, chans), F32), jax.ShapeDtypeStruct(diag, F32)]
        own, *rest = pl.pallas_call(
            functools.partial(backward_kernel, dims, band, last),
            in_specs=[smem] + [vmem] * (tm + 7 + len(carry)),
            out_specs=[vmem] * (tm + len(extra)),
            out_shape=[jax.ShapeDtypeStruct((rows, width), F32)]
            + [jax.ShapeDtypeStruct((rows, width), BF16)] * (tm - 1) + extra,
            scratch_shapes=scratch,
            compiler_params=params,
            cost_estimate=pl.CostEstimate(flops=2_500_000_000, bytes_accessed=0, transcendentals=0),
            name="attend_back",
        )(me1, *g_parts[band], gain, qkv, probs, xb, inv, proj, w_out, *carry)
        sent, carry = rest[:tm - 1], rest[tm - 1:]
        owns.append(own)
        ins += [shifted(sent[k - 1], "tm", k) for k in range(1, tm)]

    result = jax.ShapeDtypeStruct((total, width), BF16)
    finish_cost = pl.CostEstimate(flops=0, bytes_accessed=1_500_000, transcendentals=0)
    small, (ins[:-1], mix_in) = group_sum(carry[0], "dp", (ins[:-1], mix_in))
    block_out = pl.pallas_call(
        functools.partial(finish_out_kernel, bands, frames),
        in_specs=[vmem] * tm,
        out_specs=vmem,
        out_shape=result,
        compiler_params=params,
        cost_estimate=finish_cost,
        name="finish_out",
    )(mix_own, *mix_in)
    small, (block_out, ins[-1]) = group_sum(small, "space", (block_out, ins[-1]))
    tile = small[:chans // LANES, :LANES]
    tiles = [shifted(tile, "tm", k) for k in range(1, tm)]
    input_grad, bias_grad = pl.pallas_call(
        functools.partial(finish_grad_kernel, bands, frames),
        in_specs=[vmem] * (1 + bands * tm),
        out_specs=[vmem] * 2,
        out_shape=[result, jax.ShapeDtypeStruct((group, offsets), F32)],
        compiler_params=params,
        cost_estimate=finish_cost,
        name="finish_grad",
    )(small, *owns, *ins)
    tiles, input_grad = lax.optimization_barrier((tiles, input_grad))
    gain_grad = pl.pallas_call(
        gain_kernel,
        in_specs=[smem] + [vmem] * tm,
        out_specs=vmem,
        out_shape=jax.ShapeDtypeStruct((1, width), F32),
        scratch_shapes=[pltpu.VMEM(tile.shape, F32)],
        compiler_params=params,
        name="gain_sum",
    )(me1, tile, *tiles)
    return (block_out.reshape(inputs.shape), input_grad.reshape(inputs.shape), gain_grad.reshape(width), bias_grad)


def solution(mesh):
    return jax.shard_map(
        per_device,
        mesh=mesh,
        in_specs=(
            P("dp", None, "space", "tm"),
            P("dp", None, "space", "tm"),
            P(),
            P("tm", None),
            P(None, "tm"),
            P(None, "tm"),
            P(None, "tm"),
            P("tm", None),
        ),
        out_specs=(
            P("dp", None, "space", "tm"),
            P("dp", None, "space", "tm"),
            P("tm"),
            P("tm", None),
        ),
        check_vma=False,
    )
```

```python
import functools

import jax
import jax.numpy as jnp
from jax import lax
from jax.experimental import pallas as pl
from jax.experimental.pallas import tpu as pltpu
from jax.sharding import PartitionSpec as P

CHUNK = 4
BAND = 8
LANES = 128
FAR = -1e30
F32, BF16 = jnp.float32, jnp.bfloat16
NT = (((1,), (1,)), ((), ()))
NN = (((1,), (0,)), ((), ()))
TN = (((0,), (0,)), ((), ()))
VMEM_LIMIT = 24 * 1024 * 1024


def mm(a, b, dims=NN):
    return lax.dot_general(a, b, dims, preferred_element_type=F32)


def same_pixel(rows):
    row = lax.broadcasted_iota(jnp.int32, (BAND, rows), 0)
    lane = lax.broadcasted_iota(jnp.int32, (BAND, rows), 1)
    return (lane & (BAND - 1)) == row


def head_lanes(head_dim, rows):
    return lax.broadcasted_iota(jnp.int32, (rows, LANES), 1) // head_dim


def stack_heads(pair, owner, per_pair, factor=None):
    pair = pair if factor is None else pair * jnp.asarray(factor, pair.dtype)
    return jnp.concatenate([jnp.where(owner == h, pair, jnp.zeros_like(pair)) for h in range(per_pair)], 0)


def pick_heads(parts, owner):
    out = parts[0]
    for h in range(1, len(parts)):
        out = jnp.where(owner == h, parts[h], out)
    return out


def stage_kernel(frames, width, bias_ref, x_ref, wq_ref, wk_ref, wv_ref, wo_ref, gain_ref,
                 rel_ref, x_out, proj_out, wo_out, gain_out, sems):
    pairs = [(x_ref, x_out), (wo_ref, wo_out), (gain_ref, gain_out)]
    pairs += [(w, proj_out.at[:, n * width:(n + 1) * width]) for n, w in enumerate((wq_ref, wk_ref, wv_ref))]
    copies = [pltpu.make_async_copy(source, target, sems.at[n]) for n, (source, target) in enumerate(pairs)]
    for copy in copies:
        copy.start()
    rows = rel_ref.shape[2]
    for i in range(frames):
        start = (frames - 1 - i) * BAND
        rel_ref[i] = bias_ref[:, start:start + rows]
    for copy in copies:
        copy.wait()


def forward_kernel(dims, me_ref, *refs):
    tm, frames, pixels, width, group, head_dim, eps = dims
    x_refs = refs[:tm]
    gain_ref, rel_ref, proj_ref, wo_ref = refs[tm:tm + 4]
    qkv_ref, p_ref, xb_ref, inv_ref, own_ref = refs[tm + 4:tm + 9]
    msg_refs = refs[tm + 9:tm + 9 + tm - 1]
    xw_ref, normed_ref, att_ref, score_ref = refs[tm + 9 + tm - 1:]
    me = me_ref[0]
    rows = frames * BAND
    bands = pixels // BAND
    per_pair = LANES // head_dim
    scale = head_dim ** -0.5

    def place(k):
        return pl.multiple_of(lax.rem(me + k, tm) * width, width)

    for k in range(tm):
        xw_ref[:, pl.ds(place(k), width)] = x_refs[k][...]
    for f in range(0, frames, 2):
        both = xw_ref[f * pixels:(f + 2) * pixels, :].astype(F32).reshape(2, bands, BAND, -1)
        for band in range(bands):
            x = both[:, band].reshape(2 * BAND, -1)
            inv = lax.rsqrt(jnp.mean(x * x, axis=-1, keepdims=True) + eps)
            at = slice(f * BAND, (f + 2) * BAND)
            normed_ref[band, at, :] = (x * inv * gain_ref[...]).astype(BF16)
            xb_ref[band, at, :] = x.astype(BF16)
            inv_ref[band, at, :] = jnp.broadcast_to(inv, (2 * BAND, LANES))
    same = same_pixel(rows)[None]
    owner = head_lanes(head_dim, rows)
    total = frames * pixels
    qkv = mm(normed_ref[...].reshape(total, -1), proj_ref[...]).astype(BF16)
    qkv_ref[...] = qkv.reshape(bands, rows, 3 * width)
    pairs = [(band, pair) for band in range(bands) for pair in range(width // LANES)]

    def cols(n, pair):
        return slice(n * width + pair * LANES, n * width + (pair + 1) * LANES)

    for band, pair in pairs:
        stacked = stack_heads(qkv_ref[band, :, cols(0, pair)], owner, per_pair, scale)
        score_ref[band, pair] = mm(stacked, qkv_ref[band, :, cols(1, pair)], NT)
    for band, pair in pairs:
        for h in range(per_pair):
            head = pair * per_pair + h
            for f in range(0, frames, CHUNK):
                at = slice(f * BAND, (f + CHUNK) * BAND)
                s = score_ref[band, pair, h * rows + f * BAND:h * rows + (f + CHUNK) * BAND, :]
                s = s.reshape(CHUNK, BAND, rows)
                s = jnp.where(same, s + rel_ref[f:f + CHUNK, head:head + 1, :], FAR)
                s = s.reshape(CHUNK * BAND, rows)
                e = jnp.exp(s - jnp.max(s, axis=-1, keepdims=True))
                p_ref[band, head, at, :] = (e * (1.0 / jnp.sum(e, axis=-1, keepdims=True))).astype(BF16)
    for band, pair in pairs:
        outs = [mm(p_ref[band, pair * per_pair + h], qkv_ref[band, :, cols(2, pair)]) for h in range(per_pair)]
        att_ref[band, :, pair * LANES:(pair + 1) * LANES] = pick_heads(outs, owner).astype(BF16)
    att = att_ref[...].reshape(total, width)
    for k in range(1, tm):
        part = mm(att, wo_ref[:, pl.ds(place(tm - k), width)]).astype(BF16)
        msg_refs[k - 1][...] = part.reshape(bands, rows, width)
    own = mm(att, wo_ref[:, pl.ds(place(0), width)]).reshape(bands, rows, width)
    own_ref[...] = own + xb_ref[:, :, pl.ds(place(0), width)].astype(F32)


def backward_kernel(dims, band, last, me_ref, *refs):
    tm, frames, pixels, width, group, head_dim, eps = dims
    g_refs = refs[:tm]
    gain_ref, qkv_ref, p_ref, xb_ref, inv_ref, proj_ref, wo_ref = refs[tm:tm + 7]
    rest = list(refs[tm + 7:])
    carried = (rest.pop(0), rest.pop(0)) if band else None
    earlier = [rest.pop(0) for _ in range(band * (tm - 1))]
    own_ref = rest.pop(0)
    msg_refs = [rest.pop(0) for _ in range(tm - 1)]
    small_ref = rest.pop(0) if last else None
    gain_out = None if last else rest.pop(0)
    diag_ref = rest.pop() if last else rest.pop(0)
    gw_ref, dp_ref, ds_ref, grad_ref = rest
    me = me_ref[0]
    rows = frames * BAND
    per_pair = LANES // head_dim
    scale = head_dim ** -0.5
    chans = width * tm

    def place(k):
        return pl.multiple_of(lax.rem(me + k, tm) * width, width)

    for k in range(tm):
        gw_ref[:, pl.ds(place(k), width)] = g_refs[k][...]
    owner = head_lanes(head_dim, rows)
    d_att = mm(gw_ref[...], wo_ref[...], NT).astype(BF16)
    pairs = range(width // LANES)

    def part(n, pair):
        return qkv_ref[band, :, n * width + pair * LANES:n * width + (pair + 1) * LANES]

    def out_rows(pair):
        return d_att[:, pair * LANES:(pair + 1) * LANES]

    for pair in pairs:
        dp_ref[pair] = mm(stack_heads(out_rows(pair), owner, per_pair), part(2, pair), NT)
    for pair in pairs:
        for h in range(per_pair):
            head = pair * per_pair + h
            for f in range(0, frames, CHUNK):
                at = slice(f * BAND, (f + CHUNK) * BAND)
                full = p_ref[band, head, at, :].astype(F32)
                t = dp_ref[pair, h * rows + f * BAND:h * rows + (f + CHUNK) * BAND, :]
                score = full * (t - jnp.sum(full * t, axis=-1, keepdims=True))
                ds_ref[head, at, :] = (score * scale).astype(BF16)
                folded = jnp.sum(score.reshape(CHUNK, BAND, rows), axis=1, keepdims=True)
                if carried is not None:
                    folded = folded + carried[1][f:f + CHUNK, head:head + 1, :]
                diag_ref[f:f + CHUNK, head:head + 1, :] = folded
    grads = [[], [], []]
    for pair in pairs:
        turned = [None, part(0, pair).T, out_rows(pair).T]
        products = [[], [], []]
        for h in range(per_pair):
            head = pair * per_pair + h
            own = slice(h * head_dim, (h + 1) * head_dim)
            products[0].append(mm(ds_ref[head], part(1, pair)))
            products[1].append(mm(turned[1][own], ds_ref[head]))
            products[2].append(mm(turned[2][own], p_ref[band, head]))
        grads[0].append(pick_heads(products[0], owner).astype(BF16))
        for n in (1, 2):
            grads[n].append(jnp.concatenate(products[n], axis=0).astype(BF16).T)
    grad_ref[...] = mm(jnp.concatenate(grads[0] + grads[1] + grads[2], axis=1), proj_ref[...], NT)
    gain_sum = jnp.zeros((BAND, chans), F32)
    for f in range(0, frames, 2):
        at = slice(f * BAND, (f + 2) * BAND)
        grad, x = grad_ref[at, :], xb_ref[band, at, :].astype(F32)
        inv = inv_ref[band, at, :1]
        scaled = x * inv
        gain_sum = gain_sum + jnp.sum((grad * scaled).reshape(2, BAND, chans), axis=0)
        term = grad * gain_ref[...]
        inner = jnp.mean(term * scaled, axis=-1, keepdims=True)
        grad_ref[at, :] = inv * (term - scaled * inner)
    for k in range(1, tm):
        share = grad_ref[:, pl.ds(place(tm - k), width)].astype(BF16)
        if last:
            for n in range(band):
                msg_refs[k - 1][n] = earlier[n * (tm - 1) + k - 1][...]
            msg_refs[k - 1][band] = share
        else:
            msg_refs[k - 1][...] = share
    own_ref[...] = grad_ref[:, pl.ds(place(0), width)] + g_refs[0][...].astype(F32)
    gain_sum = jnp.sum(gain_sum, axis=0, keepdims=True)
    if carried is not None:
        gain_sum = gain_sum + carried[0][...]
    if not last:
        gain_out[...] = gain_sum
        return
    small_ref[...] = jnp.zeros_like(small_ref)
    for r in range(chans // LANES):
        small_ref[r:r + 1, :LANES] = gain_sum[:, r * LANES:(r + 1) * LANES]
    span = small_ref.shape[1] - LANES
    bias = jnp.zeros((group, span), F32)
    for i in range(frames):
        before = (frames - 1 - i) * BAND
        bias = bias + jnp.pad(diag_ref[i], ((0, 0), (before, span - before - rows)))
    small_ref[:group, LANES:] = bias


def finish_kernel(bands, frames, own_refs, in_refs, out_ref):
    each = len(in_refs) // bands
    parts = []
    for band in range(bands):
        value = own_refs[band][...]
        for ref in in_refs[band * each:(band + 1) * each]:
            value = value + ref[...].astype(F32)
        parts.append(value.reshape(frames, 1, BAND, value.shape[-1]))
    value = jnp.concatenate(parts, axis=1)
    out_ref[...] = value.reshape(out_ref.shape).astype(out_ref.dtype)


def finish_grad_kernel(bands, frames, small_ref, *refs):
    *refs, out_ref, bias_ref = refs
    in_refs = [ref.at[band] for band in range(bands) for ref in refs[bands:]]
    finish_kernel(bands, frames, refs[:bands], in_refs, out_ref)
    group, offsets = bias_ref.shape
    value = small_ref[:, LANES:]
    high = value.astype(BF16)
    rest = value - high.astype(F32)
    middle = rest.astype(BF16)
    low = (rest - middle.astype(F32)).astype(BF16)
    span = value.shape[1]
    lane = lax.broadcasted_iota(jnp.int32, (span, LANES), 0) // BAND
    put = (lane == lax.broadcasted_iota(jnp.int32, (span, LANES), 1)).astype(F32).astype(BF16)
    total = mm(high, put) + mm(middle, put) + mm(low, put)
    bias_ref[...] = total[:group, :offsets]


def finish_out_kernel(bands, frames, own_ref, *refs):
    in_refs = [ref.at[band] for band in range(bands) for ref in refs[:-1]]
    finish_kernel(bands, frames, [own_ref.at[band] for band in range(bands)], in_refs, refs[-1])


def gain_kernel(me_ref, *refs):
    *tile_refs, out_ref, sum_ref = refs
    total = tile_refs[0][...]
    for ref in tile_refs[1:]:
        total = total + ref[...]
    sum_ref[...] = total
    count = out_ref.shape[1] // LANES
    for r in range(count):
        out_ref[:, r * LANES:(r + 1) * LANES] = sum_ref[pl.ds(me_ref[0] * count + r, 1), :]


def shifted(value, axis, step):
    count = lax.axis_size(axis)
    return lax.ppermute(value, axis, [((i + step) % count, i) for i in range(count)])


def group_sum(value, axis, beside=()):
    count = lax.axis_size(axis)
    stride = 1
    while stride < count:
        left = count // stride
        radix = 4 if left % 4 == 0 else 2 if left % 2 == 0 else left
        parts = [value]
        for step in range(1, radix):
            pairs = []
            for i in range(count):
                digit = i // stride % radix
                other = digit ^ step if radix in (2, 4) else (digit + step) % radix
                pairs.append((i + (other - digit) * stride, i))
            parts.append(lax.ppermute(value, axis, pairs))
        parts, beside = lax.optimization_barrier((parts, beside))
        value = sum(parts[1:], parts[0])
        stride *= radix
    return value, beside


def per_device(inputs, out_grad, norm_gain, pos_bias, w_query, w_key, w_value, w_out):
    clips, frames, pixels, width = inputs.shape
    group = pos_bias.shape[0]
    tm = lax.axis_size("tm")
    me = lax.axis_index("tm")
    chans = width * tm
    head_dim = width // group
    total = frames * pixels
    bands = pixels // BAND
    rows = frames * BAND
    offsets = 2 * frames - 1
    span = -(-offsets * BAND // LANES) * LANES
    lines = -(-max(chans // LANES, group) // BAND) * BAND
    dims = (tm, frames, pixels, width, group, head_dim, 1e-06)
    x0 = inputs.reshape(total, width)
    g_bands = [out_grad[:, :, n * BAND:(n + 1) * BAND].reshape(rows, width) for n in range(bands)]
    x_parts = [x0] + [shifted(x0, "tm", k) for k in range(1, tm)]
    g_parts = [[g] + [shifted(g, "tm", k) for k in range(1, tm)] for g in g_bands]
    me1 = me.astype(jnp.int32).reshape(1)
    gain = norm_gain.reshape(1, chans)
    spread = jnp.broadcast_to(pos_bias[:, :, None], (*pos_bias.shape, BAND)).reshape(group, -1)
    smem, vmem = pl.BlockSpec(memory_space=pltpu.SMEM), pl.BlockSpec(memory_space=pltpu.VMEM)
    params = pltpu.CompilerParams(vmem_limit_bytes=VMEM_LIMIT)
    held = [x0, w_query, w_key, w_value, w_out, gain]
    held = [pltpu.with_memory_space_constraint(h, pltpu.HBM) for h in held]
    rel, x0, proj, w_out, gain = pl.pallas_call(
        functools.partial(stage_kernel, frames, width),
        in_specs=[vmem] + [pl.BlockSpec(memory_space=pltpu.HBM)] * len(held),
        out_specs=[vmem] * 5,
        out_shape=[
            pltpu.VMEM((frames, group, rows), F32),
            pltpu.VMEM((total, width), BF16),
            pltpu.VMEM((chans, 3 * width), BF16),
            pltpu.VMEM((width, chans), BF16),
            pltpu.VMEM((1, chans), F32),
        ],
        scratch_shapes=[pltpu.SemaphoreType.DMA((len(held),))],
        compiler_params=params,
        cost_estimate=pl.CostEstimate(flops=0, bytes_accessed=8_000_000, transcendentals=0),
        name="stage",
    )(spread, *held)
    x_parts[0] = x0
    qkv, probs, xb, inv, mix_own, *mix_out = pl.pallas_call(
        functools.partial(forward_kernel, dims),
        in_specs=[smem] + [vmem] * (tm + 4),
        out_specs=[vmem] * (5 + tm - 1),
        out_shape=[
            pltpu.VMEM((bands, rows, 3 * width), BF16),
            pltpu.VMEM((bands, group, rows, rows), BF16),
            pltpu.VMEM((bands, rows, chans), BF16),
            pltpu.VMEM((bands, rows, LANES), F32),
            pltpu.VMEM((bands, rows, width), F32),
        ] + [pltpu.VMEM((bands, rows, width), BF16)] * (tm - 1),
        scratch_shapes=[
            pltpu.VMEM((total, chans), BF16),
            pltpu.VMEM((bands, rows, chans), BF16),
            pltpu.VMEM((bands, rows, width), BF16),
            pltpu.VMEM((bands, width // LANES, LANES // head_dim * rows, rows), F32),
        ],
        compiler_params=params,
        cost_estimate=pl.CostEstimate(flops=4_000_000_000, bytes_accessed=8_000_000, transcendentals=0),
        name="attend",
    )(me1, *x_parts, gain, rel, proj, w_out)
    mix_in = [shifted(mix_out[k - 1], "tm", k) for k in range(1, tm)]
    owns, sent, carry = [], [], []
    diag = (frames, group, rows)
    for band in range(bands):
        last = band == bands - 1
        scratch = [
            pltpu.VMEM((rows, chans), BF16),
            pltpu.VMEM((width // LANES, LANES // head_dim * rows, rows), F32),
            pltpu.VMEM((group, rows, rows), BF16),
            pltpu.VMEM((rows, chans), F32),
        ]
        if last:
            extra = [jax.ShapeDtypeStruct((lines, LANES + span), F32)]
            scratch.append(pltpu.VMEM(diag, F32))
        else:
            extra = [jax.ShapeDtypeStruct((1, chans), F32), jax.ShapeDtypeStruct(diag, F32)]
        own, *rest = pl.pallas_call(
            functools.partial(backward_kernel, dims, band, last),
            in_specs=[smem] + [vmem] * (tm + 7 + len(carry) + len(sent)),
            out_specs=[vmem] * (tm + len(extra)),
            out_shape=[pltpu.VMEM((rows, width), F32)]
            + [pltpu.VMEM((bands, rows, width) if last else (rows, width), BF16)] * (tm - 1) + extra,
            scratch_shapes=scratch,
            compiler_params=params,
            cost_estimate=pl.CostEstimate(flops=2_500_000_000, bytes_accessed=0, transcendentals=0),
            name="attend_back",
        )(me1, *g_parts[band], gain, qkv, probs, xb, inv, proj, w_out, *carry, *sent)
        sent, carry = (rest[:tm - 1] if last else sent + rest[:tm - 1]), rest[tm - 1:]
        owns.append(own)
    grad_in = [shifted(sent[k - 1], "tm", k) for k in range(1, tm)]

    result = jax.ShapeDtypeStruct((total, width), BF16)
    finish_cost = pl.CostEstimate(flops=0, bytes_accessed=1_500_000, transcendentals=0)
    small, mix_in = group_sum(carry[0], "dp", mix_in)
    block_out = pl.pallas_call(
        functools.partial(finish_out_kernel, bands, frames),
        in_specs=[vmem] * tm,
        out_specs=vmem,
        out_shape=result,
        compiler_params=params,
        cost_estimate=finish_cost,
        name="finish_out",
    )(mix_own, *mix_in)
    small, block_out = group_sum(small, "space", block_out)
    tile = small[:chans // LANES, :LANES]
    tiles = [shifted(tile, "tm", k) for k in range(1, tm)]
    input_grad, bias_grad = pl.pallas_call(
        functools.partial(finish_grad_kernel, bands, frames),
        in_specs=[vmem] * (bands + tm),
        out_specs=[vmem] * 2,
        out_shape=[result, jax.ShapeDtypeStruct((group, offsets), F32)],
        compiler_params=params,
        cost_estimate=finish_cost,
        name="finish_grad",
    )(small, *owns, *grad_in)
    tiles, input_grad = lax.optimization_barrier((tiles, input_grad))
    gain_grad = pl.pallas_call(
        gain_kernel,
        in_specs=[smem] + [vmem] * tm,
        out_specs=vmem,
        out_shape=jax.ShapeDtypeStruct((1, width), F32),
        scratch_shapes=[pltpu.VMEM(tile.shape, F32)],
        compiler_params=params,
        name="gain_sum",
    )(me1, tile, *tiles)
    return (block_out.reshape(inputs.shape), input_grad.reshape(inputs.shape), gain_grad.reshape(width), bias_grad)


def solution(mesh):
    return jax.shard_map(
        per_device,
        mesh=mesh,
        in_specs=(
            P("dp", None, "space", "tm"),
            P("dp", None, "space", "tm"),
            P(),
            P("tm", None),
            P(None, "tm"),
            P(None, "tm"),
            P(None, "tm"),
            P("tm", None),
        ),
        out_specs=(
            P("dp", None, "space", "tm"),
            P("dp", None, "space", "tm"),
            P("tm"),
            P("tm", None),
        ),
        check_vma=False,
    )
```

```python
import functools

import jax
import jax.numpy as jnp
from jax import lax
from jax.experimental import pallas as pl
from jax.experimental.pallas import tpu as pltpu
from jax.sharding import PartitionSpec as P

CHUNK = 4
BAND = 8
LANES = 128
FAR = -1e30
F32, BF16 = jnp.float32, jnp.bfloat16
NT = (((1,), (1,)), ((), ()))
NN = (((1,), (0,)), ((), ()))
TN = (((0,), (0,)), ((), ()))
VMEM_LIMIT = 24 * 1024 * 1024


def mm(a, b, dims=NN):
    return lax.dot_general(a, b, dims, preferred_element_type=F32)


def same_pixel(rows):
    row = lax.broadcasted_iota(jnp.int32, (BAND, rows), 0)
    lane = lax.broadcasted_iota(jnp.int32, (BAND, rows), 1)
    return (lane & (BAND - 1)) == row


def head_lanes(head_dim, rows):
    return lax.broadcasted_iota(jnp.int32, (rows, LANES), 1) // head_dim


def stack_heads(pair, owner, per_pair, factor=None):
    pair = pair if factor is None else pair * jnp.asarray(factor, pair.dtype)
    return jnp.concatenate([jnp.where(owner == h, pair, jnp.zeros_like(pair)) for h in range(per_pair)], 0)


def pick_heads(parts, owner):
    out = parts[0]
    for h in range(1, len(parts)):
        out = jnp.where(owner == h, parts[h], out)
    return out


def stage_kernel(frames, width, bias_ref, x_ref, wq_ref, wk_ref, wv_ref, wo_ref, gain_ref,
                 rel_ref, x_out, proj_out, wo_out, gain_out, proj_turned, wo_turned, sems):
    pairs = [(x_ref, x_out), (wo_ref, wo_out), (gain_ref, gain_out)]
    pairs += [(w, proj_out.at[:, n * width:(n + 1) * width]) for n, w in enumerate((wq_ref, wk_ref, wv_ref))]
    copies = [pltpu.make_async_copy(source, target, sems.at[n]) for n, (source, target) in enumerate(pairs)]
    for copy in copies:
        copy.start()
    rows = rel_ref.shape[2]
    for i in range(frames):
        start = (frames - 1 - i) * BAND
        rel_ref[i] = bias_ref[:, start:start + rows]
    for copy in copies:
        copy.wait()
    for source, target in ((proj_out, proj_turned), (wo_out, wo_turned)):
        for start in range(0, source.shape[1], 2 * LANES):
            target[start:start + 2 * LANES, :] = source[:, start:start + 2 * LANES].T


def forward_kernel(dims, me_ref, *refs):
    tm, frames, pixels, width, group, head_dim, eps = dims
    x_refs = refs[:tm]
    gain_ref, rel_ref, proj_ref, wo_ref = refs[tm:tm + 4]
    qkv_ref, p_ref, xb_ref, inv_ref, own_ref = refs[tm + 4:tm + 9]
    msg_refs = refs[tm + 9:tm + 9 + tm - 1]
    xw_ref, normed_ref, att_ref, score_ref = refs[tm + 9 + tm - 1:]
    me = me_ref[0]
    rows = frames * BAND
    bands = pixels // BAND
    per_pair = LANES // head_dim
    scale = head_dim ** -0.5

    def place(k):
        return pl.multiple_of(lax.rem(me + k, tm) * width, width)

    for k in range(tm):
        xw_ref[:, pl.ds(place(k), width)] = x_refs[k][...]
    for f in range(0, frames, 2):
        both = xw_ref[f * pixels:(f + 2) * pixels, :].astype(F32).reshape(2, bands, BAND, -1)
        for band in range(bands):
            x = both[:, band].reshape(2 * BAND, -1)
            inv = lax.rsqrt(jnp.mean(x * x, axis=-1, keepdims=True) + eps)
            at = slice(f * BAND, (f + 2) * BAND)
            normed_ref[band, at, :] = (x * inv * gain_ref[...]).astype(BF16)
            xb_ref[band, at, :] = x.astype(BF16)
            inv_ref[band, at, :] = jnp.broadcast_to(inv, (2 * BAND, LANES))
    same = same_pixel(rows)[None]
    owner = head_lanes(head_dim, rows)
    total = frames * pixels
    qkv = mm(normed_ref[...].reshape(total, -1), proj_ref[...]).astype(BF16)
    qkv_ref[...] = qkv.reshape(bands, rows, 3 * width)
    pairs = [(band, pair) for band in range(bands) for pair in range(width // LANES)]

    def cols(n, pair):
        return slice(n * width + pair * LANES, n * width + (pair + 1) * LANES)

    for band, pair in pairs:
        stacked = stack_heads(qkv_ref[band, :, cols(0, pair)], owner, per_pair, scale)
        score_ref[band, pair] = mm(stacked, qkv_ref[band, :, cols(1, pair)], NT)
    for band, pair in pairs:
        for h in range(per_pair):
            head = pair * per_pair + h
            for f in range(0, frames, CHUNK):
                at = slice(f * BAND, (f + CHUNK) * BAND)
                s = score_ref[band, pair, h * rows + f * BAND:h * rows + (f + CHUNK) * BAND, :]
                s = s.reshape(CHUNK, BAND, rows)
                s = jnp.where(same, s + rel_ref[f:f + CHUNK, head:head + 1, :], FAR)
                s = s.reshape(CHUNK * BAND, rows)
                e = jnp.exp(s - jnp.max(s, axis=-1, keepdims=True))
                p_ref[band, head, at, :] = (e * (1.0 / jnp.sum(e, axis=-1, keepdims=True))).astype(BF16)
    for band, pair in pairs:
        outs = [mm(p_ref[band, pair * per_pair + h], qkv_ref[band, :, cols(2, pair)]) for h in range(per_pair)]
        att_ref[band, :, pair * LANES:(pair + 1) * LANES] = pick_heads(outs, owner).astype(BF16)
    att = att_ref[...].reshape(total, width)
    for k in range(1, tm):
        part = mm(att, wo_ref[:, pl.ds(place(tm - k), width)]).astype(BF16)
        msg_refs[k - 1][...] = part.reshape(bands, rows, width)
    own = mm(att, wo_ref[:, pl.ds(place(0), width)]).reshape(bands, rows, width)
    own_ref[...] = own + xb_ref[:, :, pl.ds(place(0), width)].astype(F32)


def backward_kernel(dims, band, last, me_ref, *refs):
    tm, frames, pixels, width, group, head_dim, eps = dims
    g_refs = refs[:tm]
    gain_ref, qkv_ref, p_ref, xb_ref, inv_ref, proj_ref, wo_ref = refs[tm:tm + 7]
    rest = list(refs[tm + 7:])
    carried = (rest.pop(0), rest.pop(0)) if band else None
    earlier = [rest.pop(0) for _ in range(band * (tm - 1))]
    own_ref = rest.pop(0)
    msg_refs = [rest.pop(0) for _ in range(tm - 1)]
    small_ref = rest.pop(0) if last else None
    gain_out = None if last else rest.pop(0)
    diag_ref = rest.pop() if last else rest.pop(0)
    gw_ref, dp_ref, ds_ref, grad_ref = rest
    me = me_ref[0]
    rows = frames * BAND
    per_pair = LANES // head_dim
    scale = head_dim ** -0.5
    chans = width * tm

    def place(k):
        return pl.multiple_of(lax.rem(me + k, tm) * width, width)

    for k in range(tm):
        gw_ref[:, pl.ds(place(k), width)] = g_refs[k][...]
    owner = head_lanes(head_dim, rows)
    d_att = mm(gw_ref[...], wo_ref[...]).astype(BF16)
    pairs = range(width // LANES)

    def part(n, pair):
        return qkv_ref[band, :, n * width + pair * LANES:n * width + (pair + 1) * LANES]

    def out_rows(pair):
        return d_att[:, pair * LANES:(pair + 1) * LANES]

    for pair in pairs:
        dp_ref[pair] = mm(stack_heads(out_rows(pair), owner, per_pair), part(2, pair), NT)
    for pair in pairs:
        for h in range(per_pair):
            head = pair * per_pair + h
            for f in range(0, frames, CHUNK):
                at = slice(f * BAND, (f + CHUNK) * BAND)
                full = p_ref[band, head, at, :].astype(F32)
                t = dp_ref[pair, h * rows + f * BAND:h * rows + (f + CHUNK) * BAND, :]
                score = full * (t - jnp.sum(full * t, axis=-1, keepdims=True))
                ds_ref[head, at, :] = (score * scale).astype(BF16)
                folded = jnp.sum(score.reshape(CHUNK, BAND, rows), axis=1, keepdims=True)
                if carried is not None:
                    folded = folded + carried[1][f:f + CHUNK, head:head + 1, :]
                diag_ref[f:f + CHUNK, head:head + 1, :] = folded
    grads = [[], [], []]
    for pair in pairs:
        turned = [None, part(0, pair).T, out_rows(pair).T]
        products = [[], [], []]
        for h in range(per_pair):
            head = pair * per_pair + h
            own = slice(h * head_dim, (h + 1) * head_dim)
            products[0].append(mm(ds_ref[head], part(1, pair)))
            products[1].append(mm(turned[1][own], ds_ref[head]))
            products[2].append(mm(turned[2][own], p_ref[band, head]))
        grads[0].append(pick_heads(products[0], owner).astype(BF16))
        for n in (1, 2):
            grads[n].append(jnp.concatenate(products[n], axis=0).astype(BF16).T)
    grad_ref[...] = mm(jnp.concatenate(grads[0] + grads[1] + grads[2], axis=1), proj_ref[...])
    gain_sum = jnp.zeros((BAND, chans), F32)
    for f in range(0, frames, 2):
        at = slice(f * BAND, (f + 2) * BAND)
        grad, x = grad_ref[at, :], xb_ref[band, at, :].astype(F32)
        inv = inv_ref[band, at, :1]
        scaled = x * inv
        gain_sum = gain_sum + jnp.sum((grad * scaled).reshape(2, BAND, chans), axis=0)
        term = grad * gain_ref[...]
        inner = jnp.mean(term * scaled, axis=-1, keepdims=True)
        grad_ref[at, :] = inv * (term - scaled * inner)
    for k in range(1, tm):
        share = grad_ref[:, pl.ds(place(tm - k), width)].astype(BF16)
        if last:
            for n in range(band):
                msg_refs[k - 1][n] = earlier[n * (tm - 1) + k - 1][...]
            msg_refs[k - 1][band] = share
        else:
            msg_refs[k - 1][...] = share
    own_ref[...] = grad_ref[:, pl.ds(place(0), width)] + g_refs[0][...].astype(F32)
    gain_sum = jnp.sum(gain_sum, axis=0, keepdims=True)
    if carried is not None:
        gain_sum = gain_sum + carried[0][...]
    if not last:
        gain_out[...] = gain_sum
        return
    small_ref[...] = jnp.zeros_like(small_ref)
    for r in range(chans // LANES):
        small_ref[r:r + 1, :LANES] = gain_sum[:, r * LANES:(r + 1) * LANES]
    span = small_ref.shape[1] - LANES
    bias = jnp.zeros((group, span), F32)
    for i in range(frames):
        before = (frames - 1 - i) * BAND
        bias = bias + jnp.pad(diag_ref[i], ((0, 0), (before, span - before - rows)))
    small_ref[:group, LANES:] = bias


def finish_kernel(bands, frames, own_refs, in_refs, out_ref):
    each = len(in_refs) // bands
    parts = []
    for band in range(bands):
        value = own_refs[band][...]
        for ref in in_refs[band * each:(band + 1) * each]:
            value = value + ref[...].astype(F32)
        parts.append(value.reshape(frames, 1, BAND, value.shape[-1]))
    value = jnp.concatenate(parts, axis=1)
    out_ref[...] = value.reshape(out_ref.shape).astype(out_ref.dtype)


def finish_grad_kernel(bands, frames, small_ref, *refs):
    *refs, out_ref, bias_ref = refs
    in_refs = [ref.at[band] for band in range(bands) for ref in refs[bands:]]
    finish_kernel(bands, frames, refs[:bands], in_refs, out_ref)
    group, offsets = bias_ref.shape
    value = small_ref[:, LANES:]
    high = value.astype(BF16)
    rest = value - high.astype(F32)
    middle = rest.astype(BF16)
    low = (rest - middle.astype(F32)).astype(BF16)
    span = value.shape[1]
    lane = lax.broadcasted_iota(jnp.int32, (span, LANES), 0) // BAND
    put = (lane == lax.broadcasted_iota(jnp.int32, (span, LANES), 1)).astype(F32).astype(BF16)
    total = mm(high, put) + mm(middle, put) + mm(low, put)
    bias_ref[...] = total[:group, :offsets]


def finish_out_kernel(bands, frames, own_ref, *refs):
    in_refs = [ref.at[band] for band in range(bands) for ref in refs[:-1]]
    finish_kernel(bands, frames, [own_ref.at[band] for band in range(bands)], in_refs, refs[-1])


def gain_kernel(me_ref, *refs):
    *tile_refs, out_ref, sum_ref = refs
    total = tile_refs[0][...]
    for ref in tile_refs[1:]:
        total = total + ref[...]
    sum_ref[...] = total
    count = out_ref.shape[1] // LANES
    for r in range(count):
        out_ref[:, r * LANES:(r + 1) * LANES] = sum_ref[pl.ds(me_ref[0] * count + r, 1), :]


def shifted(value, axis, step):
    count = lax.axis_size(axis)
    return lax.ppermute(value, axis, [((i + step) % count, i) for i in range(count)])


def group_sum(value, axis, beside=()):
    count = lax.axis_size(axis)
    stride = 1
    while stride < count:
        left = count // stride
        radix = 4 if left % 4 == 0 else 2 if left % 2 == 0 else left
        parts = [value]
        for step in range(1, radix):
            pairs = []
            for i in range(count):
                digit = i // stride % radix
                other = digit ^ step if radix in (2, 4) else (digit + step) % radix
                pairs.append((i + (other - digit) * stride, i))
            parts.append(lax.ppermute(value, axis, pairs))
        stride *= radix
        if stride == count:
            parts, beside = lax.optimization_barrier((parts, beside))
        value = sum(parts[1:], parts[0])
    return value, beside


def per_device(inputs, out_grad, norm_gain, pos_bias, w_query, w_key, w_value, w_out):
    clips, frames, pixels, width = inputs.shape
    group = pos_bias.shape[0]
    tm = lax.axis_size("tm")
    me = lax.axis_index("tm")
    chans = width * tm
    head_dim = width // group
    total = frames * pixels
    bands = pixels // BAND
    rows = frames * BAND
    offsets = 2 * frames - 1
    span = -(-offsets * BAND // LANES) * LANES
    lines = -(-max(chans // LANES, group) // BAND) * BAND
    dims = (tm, frames, pixels, width, group, head_dim, 1e-06)
    x0 = inputs.reshape(total, width)
    g_bands = [out_grad[:, :, n * BAND:(n + 1) * BAND].reshape(rows, width) for n in range(bands)]
    x_parts = [x0] + [shifted(x0, "tm", k) for k in range(1, tm)]
    g_parts = [[g] + [shifted(g, "tm", k) for k in range(1, tm)] for g in g_bands]
    me1 = me.astype(jnp.int32).reshape(1)
    gain = norm_gain.reshape(1, chans)
    spread = jnp.broadcast_to(pos_bias[:, :, None], (*pos_bias.shape, BAND)).reshape(group, -1)
    smem, vmem = pl.BlockSpec(memory_space=pltpu.SMEM), pl.BlockSpec(memory_space=pltpu.VMEM)
    params = pltpu.CompilerParams(vmem_limit_bytes=VMEM_LIMIT)
    held = [x0, w_query, w_key, w_value, w_out, gain]
    held = [pltpu.with_memory_space_constraint(h, pltpu.HBM) for h in held]
    rel, x0, proj, w_out, gain, proj_turned, out_turned = pl.pallas_call(
        functools.partial(stage_kernel, frames, width),
        in_specs=[vmem] + [pl.BlockSpec(memory_space=pltpu.HBM)] * len(held),
        out_specs=[vmem] * 7,
        out_shape=[
            pltpu.VMEM((frames, group, rows), F32),
            pltpu.VMEM((total, width), BF16),
            pltpu.VMEM((chans, 3 * width), BF16),
            pltpu.VMEM((width, chans), BF16),
            pltpu.VMEM((1, chans), F32),
            pltpu.VMEM((3 * width, chans), BF16),
            pltpu.VMEM((chans, width), BF16),
        ],
        scratch_shapes=[pltpu.SemaphoreType.DMA((len(held),))],
        compiler_params=params,
        cost_estimate=pl.CostEstimate(flops=0, bytes_accessed=8_000_000, transcendentals=0),
        name="stage",
    )(spread, *held)
    x_parts[0] = x0
    qkv, probs, xb, inv, mix_own, *mix_out = pl.pallas_call(
        functools.partial(forward_kernel, dims),
        in_specs=[smem] + [vmem] * (tm + 4),
        out_specs=[vmem] * (5 + tm - 1),
        out_shape=[
            pltpu.VMEM((bands, rows, 3 * width), BF16),
            pltpu.VMEM((bands, group, rows, rows), BF16),
            pltpu.VMEM((bands, rows, chans), BF16),
            pltpu.VMEM((bands, rows, LANES), F32),
            pltpu.VMEM((bands, rows, width), F32),
        ] + [pltpu.VMEM((bands, rows, width), BF16)] * (tm - 1),
        scratch_shapes=[
            pltpu.VMEM((total, chans), BF16),
            pltpu.VMEM((bands, rows, chans), BF16),
            pltpu.VMEM((bands, rows, width), BF16),
            pltpu.VMEM((bands, width // LANES, LANES // head_dim * rows, rows), F32),
        ],
        compiler_params=params,
        cost_estimate=pl.CostEstimate(flops=4_000_000_000, bytes_accessed=8_000_000, transcendentals=0),
        name="attend",
    )(me1, *x_parts, gain, rel, proj, w_out)
    mix_in = [shifted(mix_out[k - 1], "tm", k) for k in range(1, tm)]
    owns, sent, carry = [], [], []
    diag = (frames, group, rows)
    for band in range(bands):
        last = band == bands - 1
        scratch = [
            pltpu.VMEM((rows, chans), BF16),
            pltpu.VMEM((width // LANES, LANES // head_dim * rows, rows), F32),
            pltpu.VMEM((group, rows, rows), BF16),
            pltpu.VMEM((rows, chans), F32),
        ]
        if last:
            extra = [jax.ShapeDtypeStruct((lines, LANES + span), F32)]
            scratch.append(pltpu.VMEM(diag, F32))
        else:
            extra = [jax.ShapeDtypeStruct((1, chans), F32), jax.ShapeDtypeStruct(diag, F32)]
        own, *rest = pl.pallas_call(
            functools.partial(backward_kernel, dims, band, last),
            in_specs=[smem] + [vmem] * (tm + 7 + len(carry) + len(sent)),
            out_specs=[vmem] * (tm + len(extra)),
            out_shape=[pltpu.VMEM((rows, width), F32)]
            + [pltpu.VMEM((bands, rows, width) if last else (rows, width), BF16)] * (tm - 1) + extra,
            scratch_shapes=scratch,
            compiler_params=params,
            cost_estimate=pl.CostEstimate(flops=2_500_000_000, bytes_accessed=0, transcendentals=0),
            name="attend_back",
        )(me1, *g_parts[band], gain, qkv, probs, xb, inv, proj_turned, out_turned, *carry, *sent)
        sent, carry = (rest[:tm - 1] if last else sent + rest[:tm - 1]), rest[tm - 1:]
        owns.append(own)

    result = jax.ShapeDtypeStruct((total, width), BF16)
    finish_cost = pl.CostEstimate(flops=0, bytes_accessed=1_500_000, transcendentals=0)
    small, mix_in = group_sum(carry[0], "dp", mix_in)
    grad_in = [shifted(sent[k - 1], "tm", k) for k in range(1, tm)]
    block_out = pl.pallas_call(
        functools.partial(finish_out_kernel, bands, frames),
        in_specs=[vmem] * tm,
        out_specs=vmem,
        out_shape=result,
        compiler_params=params,
        cost_estimate=finish_cost,
        name="finish_out",
    )(mix_own, *mix_in)
    small, block_out = group_sum(small, "space", block_out)

    tile = small[:chans // LANES, :LANES]
    tiles = [shifted(tile, "tm", k) for k in range(1, tm)]
    input_grad, bias_grad = pl.pallas_call(
        functools.partial(finish_grad_kernel, bands, frames),
        in_specs=[vmem] * (bands + tm),
        out_specs=[vmem] * 2,
        out_shape=[result, jax.ShapeDtypeStruct((group, offsets), F32)],
        compiler_params=params,
        cost_estimate=finish_cost,
        name="finish_grad",
    )(small, *owns, *grad_in)
    tiles, input_grad = lax.optimization_barrier((tiles, input_grad))
    gain_grad = pl.pallas_call(
        gain_kernel,
        in_specs=[smem] + [vmem] * tm,
        out_specs=vmem,
        out_shape=jax.ShapeDtypeStruct((1, width), F32),
        scratch_shapes=[pltpu.VMEM(tile.shape, F32)],
        compiler_params=params,
        name="gain_sum",
    )(me1, tile, *tiles)
    return (block_out.reshape(inputs.shape), input_grad.reshape(inputs.shape), gain_grad.reshape(width), bias_grad)


def solution(mesh):
    return jax.shard_map(
        per_device,
        mesh=mesh,
        in_specs=(
            P("dp", None, "space", "tm"),
            P("dp", None, "space", "tm"),
            P(),
            P("tm", None),
            P(None, "tm"),
            P(None, "tm"),
            P(None, "tm"),
            P("tm", None),
        ),
        out_specs=(
            P("dp", None, "space", "tm"),
            P("dp", None, "space", "tm"),
            P("tm"),
            P("tm", None),
        ),
        check_vma=False,
    )
```

```python
import functools

import jax
import jax.numpy as jnp
from jax import lax
from jax.experimental import pallas as pl
from jax.experimental.pallas import tpu as pltpu
from jax.sharding import PartitionSpec as P

CHUNK = 4
BAND = 8
LANES = 128
FAR = -1e30
F32, BF16 = jnp.float32, jnp.bfloat16
NT = (((1,), (1,)), ((), ()))
NN = (((1,), (0,)), ((), ()))
TN = (((0,), (0,)), ((), ()))
VMEM_LIMIT = 24 * 1024 * 1024


def mm(a, b, dims=NN):
    return lax.dot_general(a, b, dims, preferred_element_type=F32)


def same_pixel(rows):
    row = lax.broadcasted_iota(jnp.int32, (BAND, rows), 0)
    lane = lax.broadcasted_iota(jnp.int32, (BAND, rows), 1)
    return (lane & (BAND - 1)) == row


def head_lanes(head_dim, rows):
    return lax.broadcasted_iota(jnp.int32, (rows, LANES), 1) // head_dim


def stack_heads(pair, owner, per_pair, factor=None):
    pair = pair if factor is None else pair * jnp.asarray(factor, pair.dtype)
    return jnp.concatenate([jnp.where(owner == h, pair, jnp.zeros_like(pair)) for h in range(per_pair)], 0)


def pick_heads(parts, owner):
    out = parts[0]
    for h in range(1, len(parts)):
        out = jnp.where(owner == h, parts[h], out)
    return out


def stage_kernel(frames, width, bias_ref, x_ref, wq_ref, wk_ref, wv_ref, wo_ref, gain_ref,
                 rel_ref, x_out, proj_out, wo_out, gain_out, proj_turned, wo_turned, sems):
    pairs = [(x_ref, x_out), (wo_ref, wo_out), (gain_ref, gain_out)]
    pairs += [(w, proj_out.at[:, n * width:(n + 1) * width]) for n, w in enumerate((wq_ref, wk_ref, wv_ref))]
    copies = [pltpu.make_async_copy(source, target, sems.at[n]) for n, (source, target) in enumerate(pairs)]
    for copy in copies:
        copy.start()
    rows = rel_ref.shape[2]
    for i in range(frames):
        start = (frames - 1 - i) * BAND
        rel_ref[i] = bias_ref[:, start:start + rows]
    for copy in copies:
        copy.wait()
    for source, target in ((proj_out, proj_turned), (wo_out, wo_turned)):
        for start in range(0, source.shape[1], 2 * LANES):
            target[start:start + 2 * LANES, :] = source[:, start:start + 2 * LANES].T


def forward_kernel(dims, me_ref, *refs):
    tm, frames, pixels, width, group, head_dim, eps = dims
    x_refs = refs[:tm]
    gain_ref, rel_ref, proj_ref, wo_ref = refs[tm:tm + 4]
    qkv_ref, p_ref, xb_ref, inv_ref, own_ref = refs[tm + 4:tm + 9]
    msg_refs = refs[tm + 9:tm + 9 + tm - 1]
    xw_ref, normed_ref, att_ref, score_ref = refs[tm + 9 + tm - 1:]
    me = me_ref[0]
    rows = frames * BAND
    bands = pixels // BAND
    per_pair = LANES // head_dim
    scale = head_dim ** -0.5

    def place(k):
        return pl.multiple_of(lax.rem(me + k, tm) * width, width)

    for k in range(tm):
        xw_ref[:, pl.ds(place(k), width)] = x_refs[k][...]
    for f in range(0, frames, 2):
        both = xw_ref[f * pixels:(f + 2) * pixels, :].astype(F32).reshape(2, bands, BAND, -1)
        for band in range(bands):
            x = both[:, band].reshape(2 * BAND, -1)
            inv = lax.rsqrt(jnp.mean(x * x, axis=-1, keepdims=True) + eps)
            at = slice(f * BAND, (f + 2) * BAND)
            normed_ref[band, at, :] = (x * inv * gain_ref[...]).astype(BF16)
            xb_ref[band, at, :] = x.astype(BF16)
            inv_ref[band, at, :] = jnp.broadcast_to(inv, (2 * BAND, LANES))
    same = same_pixel(rows)[None]
    owner = head_lanes(head_dim, rows)
    total = frames * pixels
    qkv = mm(normed_ref[...].reshape(total, -1), proj_ref[...]).astype(BF16)
    qkv_ref[...] = qkv.reshape(bands, rows, 3 * width)
    pairs = [(band, pair) for band in range(bands) for pair in range(width // LANES)]

    def cols(n, pair):
        return slice(n * width + pair * LANES, n * width + (pair + 1) * LANES)

    for band, pair in pairs:
        stacked = stack_heads(qkv_ref[band, :, cols(0, pair)], owner, per_pair, scale)
        score_ref[band, pair] = mm(stacked, qkv_ref[band, :, cols(1, pair)], NT)
    for band, pair in pairs:
        for h in range(per_pair):
            head = pair * per_pair + h
            for f in range(0, frames, CHUNK):
                at = slice(f * BAND, (f + CHUNK) * BAND)
                s = score_ref[band, pair, h * rows + f * BAND:h * rows + (f + CHUNK) * BAND, :]
                s = s.reshape(CHUNK, BAND, rows)
                s = jnp.where(same, s + rel_ref[f:f + CHUNK, head:head + 1, :], FAR)
                s = s.reshape(CHUNK * BAND, rows)
                e = jnp.exp(s - jnp.max(s, axis=-1, keepdims=True))
                p_ref[band, head, at, :] = (e * (1.0 / jnp.sum(e, axis=-1, keepdims=True))).astype(BF16)
    for band, pair in pairs:
        outs = [mm(p_ref[band, pair * per_pair + h], qkv_ref[band, :, cols(2, pair)]) for h in range(per_pair)]
        att_ref[band, :, pair * LANES:(pair + 1) * LANES] = pick_heads(outs, owner).astype(BF16)
    att = att_ref[...].reshape(total, width)
    for k in range(1, tm):
        part = mm(att, wo_ref[:, pl.ds(place(tm - k), width)]).astype(BF16)
        msg_refs[k - 1][...] = part.reshape(bands, rows, width)
    own = mm(att, wo_ref[:, pl.ds(place(0), width)]).reshape(bands, rows, width)
    own_ref[...] = own + xb_ref[:, :, pl.ds(place(0), width)].astype(F32)


def backward_kernel(dims, band, last, me_ref, *refs):
    tm, frames, pixels, width, group, head_dim, eps = dims
    g_refs = refs[:tm]
    gain_ref, qkv_ref, p_ref, xb_ref, inv_ref, proj_ref, wo_ref = refs[tm:tm + 7]
    rest = list(refs[tm + 7:])
    carried = (rest.pop(0), rest.pop(0)) if band else None
    earlier = [rest.pop(0) for _ in range(band * (tm - 1))]
    own_ref = rest.pop(0)
    msg_refs = [rest.pop(0) for _ in range(tm - 1)]
    small_ref = rest.pop(0) if last else None
    gain_out = None if last else rest.pop(0)
    diag_ref = rest.pop() if last else rest.pop(0)
    gw_ref, dp_ref, ds_ref, grad_ref = rest
    me = me_ref[0]
    rows = frames * BAND
    per_pair = LANES // head_dim
    scale = head_dim ** -0.5
    chans = width * tm

    def place(k):
        return pl.multiple_of(lax.rem(me + k, tm) * width, width)

    for k in range(tm):
        gw_ref[:, pl.ds(place(k), width)] = g_refs[k][...]
    owner = head_lanes(head_dim, rows)
    d_att = mm(gw_ref[...], wo_ref[...]).astype(BF16)
    pairs = range(width // LANES)

    def part(n, pair):
        return qkv_ref[band, :, n * width + pair * LANES:n * width + (pair + 1) * LANES]

    def out_rows(pair):
        return d_att[:, pair * LANES:(pair + 1) * LANES]

    for pair in pairs:
        dp_ref[pair] = mm(stack_heads(out_rows(pair), owner, per_pair), part(2, pair), NT)
    for pair in pairs:
        for h in range(per_pair):
            head = pair * per_pair + h
            for f in range(0, frames, CHUNK):
                at = slice(f * BAND, (f + CHUNK) * BAND)
                full = p_ref[band, head, at, :].astype(F32)
                t = dp_ref[pair, h * rows + f * BAND:h * rows + (f + CHUNK) * BAND, :]
                score = full * (t - jnp.sum(full * t, axis=-1, keepdims=True))
                ds_ref[head, at, :] = (score * scale).astype(BF16)
                folded = jnp.sum(score.reshape(CHUNK, BAND, rows), axis=1, keepdims=True)
                if carried is not None:
                    folded = folded + carried[1][f:f + CHUNK, head:head + 1, :]
                diag_ref[f:f + CHUNK, head:head + 1, :] = folded
    grads = [[], [], []]
    for pair in pairs:
        turned = [None, part(0, pair).T, out_rows(pair).T]
        products = [[], [], []]
        for h in range(per_pair):
            head = pair * per_pair + h
            own = slice(h * head_dim, (h + 1) * head_dim)
            products[0].append(mm(ds_ref[head], part(1, pair)))
            products[1].append(mm(turned[1][own], ds_ref[head]))
            products[2].append(mm(turned[2][own], p_ref[band, head]))
        grads[0].append(pick_heads(products[0], owner).astype(BF16))
        for n in (1, 2):
            grads[n].append(jnp.concatenate(products[n], axis=0).astype(BF16).T)
    grad_ref[...] = mm(jnp.concatenate(grads[0] + grads[1] + grads[2], axis=1), proj_ref[...])
    gain_sum = jnp.zeros((BAND, chans), F32)
    for f in range(0, frames, 2):
        at = slice(f * BAND, (f + 2) * BAND)
        grad, x = grad_ref[at, :], xb_ref[band, at, :].astype(F32)
        inv = inv_ref[band, at, :1]
        scaled = x * inv
        gain_sum = gain_sum + jnp.sum((grad * scaled).reshape(2, BAND, chans), axis=0)
        term = grad * gain_ref[...]
        inner = jnp.mean(term * scaled, axis=-1, keepdims=True)
        grad_ref[at, :] = inv * (term - scaled * inner)
    for k in range(1, tm):
        share = grad_ref[:, pl.ds(place(tm - k), width)].astype(BF16)
        if last:
            for n in range(band):
                msg_refs[k - 1][n] = earlier[n * (tm - 1) + k - 1][...]
            msg_refs[k - 1][band] = share
        else:
            msg_refs[k - 1][...] = share
    own_ref[...] = grad_ref[:, pl.ds(place(0), width)] + g_refs[0][...].astype(F32)
    gain_sum = jnp.sum(gain_sum, axis=0, keepdims=True)
    if carried is not None:
        gain_sum = gain_sum + carried[0][...]
    if not last:
        gain_out[...] = gain_sum
        return
    small_ref[...] = jnp.zeros_like(small_ref)
    for r in range(chans // LANES):
        small_ref[r:r + 1, :LANES] = gain_sum[:, r * LANES:(r + 1) * LANES]
    span = small_ref.shape[1] - LANES
    bias = jnp.zeros((group, span), F32)
    for i in range(frames):
        before = (frames - 1 - i) * BAND
        bias = bias + jnp.pad(diag_ref[i], ((0, 0), (before, span - before - rows)))
    small_ref[:group, LANES:] = bias


def finish_kernel(bands, frames, own_refs, in_refs, out_ref):
    each = len(in_refs) // bands
    parts = []
    for band in range(bands):
        value = own_refs[band][...]
        for ref in in_refs[band * each:(band + 1) * each]:
            value = value + ref[...].astype(F32)
        parts.append(value.reshape(frames, 1, BAND, value.shape[-1]))
    value = jnp.concatenate(parts, axis=1)
    out_ref[...] = value.reshape(out_ref.shape).astype(out_ref.dtype)


def finish_grad_kernel(bands, frames, small_ref, *refs):
    *refs, out_ref, bias_ref = refs
    in_refs = [ref.at[band] for band in range(bands) for ref in refs[bands:]]
    finish_kernel(bands, frames, refs[:bands], in_refs, out_ref)
    group, offsets = bias_ref.shape
    value = small_ref[:, LANES:]
    high = value.astype(BF16)
    rest = value - high.astype(F32)
    middle = rest.astype(BF16)
    low = (rest - middle.astype(F32)).astype(BF16)
    span = value.shape[1]
    lane = lax.broadcasted_iota(jnp.int32, (span, LANES), 0) // BAND
    put = (lane == lax.broadcasted_iota(jnp.int32, (span, LANES), 1)).astype(F32).astype(BF16)
    total = mm(high, put) + mm(middle, put) + mm(low, put)
    bias_ref[...] = total[:group, :offsets]


def finish_out_kernel(bands, frames, own_ref, *refs):
    in_refs = [ref.at[band] for band in range(bands) for ref in refs[:-1]]
    finish_kernel(bands, frames, [own_ref.at[band] for band in range(bands)], in_refs, refs[-1])


def gain_kernel(me_ref, *refs):
    *tile_refs, out_ref, sum_ref = refs
    total = tile_refs[0][...]
    for ref in tile_refs[1:]:
        total = total + ref[...]
    sum_ref[...] = total
    count = out_ref.shape[1] // LANES
    for r in range(count):
        out_ref[:, r * LANES:(r + 1) * LANES] = sum_ref[pl.ds(me_ref[0] * count + r, 1), :]


def shifted(value, axis, step):
    count = lax.axis_size(axis)
    return lax.ppermute(value, axis, [((i + step) % count, i) for i in range(count)])


def group_sum(value, axis, beside=()):
    count = lax.axis_size(axis)
    stride = 1
    while stride < count:
        left = count // stride
        radix = 4 if left % 4 == 0 else 2 if left % 2 == 0 else left
        parts = [value]
        for step in reversed(range(1, radix)):
            pairs = []
            for i in range(count):
                digit = i // stride % radix
                other = digit ^ step if radix in (2, 4) else (digit + step) % radix
                pairs.append((i + (other - digit) * stride, i))
            parts.append(lax.ppermute(value, axis, pairs))
        stride *= radix
        if stride == count:
            parts, beside = lax.optimization_barrier((parts, beside))
        value = sum(parts[1:], parts[0])
    return value, beside


def per_device(inputs, out_grad, norm_gain, pos_bias, w_query, w_key, w_value, w_out):
    clips, frames, pixels, width = inputs.shape
    group = pos_bias.shape[0]
    tm = lax.axis_size("tm")
    me = lax.axis_index("tm")
    chans = width * tm
    head_dim = width // group
    total = frames * pixels
    bands = pixels // BAND
    rows = frames * BAND
    offsets = 2 * frames - 1
    span = -(-offsets * BAND // LANES) * LANES
    lines = -(-max(chans // LANES, group) // BAND) * BAND
    dims = (tm, frames, pixels, width, group, head_dim, 1e-06)
    x0 = inputs.reshape(total, width)
    g_bands = [out_grad[:, :, n * BAND:(n + 1) * BAND].reshape(rows, width) for n in range(bands)]
    x_parts = [x0] + [shifted(x0, "tm", k) for k in range(1, tm)]
    g_parts = [[g] + [shifted(g, "tm", k) for k in range(1, tm)] for g in g_bands]
    me1 = me.astype(jnp.int32).reshape(1)
    gain = norm_gain.reshape(1, chans)
    spread = jnp.broadcast_to(pos_bias[:, :, None], (*pos_bias.shape, BAND)).reshape(group, -1)
    smem, vmem = pl.BlockSpec(memory_space=pltpu.SMEM), pl.BlockSpec(memory_space=pltpu.VMEM)
    params = pltpu.CompilerParams(vmem_limit_bytes=VMEM_LIMIT)
    held = [x0, w_query, w_key, w_value, w_out, gain]
    held = [pltpu.with_memory_space_constraint(h, pltpu.HBM) for h in held]
    rel, x0, proj, w_out, gain, proj_turned, out_turned = pl.pallas_call(
        functools.partial(stage_kernel, frames, width),
        in_specs=[vmem] + [pl.BlockSpec(memory_space=pltpu.HBM)] * len(held),
        out_specs=[vmem] * 7,
        out_shape=[
            pltpu.VMEM((frames, group, rows), F32),
            pltpu.VMEM((total, width), BF16),
            pltpu.VMEM((chans, 3 * width), BF16),
            pltpu.VMEM((width, chans), BF16),
            pltpu.VMEM((1, chans), F32),
            pltpu.VMEM((3 * width, chans), BF16),
            pltpu.VMEM((chans, width), BF16),
        ],
        scratch_shapes=[pltpu.SemaphoreType.DMA((len(held),))],
        compiler_params=params,
        cost_estimate=pl.CostEstimate(flops=0, bytes_accessed=8_000_000, transcendentals=0),
        name="stage",
    )(spread, *held)
    x_parts[0] = x0
    qkv, probs, xb, inv, mix_own, *mix_out = pl.pallas_call(
        functools.partial(forward_kernel, dims),
        in_specs=[smem] + [vmem] * (tm + 4),
        out_specs=[vmem] * (5 + tm - 1),
        out_shape=[
            pltpu.VMEM((bands, rows, 3 * width), BF16),
            pltpu.VMEM((bands, group, rows, rows), BF16),
            pltpu.VMEM((bands, rows, chans), BF16),
            pltpu.VMEM((bands, rows, LANES), F32),
            pltpu.VMEM((bands, rows, width), F32),
        ] + [pltpu.VMEM((bands, rows, width), BF16)] * (tm - 1),
        scratch_shapes=[
            pltpu.VMEM((total, chans), BF16),
            pltpu.VMEM((bands, rows, chans), BF16),
            pltpu.VMEM((bands, rows, width), BF16),
            pltpu.VMEM((bands, width // LANES, LANES // head_dim * rows, rows), F32),
        ],
        compiler_params=params,
        cost_estimate=pl.CostEstimate(flops=4_000_000_000, bytes_accessed=8_000_000, transcendentals=0),
        name="attend",
    )(me1, *x_parts, gain, rel, proj, w_out)
    mix_in = [shifted(mix_out[k - 1], "tm", k) for k in range(1, tm)]
    owns, sent, carry = [], [], []
    diag = (frames, group, rows)
    for band in range(bands):
        last = band == bands - 1
        scratch = [
            pltpu.VMEM((rows, chans), BF16),
            pltpu.VMEM((width // LANES, LANES // head_dim * rows, rows), F32),
            pltpu.VMEM((group, rows, rows), BF16),
            pltpu.VMEM((rows, chans), F32),
        ]
        if last:
            extra = [jax.ShapeDtypeStruct((lines, LANES + span), F32)]
            scratch.append(pltpu.VMEM(diag, F32))
        else:
            extra = [jax.ShapeDtypeStruct((1, chans), F32), jax.ShapeDtypeStruct(diag, F32)]
        own, *rest = pl.pallas_call(
            functools.partial(backward_kernel, dims, band, last),
            in_specs=[smem] + [vmem] * (tm + 7 + len(carry) + len(sent)),
            out_specs=[vmem] * (tm + len(extra)),
            out_shape=[pltpu.VMEM((rows, width), F32)]
            + [pltpu.VMEM((bands, rows, width) if last else (rows, width), BF16)] * (tm - 1) + extra,
            scratch_shapes=scratch,
            compiler_params=params,
            cost_estimate=pl.CostEstimate(flops=2_500_000_000, bytes_accessed=0, transcendentals=0),
            name="attend_back",
        )(me1, *g_parts[band], gain, qkv, probs, xb, inv, proj_turned, out_turned, *carry, *sent)
        sent, carry = (rest[:tm - 1] if last else sent + rest[:tm - 1]), rest[tm - 1:]
        owns.append(own)

    result = jax.ShapeDtypeStruct((total, width), BF16)
    finish_cost = pl.CostEstimate(flops=0, bytes_accessed=1_500_000, transcendentals=0)
    small, mix_in = group_sum(carry[0], "dp", mix_in)
    grad_in = [shifted(sent[k - 1], "tm", k) for k in range(1, tm)]
    block_out = pl.pallas_call(
        functools.partial(finish_out_kernel, bands, frames),
        in_specs=[vmem] * tm,
        out_specs=vmem,
        out_shape=result,
        compiler_params=params,
        cost_estimate=finish_cost,
        name="finish_out",
    )(mix_own, *mix_in)
    small, block_out = group_sum(small, "space", block_out)

    tile = small[:chans // LANES, :LANES]
    tiles = [shifted(tile, "tm", k) for k in range(1, tm)]
    input_grad, bias_grad = pl.pallas_call(
        functools.partial(finish_grad_kernel, bands, frames),
        in_specs=[vmem] * (bands + tm),
        out_specs=[vmem] * 2,
        out_shape=[result, jax.ShapeDtypeStruct((group, offsets), F32)],
        compiler_params=params,
        cost_estimate=finish_cost,
        name="finish_grad",
    )(small, *owns, *grad_in)
    tiles, input_grad = lax.optimization_barrier((tiles, input_grad))
    gain_grad = pl.pallas_call(
        gain_kernel,
        in_specs=[smem] + [vmem] * tm,
        out_specs=vmem,
        out_shape=jax.ShapeDtypeStruct((1, width), F32),
        scratch_shapes=[pltpu.VMEM(tile.shape, F32)],
        compiler_params=params,
        name="gain_sum",
    )(me1, tile, *tiles)
    return (block_out.reshape(inputs.shape), input_grad.reshape(inputs.shape), gain_grad.reshape(width), bias_grad)


def solution(mesh):
    return jax.shard_map(
        per_device,
        mesh=mesh,
        in_specs=(
            P("dp", None, "space", "tm"),
            P("dp", None, "space", "tm"),
            P(),
            P("tm", None),
            P(None, "tm"),
            P(None, "tm"),
            P(None, "tm"),
            P("tm", None),
        ),
        out_specs=(
            P("dp", None, "space", "tm"),
            P("dp", None, "space", "tm"),
            P("tm"),
            P("tm", None),
        ),
        check_vma=False,
    )
```

```python
import functools

import jax
import jax.numpy as jnp
from jax import lax
from jax.experimental import pallas as pl
from jax.experimental.pallas import tpu as pltpu
from jax.sharding import PartitionSpec as P

CHUNK = 4
BAND = 8
LANES = 128
FAR = -1e30
F32, BF16 = jnp.float32, jnp.bfloat16
NT = (((1,), (1,)), ((), ()))
NN = (((1,), (0,)), ((), ()))
TN = (((0,), (0,)), ((), ()))
VMEM_LIMIT = 24 * 1024 * 1024


def mm(a, b, dims=NN):
    return lax.dot_general(a, b, dims, preferred_element_type=F32)


def same_pixel(rows):
    row = lax.broadcasted_iota(jnp.int32, (BAND, rows), 0)
    lane = lax.broadcasted_iota(jnp.int32, (BAND, rows), 1)
    return (lane & (BAND - 1)) == row


def head_lanes(head_dim, rows):
    return lax.broadcasted_iota(jnp.int32, (rows, LANES), 1) // head_dim


def stack_heads(pair, owner, per_pair, factor=None):
    pair = pair if factor is None else pair * jnp.asarray(factor, pair.dtype)
    return jnp.concatenate([jnp.where(owner == h, pair, jnp.zeros_like(pair)) for h in range(per_pair)], 0)


def pick_heads(parts, owner):
    out = parts[0]
    for h in range(1, len(parts)):
        out = jnp.where(owner == h, parts[h], out)
    return out


def stage_kernel(frames, width, bias_ref, x_ref, wq_ref, wk_ref, wv_ref, wo_ref, gain_ref,
                 rel_ref, x_out, proj_out, wo_out, gain_out, proj_turned, wo_turned, sems):
    pairs = [(x_ref, x_out), (wo_ref, wo_out), (gain_ref, gain_out)]
    pairs += [(w, proj_out.at[:, n * width:(n + 1) * width]) for n, w in enumerate((wq_ref, wk_ref, wv_ref))]
    copies = [pltpu.make_async_copy(source, target, sems.at[n]) for n, (source, target) in enumerate(pairs)]
    for copy in copies:
        copy.start()
    rows = rel_ref.shape[2]
    for i in range(frames):
        start = (frames - 1 - i) * BAND
        rel_ref[i] = bias_ref[:, start:start + rows]
    for copy in copies:
        copy.wait()
    for source, target in ((proj_out, proj_turned), (wo_out, wo_turned)):
        for start in range(0, source.shape[1], 2 * LANES):
            target[start:start + 2 * LANES, :] = source[:, start:start + 2 * LANES].T


def forward_kernel(dims, me_ref, *refs):
    tm, frames, pixels, width, group, head_dim, eps = dims
    x_refs = refs[:tm]
    gain_ref, rel_ref, proj_ref, wo_ref = refs[tm:tm + 4]
    qkv_ref, p_ref, xb_ref, inv_ref, own_ref = refs[tm + 4:tm + 9]
    msg_refs = refs[tm + 9:tm + 9 + tm - 1]
    xw_ref, normed_ref, att_ref, score_ref = refs[tm + 9 + tm - 1:]
    me = me_ref[0]
    rows = frames * BAND
    bands = pixels // BAND
    per_pair = LANES // head_dim
    scale = head_dim ** -0.5

    def place(k):
        return pl.multiple_of(lax.rem(me + k, tm) * width, width)

    for k in range(tm):
        xw_ref[:, pl.ds(place(k), width)] = x_refs[k][...]
    for f in range(0, frames, 2):
        both = xw_ref[f * pixels:(f + 2) * pixels, :].astype(F32).reshape(2, bands, BAND, -1)
        for band in range(bands):
            x = both[:, band].reshape(2 * BAND, -1)
            inv = lax.rsqrt(jnp.mean(x * x, axis=-1, keepdims=True) + eps)
            at = slice(f * BAND, (f + 2) * BAND)
            normed_ref[band, at, :] = (x * inv * gain_ref[...]).astype(BF16)
            xb_ref[band, at, :] = x.astype(BF16)
            inv_ref[band, at, :] = jnp.broadcast_to(inv, (2 * BAND, LANES))
    same = same_pixel(rows)[None]
    owner = head_lanes(head_dim, rows)
    total = frames * pixels
    qkv = mm(normed_ref[...].reshape(total, -1), proj_ref[...]).astype(BF16)
    qkv_ref[...] = qkv.reshape(bands, rows, 3 * width)
    pairs = [(band, pair) for band in range(bands) for pair in range(width // LANES)]

    def cols(n, pair):
        return slice(n * width + pair * LANES, n * width + (pair + 1) * LANES)

    for band, pair in pairs:
        stacked = stack_heads(qkv_ref[band, :, cols(0, pair)], owner, per_pair, scale)
        score_ref[band, pair] = mm(stacked, qkv_ref[band, :, cols(1, pair)], NT)
    for band, pair in pairs:
        for h in range(per_pair):
            head = pair * per_pair + h
            for f in range(0, frames, CHUNK):
                at = slice(f * BAND, (f + CHUNK) * BAND)
                s = score_ref[band, pair, h * rows + f * BAND:h * rows + (f + CHUNK) * BAND, :]
                s = s.reshape(CHUNK, BAND, rows)
                s = jnp.where(same, s + rel_ref[f:f + CHUNK, head:head + 1, :], FAR)
                s = s.reshape(CHUNK * BAND, rows)
                e = jnp.exp(s - jnp.max(s, axis=-1, keepdims=True))
                p_ref[band, head, at, :] = (e * (1.0 / jnp.sum(e, axis=-1, keepdims=True))).astype(BF16)
    for band, pair in pairs:
        outs = [mm(p_ref[band, pair * per_pair + h], qkv_ref[band, :, cols(2, pair)]) for h in range(per_pair)]
        att_ref[band, :, pair * LANES:(pair + 1) * LANES] = pick_heads(outs, owner).astype(BF16)
    att = att_ref[...].reshape(total, width)
    for k in range(1, tm):
        part = mm(att, wo_ref[:, pl.ds(place(tm - k), width)]).astype(BF16)
        msg_refs[k - 1][...] = part.reshape(bands, rows, width)
    own = mm(att, wo_ref[:, pl.ds(place(0), width)]).reshape(bands, rows, width)
    own_ref[...] = own + xb_ref[:, :, pl.ds(place(0), width)].astype(F32)


def backward_kernel(dims, band, last, me_ref, *refs):
    tm, frames, pixels, width, group, head_dim, eps = dims
    g_refs = refs[:tm]
    gain_ref, qkv_ref, p_ref, xb_ref, inv_ref, proj_ref, wo_ref = refs[tm:tm + 7]
    rest = list(refs[tm + 7:])
    carried = (rest.pop(0), rest.pop(0)) if band else None
    earlier = [rest.pop(0) for _ in range(band * (tm - 1))]
    own_ref = rest.pop(0)
    msg_refs = [rest.pop(0) for _ in range(tm - 1)]
    small_ref = rest.pop(0) if last else None
    gain_out = None if last else rest.pop(0)
    diag_ref = rest.pop() if last else rest.pop(0)
    gw_ref, dp_ref, ds_ref, grad_ref = rest
    me = me_ref[0]
    rows = frames * BAND
    per_pair = LANES // head_dim
    scale = head_dim ** -0.5
    chans = width * tm

    def place(k):
        return pl.multiple_of(lax.rem(me + k, tm) * width, width)

    for k in range(tm):
        gw_ref[:, pl.ds(place(k), width)] = g_refs[k][...]
    owner = head_lanes(head_dim, rows)
    d_att = mm(gw_ref[...], wo_ref[...]).astype(BF16)
    pairs = range(width // LANES)

    def part(n, pair):
        return qkv_ref[band, :, n * width + pair * LANES:n * width + (pair + 1) * LANES]

    def out_rows(pair):
        return d_att[:, pair * LANES:(pair + 1) * LANES]

    for pair in pairs:
        dp_ref[pair] = mm(stack_heads(out_rows(pair), owner, per_pair), part(2, pair), NT)
    for pair in pairs:
        for h in range(per_pair):
            head = pair * per_pair + h
            for f in range(0, frames, CHUNK):
                at = slice(f * BAND, (f + CHUNK) * BAND)
                full = p_ref[band, head, at, :].astype(F32)
                t = dp_ref[pair, h * rows + f * BAND:h * rows + (f + CHUNK) * BAND, :]
                score = full * (t - jnp.sum(full * t, axis=-1, keepdims=True))
                ds_ref[head, at, :] = (score * scale).astype(BF16)
                folded = jnp.sum(score.reshape(CHUNK, BAND, rows), axis=1, keepdims=True)
                if carried is not None:
                    folded = folded + carried[1][f:f + CHUNK, head:head + 1, :]
                diag_ref[f:f + CHUNK, head:head + 1, :] = folded
    grads = [[], [], []]
    for pair in pairs:
        turned = [None, part(0, pair).T, out_rows(pair).T]
        products = [[], [], []]
        for h in range(per_pair):
            head = pair * per_pair + h
            own = slice(h * head_dim, (h + 1) * head_dim)
            products[0].append(mm(ds_ref[head], part(1, pair)))
            products[1].append(mm(turned[1][own], ds_ref[head]))
            products[2].append(mm(turned[2][own], p_ref[band, head]))
        grads[0].append(pick_heads(products[0], owner).astype(BF16))
        for n in (1, 2):
            grads[n].append(jnp.concatenate(products[n], axis=0).astype(BF16).T)
    grad_ref[...] = mm(jnp.concatenate(grads[0] + grads[1] + grads[2], axis=1), proj_ref[...])
    gain_sum = jnp.zeros((BAND, chans), F32)
    for f in range(0, frames, 2):
        at = slice(f * BAND, (f + 2) * BAND)
        grad, x = grad_ref[at, :], xb_ref[band, at, :].astype(F32)
        inv = inv_ref[band, at, :1]
        scaled = x * inv
        gain_sum = gain_sum + jnp.sum((grad * scaled).reshape(2, BAND, chans), axis=0)
        term = grad * gain_ref[...]
        inner = jnp.mean(term * scaled, axis=-1, keepdims=True)
        grad_ref[at, :] = inv * (term - scaled * inner)
    for k in range(1, tm):
        share = grad_ref[:, pl.ds(place(tm - k), width)].astype(BF16)
        if last:
            for n in range(band):
                msg_refs[k - 1][n] = earlier[n * (tm - 1) + k - 1][...]
            msg_refs[k - 1][band] = share
        else:
            msg_refs[k - 1][...] = share
    own_ref[...] = grad_ref[:, pl.ds(place(0), width)] + g_refs[0][...].astype(F32)
    gain_sum = jnp.sum(gain_sum, axis=0, keepdims=True)
    if carried is not None:
        gain_sum = gain_sum + carried[0][...]
    if not last:
        gain_out[...] = gain_sum
        return
    small_ref[...] = jnp.zeros_like(small_ref)
    for r in range(chans // LANES):
        small_ref[r:r + 1, :LANES] = gain_sum[:, r * LANES:(r + 1) * LANES]
    span = small_ref.shape[1] - LANES
    bias = jnp.zeros((group, span), F32)
    for i in range(frames):
        before = (frames - 1 - i) * BAND
        bias = bias + jnp.pad(diag_ref[i], ((0, 0), (before, span - before - rows)))
    small_ref[:group, LANES:] = bias


def finish_kernel(bands, frames, own_refs, in_refs, out_ref):
    each = len(in_refs) // bands
    parts = []
    for band in range(bands):
        value = own_refs[band][...]
        for ref in in_refs[band * each:(band + 1) * each]:
            value = value + ref[...].astype(F32)
        parts.append(value.reshape(frames, 1, BAND, value.shape[-1]))
    value = jnp.concatenate(parts, axis=1)
    out_ref[...] = value.reshape(out_ref.shape).astype(out_ref.dtype)


def finish_grad_kernel(bands, frames, small_ref, *refs):
    *refs, out_ref, bias_ref = refs
    in_refs = [ref.at[band] for band in range(bands) for ref in refs[bands:]]
    finish_kernel(bands, frames, refs[:bands], in_refs, out_ref)
    group, offsets = bias_ref.shape
    value = small_ref[:, LANES:]
    high = value.astype(BF16)
    rest = value - high.astype(F32)
    middle = rest.astype(BF16)
    low = (rest - middle.astype(F32)).astype(BF16)
    span = value.shape[1]
    lane = lax.broadcasted_iota(jnp.int32, (span, LANES), 0) // BAND
    put = (lane == lax.broadcasted_iota(jnp.int32, (span, LANES), 1)).astype(F32).astype(BF16)
    total = mm(high, put) + mm(middle, put) + mm(low, put)
    bias_ref[...] = total[:group, :offsets]


def finish_out_kernel(bands, frames, own_ref, *refs):
    in_refs = [ref.at[band] for band in range(bands) for ref in refs[:-1]]
    finish_kernel(bands, frames, [own_ref.at[band] for band in range(bands)], in_refs, refs[-1])


def gain_kernel(me_ref, *refs):
    *tile_refs, out_ref, sum_ref = refs
    total = tile_refs[0][...]
    for ref in tile_refs[1:]:
        total = total + ref[...]
    sum_ref[...] = total
    count = out_ref.shape[1] // LANES
    for r in range(count):
        out_ref[:, r * LANES:(r + 1) * LANES] = sum_ref[pl.ds(me_ref[0] * count + r, 1), :]


def shifted(value, axis, step):
    count = lax.axis_size(axis)
    return lax.ppermute(value, axis, [((i + step) % count, i) for i in range(count)])


def group_sum(value, axis, beside=()):
    count = lax.axis_size(axis)
    stride = 1
    while stride < count:
        left = count // stride
        radix = 4 if left % 4 == 0 else 2 if left % 2 == 0 else left
        parts = [value]
        for step in reversed(range(1, radix)):
            pairs = []
            for i in range(count):
                digit = i // stride % radix
                other = digit ^ step if radix in (2, 4) else (digit + step) % radix
                pairs.append((i + (other - digit) * stride, i))
            parts.append(lax.ppermute(value, axis, pairs))
        stride *= radix
        if stride == count:
            parts, beside = lax.optimization_barrier((parts, beside))
        value = sum(parts[1:], parts[0])
    return value, beside


def per_device(inputs, out_grad, norm_gain, pos_bias, w_query, w_key, w_value, w_out):
    clips, frames, pixels, width = inputs.shape
    group = pos_bias.shape[0]
    tm = lax.axis_size("tm")
    me = lax.axis_index("tm")
    chans = width * tm
    head_dim = width // group
    total = frames * pixels
    bands = pixels // BAND
    rows = frames * BAND
    offsets = 2 * frames - 1
    span = -(-offsets * BAND // LANES) * LANES
    lines = -(-max(chans // LANES, group) // BAND) * BAND
    dims = (tm, frames, pixels, width, group, head_dim, 1e-06)
    x0 = inputs.reshape(total, width)
    g_bands = [out_grad[:, :, n * BAND:(n + 1) * BAND].reshape(rows, width) for n in range(bands)]
    x_parts = [x0] + [shifted(x0, "tm", k) for k in range(1, tm)]
    g_parts = [[g] + [shifted(g, "tm", k) for k in range(1, tm)] for g in g_bands]
    me1 = me.astype(jnp.int32).reshape(1)
    gain = norm_gain.reshape(1, chans)
    spread = jnp.broadcast_to(pos_bias[:, :, None], (*pos_bias.shape, BAND)).reshape(group, -1)
    smem, vmem = pl.BlockSpec(memory_space=pltpu.SMEM), pl.BlockSpec(memory_space=pltpu.VMEM)
    params = pltpu.CompilerParams(vmem_limit_bytes=VMEM_LIMIT)
    held = [x0, w_query, w_key, w_value, w_out, gain]
    held = [pltpu.with_memory_space_constraint(h, pltpu.HBM) for h in held]
    rel, x0, proj, w_out, gain, proj_turned, out_turned = pl.pallas_call(
        functools.partial(stage_kernel, frames, width),
        in_specs=[vmem] + [pl.BlockSpec(memory_space=pltpu.HBM)] * len(held),
        out_specs=[vmem] * 7,
        out_shape=[
            pltpu.VMEM((frames, group, rows), F32),
            pltpu.VMEM((total, width), BF16),
            pltpu.VMEM((chans, 3 * width), BF16),
            pltpu.VMEM((width, chans), BF16),
            pltpu.VMEM((1, chans), F32),
            pltpu.VMEM((3 * width, chans), BF16),
            pltpu.VMEM((chans, width), BF16),
        ],
        scratch_shapes=[pltpu.SemaphoreType.DMA((len(held),))],
        compiler_params=params,
        cost_estimate=pl.CostEstimate(flops=0, bytes_accessed=8_000_000, transcendentals=0),
        name="stage",
    )(spread, *held)
    x_parts[0] = x0
    qkv, probs, xb, inv, mix_own, *mix_out = pl.pallas_call(
        functools.partial(forward_kernel, dims),
        in_specs=[smem] + [vmem] * (tm + 4),
        out_specs=[vmem] * (5 + tm - 1),
        out_shape=[
            pltpu.VMEM((bands, rows, 3 * width), BF16),
            pltpu.VMEM((bands, group, rows, rows), BF16),
            pltpu.VMEM((bands, rows, chans), BF16),
            pltpu.VMEM((bands, rows, LANES), F32),
            pltpu.VMEM((bands, rows, width), F32),
        ] + [pltpu.VMEM((bands, rows, width), BF16)] * (tm - 1),
        scratch_shapes=[
            pltpu.VMEM((total, chans), BF16),
            pltpu.VMEM((bands, rows, chans), BF16),
            pltpu.VMEM((bands, rows, width), BF16),
            pltpu.VMEM((bands, width // LANES, LANES // head_dim * rows, rows), F32),
        ],
        compiler_params=params,
        cost_estimate=pl.CostEstimate(flops=4_000_000_000, bytes_accessed=8_000_000, transcendentals=0),
        name="attend",
    )(me1, *x_parts, gain, rel, proj, w_out)
    mix_in = [shifted(mix_out[k - 1], "tm", k) for k in range(1, tm)]
    owns, sent, carry = [], [], []
    diag = (frames, group, rows)
    for band in range(bands):
        last = band == bands - 1
        scratch = [
            pltpu.VMEM((rows, chans), BF16),
            pltpu.VMEM((width // LANES, LANES // head_dim * rows, rows), F32),
            pltpu.VMEM((group, rows, rows), BF16),
            pltpu.VMEM((rows, chans), F32),
        ]
        if last:
            extra = [jax.ShapeDtypeStruct((lines, LANES + span), F32)]
            scratch.append(pltpu.VMEM(diag, F32))
        else:
            extra = [jax.ShapeDtypeStruct((1, chans), F32), jax.ShapeDtypeStruct(diag, F32)]
        own, *rest = pl.pallas_call(
            functools.partial(backward_kernel, dims, band, last),
            in_specs=[smem] + [vmem] * (tm + 7 + len(carry) + len(sent)),
            out_specs=[vmem] * (tm + len(extra)),
            out_shape=[pltpu.VMEM((rows, width), F32)]
            + [pltpu.VMEM((bands, rows, width) if last else (rows, width), BF16)] * (tm - 1) + extra,
            scratch_shapes=scratch,
            compiler_params=params,
            cost_estimate=pl.CostEstimate(flops=2_500_000_000, bytes_accessed=0, transcendentals=0),
            name="attend_back",
        )(me1, *g_parts[band], gain, qkv, probs, xb, inv, proj_turned, out_turned, *carry, *sent)
        sent, carry = (rest[:tm - 1] if last else sent + rest[:tm - 1]), rest[tm - 1:]
        owns.append(own)

    result = jax.ShapeDtypeStruct((total, width), BF16)
    finish_cost = pl.CostEstimate(flops=0, bytes_accessed=1_500_000, transcendentals=0)
    small, mix_in = group_sum(carry[0], "dp", mix_in)
    grad_in = [shifted(sent[k - 1], "tm", k) for k in range(1, tm)]
    block_out = pl.pallas_call(
        functools.partial(finish_out_kernel, bands, frames),
        in_specs=[vmem] * tm,
        out_specs=vmem,
        out_shape=result,
        compiler_params=params,
        cost_estimate=finish_cost,
        name="finish_out",
    )(mix_own, *mix_in)
    small, (block_out, grad_in) = group_sum(small, "space", (block_out, grad_in))

    tile = small[:chans // LANES, :LANES]
    tiles = [shifted(tile, "tm", k) for k in range(1, tm)]
    input_grad, bias_grad = pl.pallas_call(
        functools.partial(finish_grad_kernel, bands, frames),
        in_specs=[vmem] * (bands + tm),
        out_specs=[vmem] * 2,
        out_shape=[result, jax.ShapeDtypeStruct((group, offsets), F32)],
        compiler_params=params,
        cost_estimate=finish_cost,
        name="finish_grad",
    )(small, *owns, *grad_in)
    tiles, input_grad = lax.optimization_barrier((tiles, input_grad))
    gain_grad = pl.pallas_call(
        gain_kernel,
        in_specs=[smem] + [vmem] * tm,
        out_specs=vmem,
        out_shape=jax.ShapeDtypeStruct((1, width), F32),
        scratch_shapes=[pltpu.VMEM(tile.shape, F32)],
        compiler_params=params,
        name="gain_sum",
    )(me1, tile, *tiles)
    return (block_out.reshape(inputs.shape), input_grad.reshape(inputs.shape), gain_grad.reshape(width), bias_grad)


def solution(mesh):
    return jax.shard_map(
        per_device,
        mesh=mesh,
        in_specs=(
            P("dp", None, "space", "tm"),
            P("dp", None, "space", "tm"),
            P(),
            P("tm", None),
            P(None, "tm"),
            P(None, "tm"),
            P(None, "tm"),
            P("tm", None),
        ),
        out_specs=(
            P("dp", None, "space", "tm"),
            P("dp", None, "space", "tm"),
            P("tm"),
            P("tm", None),
        ),
        check_vma=False,
    )
```

```python
import functools

import jax
import jax.numpy as jnp
from jax import lax
from jax.experimental import pallas as pl
from jax.experimental.pallas import tpu as pltpu
from jax.sharding import PartitionSpec as P

CHUNK = 4
BAND = 8
LANES = 128
FAR = -1e30
F32, BF16 = jnp.float32, jnp.bfloat16
NT = (((1,), (1,)), ((), ()))
NN = (((1,), (0,)), ((), ()))
TN = (((0,), (0,)), ((), ()))
VMEM_LIMIT = 24 * 1024 * 1024


def mm(a, b, dims=NN):
    return lax.dot_general(a, b, dims, preferred_element_type=F32)


def same_pixel(rows):
    row = lax.broadcasted_iota(jnp.int32, (BAND, rows), 0)
    lane = lax.broadcasted_iota(jnp.int32, (BAND, rows), 1)
    return (lane & (BAND - 1)) == row


def head_lanes(head_dim, rows):
    return lax.broadcasted_iota(jnp.int32, (rows, LANES), 1) // head_dim


def stack_heads(pair, owner, per_pair, factor=None):
    pair = pair if factor is None else pair * jnp.asarray(factor, pair.dtype)
    return jnp.concatenate([jnp.where(owner == h, pair, jnp.zeros_like(pair)) for h in range(per_pair)], 0)


def pick_heads(parts, owner):
    out = parts[0]
    for h in range(1, len(parts)):
        out = jnp.where(owner == h, parts[h], out)
    return out


def stage_kernel(frames, width, bias_ref, x_ref, wq_ref, wk_ref, wv_ref, wo_ref, gain_ref,
                 rel_ref, x_out, proj_out, wo_out, gain_out, proj_turned, wo_turned, sems):
    pairs = [(x_ref, x_out), (wo_ref, wo_out), (gain_ref, gain_out)]
    pairs += [(w, proj_out.at[:, n * width:(n + 1) * width]) for n, w in enumerate((wq_ref, wk_ref, wv_ref))]
    copies = [pltpu.make_async_copy(source, target, sems.at[n]) for n, (source, target) in enumerate(pairs)]
    for copy in copies:
        copy.start()
    rows = rel_ref.shape[2]
    for i in range(frames):
        start = (frames - 1 - i) * BAND
        rel_ref[i] = bias_ref[:, start:start + rows]
    for copy in copies:
        copy.wait()
    for source, target in ((proj_out, proj_turned), (wo_out, wo_turned)):
        for start in range(0, source.shape[1], 2 * LANES):
            target[start:start + 2 * LANES, :] = source[:, start:start + 2 * LANES].T


def forward_kernel(dims, me_ref, *refs):
    tm, frames, pixels, width, group, head_dim, eps = dims
    x_refs = refs[:tm]
    gain_ref, rel_ref, proj_ref, wo_ref = refs[tm:tm + 4]
    qkv_ref, p_ref, xb_ref, inv_ref, own_ref = refs[tm + 4:tm + 9]
    msg_refs = refs[tm + 9:tm + 9 + tm - 1]
    xw_ref, normed_ref, att_ref, score_ref = refs[tm + 9 + tm - 1:]
    me = me_ref[0]
    rows = frames * BAND
    bands = pixels // BAND
    per_pair = LANES // head_dim
    scale = head_dim ** -0.5

    def place(k):
        return pl.multiple_of(lax.rem(me + k, tm) * width, width)

    for k in range(tm):
        xw_ref[:, pl.ds(place(k), width)] = x_refs[k][...]
    for f in range(0, frames, 2):
        both = xw_ref[f * pixels:(f + 2) * pixels, :].astype(F32).reshape(2, bands, BAND, -1)
        for band in range(bands):
            x = both[:, band].reshape(2 * BAND, -1)
            inv = lax.rsqrt(jnp.mean(x * x, axis=-1, keepdims=True) + eps)
            at = slice(f * BAND, (f + 2) * BAND)
            normed_ref[band, at, :] = (x * inv * gain_ref[...]).astype(BF16)
            xb_ref[band, at, :] = x.astype(BF16)
            inv_ref[band, at, :] = jnp.broadcast_to(inv, (2 * BAND, LANES))
    same = same_pixel(rows)[None]
    owner = head_lanes(head_dim, rows)
    total = frames * pixels
    qkv = mm(normed_ref[...].reshape(total, -1), proj_ref[...]).astype(BF16)
    qkv_ref[...] = qkv.reshape(bands, rows, 3 * width)
    pairs = [(band, pair) for band in range(bands) for pair in range(width // LANES)]

    def cols(n, pair):
        return slice(n * width + pair * LANES, n * width + (pair + 1) * LANES)

    for band, pair in pairs:
        stacked = stack_heads(qkv_ref[band, :, cols(0, pair)], owner, per_pair, scale)
        score_ref[band, pair] = mm(stacked, qkv_ref[band, :, cols(1, pair)], NT)
    for band, pair in pairs:
        for h in range(per_pair):
            head = pair * per_pair + h
            for f in range(0, frames, CHUNK):
                at = slice(f * BAND, (f + CHUNK) * BAND)
                s = score_ref[band, pair, h * rows + f * BAND:h * rows + (f + CHUNK) * BAND, :]
                s = s.reshape(CHUNK, BAND, rows)
                s = jnp.where(same, s + rel_ref[f:f + CHUNK, head:head + 1, :], FAR)
                s = s.reshape(CHUNK * BAND, rows)
                e = jnp.exp(s - jnp.max(s, axis=-1, keepdims=True))
                p_ref[band, head, at, :] = (e * (1.0 / jnp.sum(e, axis=-1, keepdims=True))).astype(BF16)
    for band, pair in pairs:
        outs = [mm(p_ref[band, pair * per_pair + h], qkv_ref[band, :, cols(2, pair)]) for h in range(per_pair)]
        att_ref[band, :, pair * LANES:(pair + 1) * LANES] = pick_heads(outs, owner).astype(BF16)
    att = att_ref[...].reshape(total, width)
    for k in range(1, tm):
        part = mm(att, wo_ref[:, pl.ds(place(tm - k), width)]).astype(BF16)
        msg_refs[k - 1][...] = part.reshape(bands, rows, width)
    own = mm(att, wo_ref[:, pl.ds(place(0), width)]).reshape(bands, rows, width)
    own_ref[...] = own + xb_ref[:, :, pl.ds(place(0), width)].astype(F32)


def backward_kernel(dims, band, last, me_ref, *refs):
    tm, frames, pixels, width, group, head_dim, eps = dims
    g_refs = refs[:tm]
    gain_ref, qkv_ref, p_ref, xb_ref, inv_ref, proj_ref, wo_ref = refs[tm:tm + 7]
    rest = list(refs[tm + 7:])
    carried = (rest.pop(0), rest.pop(0)) if band else None
    earlier = [rest.pop(0) for _ in range(band * (tm - 1))]
    own_ref = rest.pop(0)
    msg_refs = [rest.pop(0) for _ in range(tm - 1)]
    small_ref = rest.pop(0) if last else None
    gain_out = None if last else rest.pop(0)
    diag_ref = rest.pop() if last else rest.pop(0)
    gw_ref, dp_ref, ds_ref, grad_ref = rest
    me = me_ref[0]
    rows = frames * BAND
    per_pair = LANES // head_dim
    scale = head_dim ** -0.5
    chans = width * tm

    def place(k):
        return pl.multiple_of(lax.rem(me + k, tm) * width, width)

    for k in range(tm):
        gw_ref[:, pl.ds(place(k), width)] = g_refs[k][...]
    owner = head_lanes(head_dim, rows)
    d_att = mm(gw_ref[...], wo_ref[...]).astype(BF16)
    pairs = range(width // LANES)

    def part(n, pair):
        return qkv_ref[band, :, n * width + pair * LANES:n * width + (pair + 1) * LANES]

    def out_rows(pair):
        return d_att[:, pair * LANES:(pair + 1) * LANES]

    for pair in pairs:
        dp_ref[pair] = mm(stack_heads(out_rows(pair), owner, per_pair), part(2, pair), NT)
    for pair in pairs:
        for h in range(per_pair):
            head = pair * per_pair + h
            for f in range(0, frames, CHUNK):
                at = slice(f * BAND, (f + CHUNK) * BAND)
                full = p_ref[band, head, at, :].astype(F32)
                t = dp_ref[pair, h * rows + f * BAND:h * rows + (f + CHUNK) * BAND, :]
                score = full * (t - jnp.sum(full * t, axis=-1, keepdims=True))
                ds_ref[head, at, :] = (score * scale).astype(BF16)
                folded = jnp.sum(score.reshape(CHUNK, BAND, rows), axis=1, keepdims=True)
                if carried is not None:
                    folded = folded + carried[1][f:f + CHUNK, head:head + 1, :]
                diag_ref[f:f + CHUNK, head:head + 1, :] = folded
    grads = [[], [], []]
    for pair in pairs:
        turned = [None, part(0, pair).T, out_rows(pair).T]
        products = [[], [], []]
        for h in range(per_pair):
            head = pair * per_pair + h
            own = slice(h * head_dim, (h + 1) * head_dim)
            products[0].append(mm(ds_ref[head], part(1, pair)))
            products[1].append(mm(turned[1][own], ds_ref[head]))
            products[2].append(mm(turned[2][own], p_ref[band, head]))
        grads[0].append(pick_heads(products[0], owner).astype(BF16))
        for n in (1, 2):
            grads[n].append(jnp.concatenate(products[n], axis=0).astype(BF16).T)
    grad_ref[...] = mm(jnp.concatenate(grads[0] + grads[1] + grads[2], axis=1), proj_ref[...])
    gain_sum = jnp.zeros((BAND, chans), F32)
    for f in range(0, frames, 2):
        at = slice(f * BAND, (f + 2) * BAND)
        grad, x = grad_ref[at, :], xb_ref[band, at, :].astype(F32)
        inv = inv_ref[band, at, :1]
        scaled = x * inv
        gain_sum = gain_sum + jnp.sum((grad * scaled).reshape(2, BAND, chans), axis=0)
        term = grad * gain_ref[...]
        inner = jnp.mean(term * scaled, axis=-1, keepdims=True)
        grad_ref[at, :] = inv * (term - scaled * inner)
    for k in range(1, tm):
        share = grad_ref[:, pl.ds(place(tm - k), width)].astype(BF16)
        if last:
            for n in range(band):
                msg_refs[k - 1][n] = earlier[n * (tm - 1) + k - 1][...]
            msg_refs[k - 1][band] = share
        else:
            msg_refs[k - 1][...] = share
    own_ref[...] = grad_ref[:, pl.ds(place(0), width)] + g_refs[0][...].astype(F32)
    gain_sum = jnp.sum(gain_sum, axis=0, keepdims=True)
    if carried is not None:
        gain_sum = gain_sum + carried[0][...]
    if not last:
        gain_out[...] = gain_sum
        return
    small_ref[...] = jnp.zeros_like(small_ref)
    for r in range(chans // LANES):
        small_ref[r:r + 1, :LANES] = gain_sum[:, r * LANES:(r + 1) * LANES]
    span = small_ref.shape[1] - LANES
    bias = jnp.zeros((group, span), F32)
    for i in range(frames):
        before = (frames - 1 - i) * BAND
        bias = bias + jnp.pad(diag_ref[i], ((0, 0), (before, span - before - rows)))
    small_ref[:group, LANES:] = bias


def finish_kernel(bands, frames, own_refs, in_refs, out_ref):
    each = len(in_refs) // bands
    parts = []
    for band in range(bands):
        value = own_refs[band][...]
        for ref in in_refs[band * each:(band + 1) * each]:
            value = value + ref[...].astype(F32)
        parts.append(value.reshape(frames, 1, BAND, value.shape[-1]))
    value = jnp.concatenate(parts, axis=1)
    out_ref[...] = value.reshape(out_ref.shape).astype(out_ref.dtype)


def finish_grad_kernel(bands, frames, small_ref, *refs):
    *refs, out_ref, bias_ref = refs
    in_refs = [ref.at[band] for band in range(bands) for ref in refs[bands:]]
    finish_kernel(bands, frames, refs[:bands], in_refs, out_ref)
    group, offsets = bias_ref.shape
    value = small_ref[:, LANES:]
    high = value.astype(BF16)
    rest = value - high.astype(F32)
    middle = rest.astype(BF16)
    low = (rest - middle.astype(F32)).astype(BF16)
    span = value.shape[1]
    lane = lax.broadcasted_iota(jnp.int32, (span, LANES), 0) // BAND
    put = (lane == lax.broadcasted_iota(jnp.int32, (span, LANES), 1)).astype(F32).astype(BF16)
    total = mm(high, put) + mm(middle, put) + mm(low, put)
    bias_ref[...] = total[:group, :offsets]


def finish_out_kernel(bands, frames, own_ref, *refs):
    in_refs = [ref.at[band] for band in range(bands) for ref in refs[:-1]]
    finish_kernel(bands, frames, [own_ref.at[band] for band in range(bands)], in_refs, refs[-1])


def gain_kernel(me_ref, *refs):
    *tile_refs, out_ref, sum_ref = refs
    total = tile_refs[0][...]
    for ref in tile_refs[1:]:
        total = total + ref[...]
    sum_ref[...] = total
    count = out_ref.shape[1] // LANES
    for r in range(count):
        out_ref[:, r * LANES:(r + 1) * LANES] = sum_ref[pl.ds(me_ref[0] * count + r, 1), :]


def shifted(value, axis, step):
    count = lax.axis_size(axis)
    return lax.ppermute(value, axis, [((i + step) % count, i) for i in range(count)])


def group_sum(value, axis, beside=()):
    count = lax.axis_size(axis)
    stride = 1
    while stride < count:
        left = count // stride
        radix = 4 if left % 4 == 0 else 2 if left % 2 == 0 else left
        parts = [value]
        for step in (2, 3, 1) if radix == 4 else range(1, radix):
            pairs = []
            for i in range(count):
                digit = i // stride % radix
                other = digit ^ step if radix in (2, 4) else (digit + step) % radix
                pairs.append((i + (other - digit) * stride, i))
            parts.append(lax.ppermute(value, axis, pairs))
        stride *= radix
        if stride == count:
            parts, beside = lax.optimization_barrier((parts, beside))
        value = sum(parts[1:], parts[0])
    return value, beside


def per_device(inputs, out_grad, norm_gain, pos_bias, w_query, w_key, w_value, w_out):
    clips, frames, pixels, width = inputs.shape
    group = pos_bias.shape[0]
    tm = lax.axis_size("tm")
    me = lax.axis_index("tm")
    chans = width * tm
    head_dim = width // group
    total = frames * pixels
    bands = pixels // BAND
    rows = frames * BAND
    offsets = 2 * frames - 1
    span = -(-offsets * BAND // LANES) * LANES
    lines = -(-max(chans // LANES, group) // BAND) * BAND
    dims = (tm, frames, pixels, width, group, head_dim, 1e-06)
    x0 = inputs.reshape(total, width)
    g_bands = [out_grad[:, :, n * BAND:(n + 1) * BAND].reshape(rows, width) for n in range(bands)]
    x_parts = [x0] + [shifted(x0, "tm", k) for k in range(1, tm)]
    g_parts = [[g] + [shifted(g, "tm", k) for k in range(1, tm)] for g in g_bands]
    me1 = me.astype(jnp.int32).reshape(1)
    gain = norm_gain.reshape(1, chans)
    spread = jnp.broadcast_to(pos_bias[:, :, None], (*pos_bias.shape, BAND)).reshape(group, -1)
    smem, vmem = pl.BlockSpec(memory_space=pltpu.SMEM), pl.BlockSpec(memory_space=pltpu.VMEM)
    params = pltpu.CompilerParams(vmem_limit_bytes=VMEM_LIMIT)
    held = [x0, w_query, w_key, w_value, w_out, gain]
    held = [pltpu.with_memory_space_constraint(h, pltpu.HBM) for h in held]
    rel, x0, proj, w_out, gain, proj_turned, out_turned = pl.pallas_call(
        functools.partial(stage_kernel, frames, width),
        in_specs=[vmem] + [pl.BlockSpec(memory_space=pltpu.HBM)] * len(held),
        out_specs=[vmem] * 7,
        out_shape=[
            pltpu.VMEM((frames, group, rows), F32),
            pltpu.VMEM((total, width), BF16),
            pltpu.VMEM((chans, 3 * width), BF16),
            pltpu.VMEM((width, chans), BF16),
            pltpu.VMEM((1, chans), F32),
            pltpu.VMEM((3 * width, chans), BF16),
            pltpu.VMEM((chans, width), BF16),
        ],
        scratch_shapes=[pltpu.SemaphoreType.DMA((len(held),))],
        compiler_params=params,
        cost_estimate=pl.CostEstimate(flops=0, bytes_accessed=8_000_000, transcendentals=0),
        name="stage",
    )(spread, *held)
    x_parts[0] = x0
    qkv, probs, xb, inv, mix_own, *mix_out = pl.pallas_call(
        functools.partial(forward_kernel, dims),
        in_specs=[smem] + [vmem] * (tm + 4),
        out_specs=[vmem] * (5 + tm - 1),
        out_shape=[
            pltpu.VMEM((bands, rows, 3 * width), BF16),
            pltpu.VMEM((bands, group, rows, rows), BF16),
            pltpu.VMEM((bands, rows, chans), BF16),
            pltpu.VMEM((bands, rows, LANES), F32),
            pltpu.VMEM((bands, rows, width), F32),
        ] + [pltpu.VMEM((bands, rows, width), BF16)] * (tm - 1),
        scratch_shapes=[
            pltpu.VMEM((total, chans), BF16),
            pltpu.VMEM((bands, rows, chans), BF16),
            pltpu.VMEM((bands, rows, width), BF16),
            pltpu.VMEM((bands, width // LANES, LANES // head_dim * rows, rows), F32),
        ],
        compiler_params=params,
        cost_estimate=pl.CostEstimate(flops=4_000_000_000, bytes_accessed=8_000_000, transcendentals=0),
        name="attend",
    )(me1, *x_parts, gain, rel, proj, w_out)
    mix_in = [shifted(mix_out[k - 1], "tm", k) for k in range(1, tm)]
    owns, sent, carry = [], [], []
    diag = (frames, group, rows)
    for band in range(bands):
        last = band == bands - 1
        scratch = [
            pltpu.VMEM((rows, chans), BF16),
            pltpu.VMEM((width // LANES, LANES // head_dim * rows, rows), F32),
            pltpu.VMEM((group, rows, rows), BF16),
            pltpu.VMEM((rows, chans), F32),
        ]
        if last:
            extra = [jax.ShapeDtypeStruct((lines, LANES + span), F32)]
            scratch.append(pltpu.VMEM(diag, F32))
        else:
            extra = [jax.ShapeDtypeStruct((1, chans), F32), jax.ShapeDtypeStruct(diag, F32)]
        own, *rest = pl.pallas_call(
            functools.partial(backward_kernel, dims, band, last),
            in_specs=[smem] + [vmem] * (tm + 7 + len(carry) + len(sent)),
            out_specs=[vmem] * (tm + len(extra)),
            out_shape=[pltpu.VMEM((rows, width), F32)]
            + [pltpu.VMEM((bands, rows, width) if last else (rows, width), BF16)] * (tm - 1) + extra,
            scratch_shapes=scratch,
            compiler_params=params,
            cost_estimate=pl.CostEstimate(flops=2_500_000_000, bytes_accessed=0, transcendentals=0),
            name="attend_back",
        )(me1, *g_parts[band], gain, qkv, probs, xb, inv, proj_turned, out_turned, *carry, *sent)
        sent, carry = (rest[:tm - 1] if last else sent + rest[:tm - 1]), rest[tm - 1:]
        owns.append(own)

    result = jax.ShapeDtypeStruct((total, width), BF16)
    finish_cost = pl.CostEstimate(flops=0, bytes_accessed=1_500_000, transcendentals=0)
    small, mix_in = group_sum(carry[0], "dp", mix_in)
    grad_in = [shifted(sent[k - 1], "tm", k) for k in range(1, tm)]
    block_out = pl.pallas_call(
        functools.partial(finish_out_kernel, bands, frames),
        in_specs=[vmem] * tm,
        out_specs=vmem,
        out_shape=result,
        compiler_params=params,
        cost_estimate=finish_cost,
        name="finish_out",
    )(mix_own, *mix_in)
    small, block_out = group_sum(small, "space", block_out)

    tile = small[:chans // LANES, :LANES]
    tiles = [shifted(tile, "tm", k) for k in range(1, tm)]
    input_grad, bias_grad = pl.pallas_call(
        functools.partial(finish_grad_kernel, bands, frames),
        in_specs=[vmem] * (bands + tm),
        out_specs=[vmem] * 2,
        out_shape=[result, jax.ShapeDtypeStruct((group, offsets), F32)],
        compiler_params=params,
        cost_estimate=finish_cost,
        name="finish_grad",
    )(small, *owns, *grad_in)
    tiles, input_grad = lax.optimization_barrier((tiles, input_grad))
    gain_grad = pl.pallas_call(
        gain_kernel,
        in_specs=[smem] + [vmem] * tm,
        out_specs=vmem,
        out_shape=jax.ShapeDtypeStruct((1, width), F32),
        scratch_shapes=[pltpu.VMEM(tile.shape, F32)],
        compiler_params=params,
        name="gain_sum",
    )(me1, tile, *tiles)
    return (block_out.reshape(inputs.shape), input_grad.reshape(inputs.shape), gain_grad.reshape(width), bias_grad)


def solution(mesh):
    return jax.shard_map(
        per_device,
        mesh=mesh,
        in_specs=(
            P("dp", None, "space", "tm"),
            P("dp", None, "space", "tm"),
            P(),
            P("tm", None),
            P(None, "tm"),
            P(None, "tm"),
            P(None, "tm"),
            P("tm", None),
        ),
        out_specs=(
            P("dp", None, "space", "tm"),
            P("dp", None, "space", "tm"),
            P("tm"),
            P("tm", None),
        ),
        check_vma=False,
    )
```
